1024 devices in a mesh: gx: 8 (over y), gy: 16 (over z), gz: 8 (over x, core).
Axes of the slice: x: 4, y: 8, z: 16, core: 2. Of those that a mesh axis runs over, the one named last changes fastest.
Arguments:
- populations: float32 [27, 64, 128, 1024], P(None, 'gx', 'gy', 'gz'), may hold values from 0 to 0.4, as said below
- solid_mask: int32 [64, 128, 1024], P('gx', 'gy', 'gz'), may hold values 0 or 1
- jet_mask: int32 [64, 128, 1024], P('gx', 'gy', 'gz'), may hold values 0 or 1
- visibility: int32 [8], replicated, may hold values from 0 to 7, each once
Outputs:
- advanced: float32 [27, 64, 128, 1024], P(None, 'gx', 'gy', 'gz')
- image: float32 [4, 256, 512], P(None, 'gx', ('gy', 'gz'))
The draws below stay inside these ranges and needn't reach their ends.
Inputs may be any that keep to these rules, and one draw needn't show every extreme that they name: `populations`: each population is positive and below 1.6 times its direction's weight.
All inputs are finite; a program needn't handle non-finite values. No bound on the sum of `solid_mask` or of `jet_mask` on one device may be relied on, other than what follows from the above.
Results may differ from the reference program's by a relative error of at most 0.0001.
Values sent between devices are 32-bit elements; how exact they have to be, the bound alone decides.
No kernel may reach another device: no remote copies, remote signals or barrier semaphores. Data moves between devices by JAX's collectives and lax.ppermute only.
A program may use at most 32 MiB of HBM per device.

```python
import jax
import jax.numpy as jnp
import numpy as np

CZ = 128
STEPS = 2
UP = 4
SLABS = 8
NX = 64
NY = 128
NZ = 1024


def draw_populations(key, part):
    key = jax.random.fold_in(key, 11)
    dirs = np.array([(a, b, c) for a in (-1, 0, 1) for b in (-1, 0, 1) for c in (-1, 0, 1)], dtype=np.int64)
    table = np.array([8.0 / 27.0, 2.0 / 27.0, 1.0 / 54.0, 1.0 / 216.0])
    wtable = jnp.asarray(table[np.abs(dirs).sum(axis=1)], jnp.float32).reshape(27, 1, 1, 1)
    noise = jax.random.uniform(key, (27, NX, NY, NZ), jnp.float32, -1.0, 1.0)
    values = wtable * (1.0 + 0.3 * noise)
    return values.astype(jnp.float32)


def plant(result, stream_key, least, top_value):
    shape = result.shape
    spot = [jax.random.randint(jax.random.fold_in(stream_key, axis), (), 0, shape[axis]) for axis in range(len(shape))]
    result = result.at[tuple(spot)].set(least)
    longest = shape.index(max(shape))
    spot[longest] = (spot[longest] + 1) % shape[longest]
    return result.at[tuple(spot)].set(top_value)


def setup_inputs(seed: int = 0) -> dict:
    splits = jax.random.split(jax.random.key(seed), 5)
    return {
        "populations": draw_populations(jax.random.fold_in(splits[4], 71), 0),
        "solid_mask": plant((jax.random.randint(splits[1], (NX, NY, NZ), 0, 32) < 1).astype(jnp.int32), jax.random.fold_in(splits[1], 1), 0, 1),
        "jet_mask": plant((jax.random.randint(splits[2], (NX, NY, NZ), 0, 64) < 1).astype(jnp.int32), jax.random.fold_in(splits[2], 1), 0, 1),
        "visibility": jax.random.permutation(splits[3], SLABS).astype(jnp.int32),
    }


omega_rate = 1.25
jet_speed = 0.12
alpha_top = 0.03
solid_alpha = 0.15
shade_scale = 0.002


def lattice_tables():
    dirs = np.array([(a, b, c) for a in (-1, 0, 1) for b in (-1, 0, 1) for c in (-1, 0, 1)], dtype=np.int64)
    table = np.array([8.0 / 27.0, 2.0 / 27.0, 1.0 / 54.0, 1.0 / 216.0])
    weights = table[np.abs(dirs).sum(axis=1)]
    return dirs, weights


def equil_one(index, density, vel_first, vel_second, vel_third):
    dirs, weights = lattice_tables()
    along = float(dirs[index, 0]) * vel_first + float(dirs[index, 1]) * vel_second + float(dirs[index, 2]) * vel_third
    square = vel_first * vel_first + vel_second * vel_second + vel_third * vel_third
    return float(weights[index]) * density * (1.0 + 3.0 * along + 4.5 * along * along - 1.5 * square)


def moments(popul):
    dirs, weights = lattice_tables()
    density = jnp.sum(popul, axis=0)
    comps = []
    for axis_id in range(3):
        plus_ids = [i for i in range(27) if dirs[i, axis_id] == 1]
        minus_ids = [i for i in range(27) if dirs[i, axis_id] == -1]
        total = popul[plus_ids[0]]
        for i in plus_ids[1:]:
            total = total + popul[i]
        for i in minus_ids:
            total = total - popul[i]
        comps.append(total / density)
    return density, comps


def shade(s_two, flow_first, solid_mask):
    ratio = s_two / (s_two + shade_scale)
    fluid_alpha = alpha_top * (1.0 - jnp.exp(-s_two / shade_scale))
    solid_on = solid_mask == 1
    alpha = jnp.where(solid_on, solid_alpha, fluid_alpha)
    red = jnp.where(solid_on, 0.6, 0.3 + 1.5 * ratio)
    green = jnp.where(solid_on, 0.6, 1.2 - 0.9 * ratio)
    blue = jnp.where(solid_on, 0.6, 0.8 + 0.4 * jnp.tanh(20.0 * flow_first))
    colour = jnp.stack([red, green, blue], axis=0) * alpha[None]
    return alpha, colour


def slab_pass(alpha, colour):
    logs = jnp.log1p(-alpha)
    running = jnp.cumsum(logs, axis=-1)
    weight = jnp.exp(running - logs)
    slab_colour = jnp.sum(colour * weight[None], axis=-1)
    return running[..., -1], slab_colour


def upsample(flat):
    chans, rows, cols = flat.shape
    wide = jnp.broadcast_to(flat[:, :, None, :, None], (chans, rows, UP, cols, UP))
    return wide.reshape(chans, rows * UP, cols * UP)


def reference(populations, solid_mask, jet_mask, visibility):
    dirs, weights = lattice_tables()
    popul = populations
    jet_on = jet_mask == 1
    solid_on = solid_mask == 1
    for step in range(STEPS):
        density, comps = moments(popul)
        zeros_field = jnp.zeros_like(density)
        jet_first = zeros_field + jet_speed
        moved = []
        for index in range(27):
            here = popul[index]
            post = here + omega_rate * (equil_one(index, density, comps[0], comps[1], comps[2]) - here)
            jet_state = equil_one(index, density, jet_first, zeros_field, zeros_field)
            post = jnp.where(jet_on, jet_state, post)
            post = jnp.where(solid_on, popul[26 - index], post)
            shift_by = (int(dirs[index, 0]), int(dirs[index, 1]), int(dirs[index, 2]))
            moved.append(jnp.roll(post, shift_by, axis=(0, 1, 2)))
        popul = jnp.stack(moved, axis=0)
    density, comps = moments(popul)
    fluid = 1.0 - solid_mask.astype(jnp.float32)
    flow = [comp * fluid for comp in comps]

    def derive(field, axis_id):
        return 0.5 * (jnp.roll(field, -1, axis_id) - jnp.roll(field, 1, axis_id))

    vort_first = derive(flow[2], 1) - derive(flow[1], 2)
    vort_second = derive(flow[0], 2) - derive(flow[2], 0)
    vort_third = derive(flow[1], 0) - derive(flow[0], 1)
    s_two = vort_first * vort_first + vort_second * vort_second + vort_third * vort_third
    alpha, colour = shade(s_two, flow[0], solid_mask)
    alpha = alpha.reshape(NX, NY, SLABS, CZ)
    colour = colour.reshape(3, NX, NY, SLABS, CZ)
    slab_log, slab_colour = slab_pass(alpha, colour)
    slab_log = jnp.moveaxis(slab_log, 2, 0)
    slab_colour = jnp.moveaxis(slab_colour, 3, 0)
    order = (visibility[None, :] < visibility[:, None]).astype(jnp.float32)
    front = jnp.sum(order[:, :, None, None] * slab_log[None], axis=1)
    rgb = jnp.sum(jnp.exp(front)[:, None] * slab_colour, axis=0)
    opacity = 1.0 - jnp.exp(jnp.sum(slab_log, axis=0))
    flat = jnp.concatenate([rgb, opacity[None]], axis=0)
    return popul, upsample(flat)
```

```python
import jax
import jax.numpy as jnp
import numpy as np
from jax import lax
from jax.experimental import pallas as pl
from jax.experimental.pallas import tpu as pltpu
from jax.sharding import PartitionSpec as P

UP = 4
CELLS = 8
LANES = 128
REACH = 3
SPAN = CELLS + 2 * REACH
RING = 16
GROUP = 8

omega_rate = 1.25
jet_speed = 0.12
alpha_top = 0.03
solid_alpha = 0.15
shade_scale = 0.002

DIRS = [(a, b, c) for a in (-1, 0, 1) for b in (-1, 0, 1) for c in (-1, 0, 1)]
WEIGHTS = [(8.0 / 27.0, 2.0 / 27.0, 1.0 / 54.0, 1.0 / 216.0)[abs(a) + abs(b) + abs(c)] for a, b, c in DIRS]
SOLID, JET = 27, 28
MASKS = (SOLID, JET)


def axis_list(axis, inward):
    out = []
    for dist, allowed in ((1, (-1, 0, 1)), (2, (0, inward)), (3, (inward,))):
        out += [(i, dist) for i in range(27) if DIRS[i][axis] in allowed]
    out += [(m, dist) for m in MASKS for dist in (1, 2)]
    return out


def held(key, x):
    dist, inward = (-x, 1) if x < 0 else (x - CELLS + 1, -1)
    if dist <= 0:
        return True
    return (key, dist) in axis_list(0, inward)


def corner_list(inward):
    out = []
    for key, dist in axis_list(1, inward):
        for x in (-3, -2, -1, 8, 9, 10):
            if held(key, x) and not (dist == 3 and x in (-3, 10)):
                out.append((key, dist, x))
    return out


X_COUNT = len(axis_list(0, 1))
Y_OWN = len(axis_list(1, 1)) * CELLS
Y_COUNT = Y_OWN + -(-len(corner_list(1)) // 8) * 8


def moments(f):
    third = None
    parts = []
    for a in range(3):
        row = []
        for b in range(3):
            lo, mid, hi = f[9 * a + 3 * b], f[9 * a + 3 * b + 1], f[9 * a + 3 * b + 2]
            row.append((lo + hi) + mid)
            diff = hi - lo
            third = diff if third is None else third + diff
        parts.append(row)
    sums = [(row[0] + row[2]) + row[1] for row in parts]
    second = (parts[0][2] - parts[0][0]) + (parts[1][2] - parts[1][0]) + (parts[2][2] - parts[2][0])
    return (sums[0] + sums[2]) + sums[1], sums[2] - sums[0], second, third


def collide(f, solid, jet):
    density, first, second, third = moments(f)
    scale = 1.0 / density
    ux = jnp.where(jet, jet_speed, first * scale)
    uy = jnp.where(jet, 0.0, second * scale)
    uz = jnp.where(jet, 0.0, third * scale)
    gain = jnp.where(jet, 1.0, omega_rate) * density
    keep = jnp.where(jet, 0.0, 1.0 - omega_rate)
    base = 1.0 - 1.5 * (ux * ux + uy * uy + uz * uz)
    strength = {w: gain * w for w in set(WEIGHTS)}
    post = [None] * 27
    comps = (ux, uy, uz)
    for i in range(14):
        w = strength[WEIGHTS[i]]
        if i == 13:
            post[i] = jnp.where(solid, f[i], w * base + keep * f[i])
            continue
        along = None
        for c, u in zip(DIRS[i], comps):
            if c == 0:
                continue
            if along is None:
                along = u if c > 0 else -u
            else:
                along = along + u if c > 0 else along - u
        even = w * (base + 4.5 * (along * along))
        odd = w * (3.0 * along)
        j = 26 - i
        post[i] = jnp.where(solid, f[j], (even + odd) + keep * f[i])
        post[j] = jnp.where(solid, f[i], (even - odd) + keep * f[j])
    return post


def lanes_of(rows):
    return lax.broadcasted_iota(jnp.int32, (rows, LANES), 1)


def turn(value, shift, axis):
    size = value.shape[axis]
    if isinstance(shift, int):
        shift = shift % size
        if shift == 0:
            return value
    return pltpu.roll(value, shift, axis)


def first_kernel(f_ref, solid_ref, jet_ref, p_ref, lo_ref, hi_ref):
    def plane(x, carry):
        start = pl.multiple_of(x * CELLS, CELLS)
        rows = pl.ds(start, CELLS)
        f = [f_ref[i, rows, :] for i in range(27)]
        post = collide(f, solid_ref[rows, :] == 1, jet_ref[rows, :] == 1)
        for i in range(27):
            p_ref[i, rows, :] = post[i]
        return carry

    lax.fori_loop(0, CELLS, plane, 0)

    def plane_of(key, x):
        rows = pl.ds(x * CELLS, CELLS)
        if key == SOLID:
            return solid_ref[rows, :].astype(jnp.float32)
        if key == JET:
            return jet_ref[rows, :].astype(jnp.float32)
        return p_ref[key, rows, :]

    for k, (key, dist) in enumerate(axis_list(0, -1)):
        lo_ref[k] = plane_of(key, dist - 1)
    for k, (key, dist) in enumerate(axis_list(0, 1)):
        hi_ref[k] = plane_of(key, CELLS - dist)


def second_kernel(p_ref, solid_ref, jet_ref, xlo_ref, xhi_ref, lo_ref, hi_ref):
    low_at = {entry: k for k, entry in enumerate(axis_list(0, 1))}
    high_at = {entry: k for k, entry in enumerate(axis_list(0, -1))}

    def own_rows(key, row):
        rows = pl.ds(row, CELLS, stride=CELLS)
        if key == SOLID:
            return solid_ref[rows, :].astype(jnp.float32)
        if key == JET:
            return jet_ref[rows, :].astype(jnp.float32)
        return p_ref[key, rows, :]

    for inward, out_ref in ((-1, lo_ref), (1, hi_ref)):
        for k, (key, dist) in enumerate(axis_list(1, inward)):
            row = dist - 1 if inward < 0 else CELLS - dist
            out_ref[pl.ds(k * CELLS, CELLS), :] = own_rows(key, row)
        for k, (key, dist, x) in enumerate(corner_list(inward)):
            row = dist - 1 if inward < 0 else CELLS - dist
            if x < 0:
                value = xlo_ref[low_at[(key, -x)], pl.ds(row, 1), :]
            else:
                value = xhi_ref[high_at[(key, x - CELLS + 1)], pl.ds(row, 1), :]
            out_ref[pl.ds(Y_OWN + k, 1), :] = value


def third_kernel(p_ref, solid_ref, jet_ref, xlo_ref, xhi_ref, ylo_ref, yhi_ref, e_ref, z_ref):
    for x in range(CELLS):
        rows = pl.ds((x + REACH) * RING, CELLS)
        for i in range(27):
            e_ref[i, rows, :] = p_ref[i, pl.ds(x * CELLS, CELLS), :]
        e_ref[SOLID, rows, :] = solid_ref[pl.ds(x * CELLS, CELLS), :].astype(jnp.float32)
        e_ref[JET, rows, :] = jet_ref[pl.ds(x * CELLS, CELLS), :].astype(jnp.float32)
    for k, (key, dist) in enumerate(axis_list(0, 1)):
        e_ref[key, pl.ds((REACH - dist) * RING, CELLS), :] = xlo_ref[k]
    for k, (key, dist) in enumerate(axis_list(0, -1)):
        e_ref[key, pl.ds((REACH + CELLS - 1 + dist) * RING, CELLS), :] = xhi_ref[k]
    for inward, in_ref in ((1, ylo_ref), (-1, yhi_ref)):
        for k, (key, dist) in enumerate(axis_list(1, inward)):
            ring = RING - dist if inward > 0 else CELLS - 1 + dist
            e_ref[key, pl.ds(REACH * RING + ring, CELLS, stride=RING), :] = in_ref[pl.ds(k * CELLS, CELLS), :]
        for k, (key, dist, x) in enumerate(corner_list(inward)):
            ring = RING - dist if inward > 0 else CELLS - 1 + dist
            e_ref[key, pl.ds((x + REACH) * RING + ring, 1), :] = in_ref[pl.ds(Y_OWN + k, 1), :]
    group = lanes_of(RING) // GROUP

    def pack(key, carry):
        acc = jnp.zeros((RING, LANES), jnp.float32)
        for plane in range(SPAN):
            value = turn(e_ref[key, pl.ds(plane * RING, RING), :], GROUP * plane + 3, 1)
            acc = jnp.where(group == plane, value, acc)
        z_ref[key] = acc
        return carry

    lax.fori_loop(0, 29, pack, 0)


def fourth_kernel(e_ref, z_ref, zlo_ref, zhi_ref, adv_ref, out_ref, g_ref, ge_ref, h_ref, flow_ref):
    lane = lanes_of(RING)
    slot = lane % GROUP

    def edges(key, own):
        mixed = jnp.where(slot < 3, zlo_ref[key], own)
        return jnp.where(slot >= 5, turn(zhi_ref[key], 2, 1), mixed)

    for i in range(27):
        own = z_ref[i]
        if DIRS[i][2] == 1:
            own = turn(own, 2, 1)
        ge_ref[i] = edges(i, own)
    nothing = jnp.zeros((RING, LANES), jnp.float32)
    edge_solid = edges(SOLID, nothing)
    edge_jet = edges(JET, nothing)

    def stream_edges():
        out = []
        for i, (a, b, c) in enumerate(DIRS):
            out.append(turn(turn(ge_ref[i], b, 0), GROUP * a + c, 1))
        return out

    def stream(load, plane):
        out = []
        for i, (a, b, c) in enumerate(DIRS):
            source = plane - a
            value = load(i, source)
            if c == 1:
                value = jnp.where(lane == LANES - 1, turn(ge_ref[i], LANES - 1 - 2 - GROUP * source, 1), value)
            elif c == -1:
                value = jnp.where(lane == 0, turn(ge_ref[i], LANES - 5 - GROUP * source, 1), value)
            out.append(turn(turn(value, b, 0), c, 1))
        return out

    def rows_of(plane):
        return pl.ds(pl.multiple_of(plane * RING, RING), RING)

    def from_block(i, plane):
        return e_ref[i, rows_of(plane), :]

    def from_step(i, plane):
        return g_ref[i, rows_of(plane), :]

    edge_post = collide(stream_edges(), edge_solid > 0.5, edge_jet > 0.5)
    for i in range(27):
        h_ref[i] = edge_post[i]

    def step_one(plane, carry):
        f = stream(from_block, plane)
        post = collide(f, e_ref[SOLID, rows_of(plane), :] > 0.5, e_ref[JET, rows_of(plane), :] > 0.5)
        for i in range(27):
            g_ref[i, rows_of(plane), :] = post[i]
            c = DIRS[i][2]
            if c == -1:
                h_ref[i] = jnp.where(lane == GROUP * plane + 3, turn(post[i], GROUP * plane + 3, 1), h_ref[i])
            elif c == 1:
                h_ref[i] = jnp.where(lane == GROUP * plane + 4, turn(post[i], GROUP * plane + 5, 1), h_ref[i])
        return carry

    lax.fori_loop(1, SPAN - 1, step_one, 0)
    for i in range(27):
        ge_ref[i] = h_ref[i]

    def velocity(f, solid):
        density, first, second, third = moments(f)
        scale = (1.0 - solid) / density
        return first * scale, second * scale, third * scale

    edge_flow = velocity(stream_edges(), edge_solid)

    def step_two(plane, keep):
        f = stream(from_step, plane)
        if keep:
            for i in range(27):
                adv_ref[i, plane - REACH] = f[i][:CELLS]
        for c, value in enumerate(velocity(f, e_ref[SOLID, rows_of(plane), :])):
            flow_ref[c, rows_of(plane), :] = value

    step_two(REACH - 1, False)
    step_two(REACH + CELLS, False)

    def step_two_own(plane, carry):
        step_two(plane, True)
        return carry

    lax.fori_loop(REACH, REACH + CELLS, step_two_own, 0)

    short = lanes_of(CELLS)

    def render(x, acc):
        plane = x + REACH
        flow = [flow_ref[c, rows_of(plane), :] for c in range(3)]
        ahead = [flow_ref[c, rows_of(plane + 1), :][:CELLS] for c in range(3)]
        behind = [flow_ref[c, rows_of(plane - 1), :][:CELLS] for c in range(3)]

        def along_first(c):
            return 0.5 * (ahead[c] - behind[c])

        def along_second(c):
            return 0.5 * (turn(flow[c], -1, 0) - turn(flow[c], 1, 0))[:CELLS]

        def along_third(c):
            here = flow[c][:CELLS]
            edge = edge_flow[c][:CELLS]
            low = jnp.where(short == 0, turn(edge, LANES - 2 - GROUP * plane, 1), turn(here, 1, 1))
            high = jnp.where(
                short == LANES - 1, turn(edge, LANES - 1 - 5 - GROUP * plane, 1), turn(here, -1, 1)
            )
            return 0.5 * (high - low)

        vort_first = along_second(2) - along_third(1)
        vort_second = along_third(0) - along_first(2)
        vort_third = along_first(1) - along_second(0)
        s_two = vort_first * vort_first + vort_second * vort_second + vort_third * vort_third
        solid_on = e_ref[SOLID, pl.ds(pl.multiple_of(plane * RING, RING), CELLS), :] > 0.5
        ratio = s_two / (s_two + shade_scale)
        alpha = jnp.where(solid_on, solid_alpha, alpha_top * (1.0 - jnp.exp(-s_two / shade_scale)))
        red = jnp.where(solid_on, 0.6, 0.3 + 1.5 * ratio)
        green = jnp.where(solid_on, 0.6, 1.2 - 0.9 * ratio)
        blue = jnp.where(solid_on, 0.6, 0.8 + 0.4 * jnp.tanh(20.0 * flow[0][:CELLS]))
        logs = jnp.log1p(-alpha)
        running = logs
        for step in (1, 2, 4, 8, 16, 32, 64):
            running = running + jnp.where(short >= step, turn(running, step, 1), 0.0)
        weight = alpha * jnp.exp(running - logs)
        for ch, value in enumerate((red * weight, green * weight, blue * weight, logs)):
            total = jnp.sum(value, axis=1, keepdims=True)
            acc = jnp.where(short // UP == ch * CELLS + x, total, acc)
        return acc

    out_ref[...] = lax.fori_loop(0, CELLS, render, jnp.zeros((CELLS, LANES), jnp.float32))


def last_kernel(slab_ref, rank_ref, out_ref):
    slabs = slab_ref[...]
    rank = rank_ref[...]
    channel = lanes_of(CELLS) // (CELLS * UP)
    logs = slabs
    for ch in range(3):
        logs = jnp.where(channel == ch, turn(slabs, (ch + 1) * CELLS * UP, 1), logs)
    front = jnp.zeros_like(slabs)
    for s in range(CELLS):
        front = front + jnp.where(rank[s : s + 1] < rank, logs[s : s + 1], 0.0)
    colour = jnp.sum(jnp.exp(front) * slabs, axis=0, keepdims=True)
    opacity = 1.0 - jnp.exp(jnp.sum(logs, axis=0, keepdims=True))
    row = jnp.where(channel[:1] == 3, opacity, colour)
    for ch in range(4):
        out_ref[ch] = jnp.broadcast_to(turn(row, -ch * CELLS * UP, 1)[:, : CELLS * UP], (UP, CELLS * UP))


def call(kernel, outs, scratch=()):
    shapes = tuple(jax.ShapeDtypeStruct(shape, jnp.float32) for shape in outs)
    return pl.pallas_call(
        kernel,
        out_shape=shapes,
        scratch_shapes=[pltpu.VMEM(shape, jnp.float32) for shape in scratch],
        compiler_params=pltpu.CompilerParams(vmem_limit_bytes=24 * 1024 * 1024),
    )


def both_ways(lo, hi, axis):
    count = lax.axis_size(axis)
    forward = [(i, (i + 1) % count) for i in range(count)]
    backward = [(target, source) for source, target in forward]
    return lax.ppermute(hi, axis, forward), lax.ppermute(lo, axis, backward)


def body(populations, solid_mask, jet_mask, visibility):
    cells = CELLS * CELLS
    f = populations.reshape(27, cells, LANES)
    solid = solid_mask.reshape(cells, LANES)
    jet = jet_mask.reshape(cells, LANES)
    x_shape = (X_COUNT, CELLS, LANES)
    post, lo, hi = call(first_kernel, ((27, cells, LANES), x_shape, x_shape))(f, solid, jet)
    xlo, xhi = both_ways(lo, hi, "gx")
    y_shape = (Y_COUNT, LANES)
    lo, hi = call(second_kernel, (y_shape, y_shape))(post, solid, jet, xlo, xhi)
    ylo, yhi = both_ways(lo, hi, "gy")
    block, face = call(third_kernel, ((29, SPAN * RING, LANES), (29, RING, LANES)))(
        post, solid, jet, xlo, xhi, ylo, yhi
    )
    zlo, zhi = both_ways(face, face, "gz")
    advanced, slabs = call(
        fourth_kernel,
        ((27, CELLS, CELLS, LANES), (CELLS, LANES)),
        (
            (27, SPAN * RING, LANES),
            (27, RING, LANES),
            (27, RING, LANES),
            (3, SPAN * RING, LANES),
        ),
    )(block, face, zlo, zhi)
    slabs = lax.all_to_all(slabs, "gz", 0, 0, tiled=True)
    rank = jnp.broadcast_to(visibility[:, None], (CELLS, LANES))
    (image,) = call(last_kernel, ((4, UP, CELLS * UP),))(slabs, rank)
    return advanced, jnp.swapaxes(image, 1, 2)


def solution(mesh):
    return jax.shard_map(
        body,
        mesh=mesh,
        in_specs=(P(None, "gx", "gy", "gz"), P("gx", "gy", "gz"), P("gx", "gy", "gz"), P()),
        out_specs=(P(None, "gx", "gy", "gz"), P(None, "gx", ("gy", "gz"))),
        check_vma=False,
    )
```

```python
import jax
import jax.numpy as jnp
import numpy as np
from jax import lax
from jax.experimental import pallas as pl
from jax.experimental.pallas import tpu as pltpu
from jax.sharding import PartitionSpec as P

UP = 4
CELLS = 8
LANES = 128
REACH = 3
SPAN = CELLS + 2 * REACH
LAST = SPAN - 1
ROWS = 16
HALF = 15
GROUP = 8

omega_rate = 1.25
jet_speed = 0.12
alpha_top = 0.03
solid_alpha = 0.15
shade_scale = 0.002

DIRS = [(a, b, c) for a in (-1, 0, 1) for b in (-1, 0, 1) for c in (-1, 0, 1)]
WEIGHTS = [(8.0 / 27.0, 2.0 / 27.0, 1.0 / 54.0, 1.0 / 216.0)[abs(a) + abs(b) + abs(c)] for a, b, c in DIRS]
SOLID, JET = 27, 28
MASKS = (SOLID, JET)


def axis_list(axis, inward):
    out = []
    for dist, allowed in ((1, (-1, 0, 1)), (2, (0, inward)), (3, (inward,))):
        out += [(i, dist) for i in range(27) if DIRS[i][axis] in allowed]
    out += [(m, dist) for m in MASKS for dist in (1, 2)]
    return out


def held(key, x):
    dist, inward = (-x, 1) if x < 0 else (x - CELLS + 1, -1)
    if dist <= 0:
        return True
    return (key, dist) in axis_list(0, inward)


def corner_list(inward):
    out = []
    for key, dist in axis_list(1, inward):
        for x in (-3, -2, -1, 8, 9, 10):
            if held(key, x) and not (dist == 3 and x in (-3, 10)):
                out.append((key, dist, x))
    return out


X_COUNT = len(axis_list(0, 1))
Y_OWN = len(axis_list(1, 1)) * CELLS
Y_COUNT = Y_OWN + -(-len(corner_list(1)) // 8) * 8


def moments(f):
    third = None
    parts = []
    for a in range(3):
        row = []
        for b in range(3):
            lo, mid, hi = f[9 * a + 3 * b], f[9 * a + 3 * b + 1], f[9 * a + 3 * b + 2]
            row.append((lo + hi) + mid)
            diff = hi - lo
            third = diff if third is None else third + diff
        parts.append(row)
    sums = [(row[0] + row[2]) + row[1] for row in parts]
    second = (parts[0][2] - parts[0][0]) + (parts[1][2] - parts[1][0]) + (parts[2][2] - parts[2][0])
    return (sums[0] + sums[2]) + sums[1], sums[2] - sums[0], second, third


def collide(f, solid, jet):
    density, first, second, third = moments(f)
    scale = 1.0 / density
    ux = jnp.where(jet, jet_speed, first * scale)
    uy = jnp.where(jet, 0.0, second * scale)
    uz = jnp.where(jet, 0.0, third * scale)
    gain = jnp.where(jet, 1.0, omega_rate) * density
    keep = jnp.where(jet, 0.0, 1.0 - omega_rate)
    base = 1.0 - 1.5 * (ux * ux + uy * uy + uz * uz)
    strength = {w: gain * w for w in set(WEIGHTS)}
    post = [None] * 27
    comps = (ux, uy, uz)
    for i in range(14):
        w = strength[WEIGHTS[i]]
        if i == 13:
            post[i] = jnp.where(solid, f[i], w * base + keep * f[i])
            continue
        along = None
        for c, u in zip(DIRS[i], comps):
            if c == 0:
                continue
            if along is None:
                along = u if c > 0 else -u
            else:
                along = along + u if c > 0 else along - u
        even = w * (base + 4.5 * (along * along))
        odd = w * (3.0 * along)
        j = 26 - i
        post[i] = jnp.where(solid, f[j], (even + odd) + keep * f[i])
        post[j] = jnp.where(solid, f[i], (even - odd) + keep * f[j])
    return post


def lanes_of(rows):
    return lax.broadcasted_iota(jnp.int32, (rows, LANES), 1)


def turn(value, shift, axis):
    size = value.shape[axis]
    if isinstance(shift, int):
        shift = shift % size
        if shift == 0:
            return value
    return pltpu.roll(value, shift, axis)


def first_kernel(f_hbm, solid_hbm, jet_hbm, p_ref, lo_ref, hi_ref, f_ref, solid_ref, jet_ref, sems):
    masks = [
        pltpu.make_async_copy(solid_hbm, solid_ref, sems.at[CELLS]),
        pltpu.make_async_copy(jet_hbm, jet_ref, sems.at[CELLS + 1]),
    ]
    copies = []
    for x in range(CELLS):
        rows = pl.ds(x * CELLS, CELLS)
        copies.append(pltpu.make_async_copy(f_hbm.at[:, rows, :], f_ref.at[:, rows, :], sems.at[x]))
    for copy in masks + copies:
        copy.start()
    for copy in masks:
        copy.wait()
    p_ref[SOLID] = solid_ref[...].astype(jnp.float32)
    p_ref[JET] = jet_ref[...].astype(jnp.float32)

    def plane(x):
        rows = pl.ds(x * CELLS, CELLS)
        f = [f_ref[i, rows, :] for i in range(27)]
        post = collide(f, solid_ref[rows, :] == 1, jet_ref[rows, :] == 1)
        for i in range(27):
            p_ref[i, rows, :] = post[i]

    for x in range(CELLS):
        copies[x].wait()
        plane(x)
    for k, (key, dist) in enumerate(axis_list(0, -1)):
        lo_ref[k] = p_ref[key, pl.ds((dist - 1) * CELLS, CELLS), :]
    for k, (key, dist) in enumerate(axis_list(0, 1)):
        hi_ref[k] = p_ref[key, pl.ds((CELLS - dist) * CELLS, CELLS), :]


LOW_AT = {entry: k for k, entry in enumerate(axis_list(0, 1))}
HIGH_AT = {entry: k for k, entry in enumerate(axis_list(0, -1))}


def plane_ref(key, x, p_ref, xlo_ref, xhi_ref):
    if x < 0:
        return xlo_ref.at[LOW_AT[(key, -x)]]
    if x >= CELLS:
        return xhi_ref.at[HIGH_AT[(key, x - CELLS + 1)]]
    return p_ref.at[key, pl.ds(x * CELLS, CELLS), :]


def second_kernel(p_ref, xlo_ref, xhi_ref, lo_ref, hi_ref):
    for inward, out_ref in ((-1, lo_ref), (1, hi_ref)):
        for k, (key, dist) in enumerate(axis_list(1, inward)):
            row = dist - 1 if inward < 0 else CELLS - dist
            out_ref[pl.ds(k * CELLS, CELLS), :] = p_ref[key, pl.ds(row, CELLS, stride=CELLS), :]
        for k, (key, dist, x) in enumerate(corner_list(inward)):
            row = dist - 1 if inward < 0 else CELLS - dist
            out_ref[pl.ds(Y_OWN + k, 1), :] = plane_ref(key, x, p_ref, xlo_ref, xhi_ref)[pl.ds(row, 1), :]


def faces_kernel(p_ref, xlo_ref, xhi_ref, z_ref):
    group = lanes_of(CELLS) // GROUP
    for key in range(29):
        acc = jnp.zeros((CELLS, LANES), jnp.float32)
        for plane in range(SPAN):
            if held(key, plane - REACH):
                value = plane_ref(key, plane - REACH, p_ref, xlo_ref, xhi_ref)[...]
                acc = jnp.where(group == LAST - plane, turn(value, GROUP * (LAST - plane) + 3, 1), acc)
        z_ref[key] = acc


def third_kernel(ylo_ref, yhi_ref, zmain_ref, h_ref, z_ref, lo_ref, hi_ref):
    for inward, in_ref in ((1, ylo_ref), (-1, yhi_ref)):
        for k, (key, dist) in enumerate(axis_list(1, inward)):
            start = CELLS * REACH + CELLS - dist if inward > 0 else CELLS * (REACH + 1) + dist - 1
            h_ref[key, pl.ds(start, CELLS, stride=CELLS), :] = in_ref[pl.ds(k * CELLS, CELLS), :]
        for k, (key, dist, x) in enumerate(corner_list(inward)):
            plane = x + REACH
            row = CELLS * plane + CELLS - dist if inward > 0 else CELLS * (plane + 1) + dist - 1
            h_ref[key, pl.ds(row, 1), :] = in_ref[pl.ds(Y_OWN + k, 1), :]
    lane = lanes_of(CELLS)
    group = lane // GROUP
    upper = lax.broadcasted_iota(jnp.int32, (CELLS, LANES), 0) < CELLS // 2
    for key in range(29):
        acc = jnp.zeros((CELLS, LANES), jnp.float32)
        for tile in range(SPAN + 1):
            value = turn(h_ref[key, pl.ds(tile * CELLS, CELLS), :], GROUP * (LAST - tile) + 3, 1)
            acc = jnp.where(group == (LAST - tile) % (LANES // GROUP), value, acc)
        z_ref[key, pl.ds(0, CELLS), :] = zmain_ref[key]
        z_ref[key, pl.ds(CELLS, CELLS), :] = jnp.where(upper, turn(acc, GROUP, 1), acc)
    early = lanes_of(2 * CELLS) % GROUP < REACH
    for k in range(HALF):
        first = z_ref[k]
        if k + HALF < 29:
            second = z_ref[k + HALF]
            lo_ref[k] = jnp.where(early, turn(second, -REACH, 1), first)
            hi_ref[k] = jnp.where(early, first, turn(second, REACH, 1))
        else:
            lo_ref[k] = first
            hi_ref[k] = first


def block_kernel(p_ref, xlo_ref, xhi_ref, h_ref, e_ref):
    for plane in range(SPAN):
        for key in range(29):
            if held(key, plane - REACH):
                e_ref[key, pl.ds(plane * ROWS + CELLS, CELLS), :] = plane_ref(
                    key, plane - REACH, p_ref, xlo_ref, xhi_ref
                )[...]
    for tile in range(SPAN + 1):
        for key in range(29):
            e_ref[key, pl.ds(tile * ROWS, CELLS), :] = h_ref[key, pl.ds(tile * CELLS, CELLS), :]


def face_sums(values):
    rows = [(row[0] + row[2]) + row[1] for row in values]
    second = (values[0][2] - values[0][0]) + (values[1][2] - values[1][0]) + (values[2][2] - values[2][0])
    return (rows[0] + rows[2]) + rows[1], rows[2] - rows[0], second


def fourth_kernel(e_ref, z_ref, zlo_ref, zhi_ref, adv_hbm, out_ref, g_ref, ge_ref, he_ref, flow_ref, adv_ref, sem):
    lane = lanes_of(CELLS)
    slot = lane % GROUP

    wide_slot = lanes_of(2 * CELLS) % GROUP
    for key in range(29):
        if key < HALF:
            low, high = zlo_ref[key], turn(zhi_ref[key], 2, 1)
        else:
            low, high = turn(zlo_ref[key - HALF], -REACH, 1), turn(zhi_ref[key - HALF], REACH + 2, 1)
        value = jnp.where(wide_slot < 3, low, high)
        if key < 27 and DIRS[key][2] == -1:
            value = jnp.where(wide_slot == 3, z_ref[key], value)
        elif key < 27 and DIRS[key][2] == 1:
            value = jnp.where(wide_slot == 4, turn(z_ref[key], 2, 1), value)
        ge_ref[key, pl.ds(CELLS, 2 * CELLS), :] = value
        ge_ref[key, pl.ds(0, CELLS), :] = value[CELLS:]

    def edge_stream(ref, y):
        return [
            turn(ref[i, pl.ds(CELLS + y - b, CELLS), :], c - GROUP * a, 1) for i, (a, b, c) in enumerate(DIRS)
        ]

    for y in (-2, 6):
        rows = pl.ds(CELLS + y, CELLS)
        post = collide(edge_stream(ge_ref, y), ge_ref[SOLID, rows, :] > 0.5, ge_ref[JET, rows, :] > 0.5)
        for i in range(27):
            he_ref[i, rows, :] = post[i]

    def settle(c, value, edge):
        return jnp.where(lane == (0 if c > 0 else LANES - 1), edge, turn(value, c, 1))

    def shift_to_end(c, plane):
        return (LANES - 2 if c > 0 else LANES - 6) - GROUP * (LAST - plane)

    def plane_rows(plane, y):
        return pl.ds(plane * ROWS + CELLS + y, CELLS)

    def plane_stream(ref, edge_ref, plane, y):
        still, out = [], []
        for i, (a, b, c) in enumerate(DIRS):
            value = ref[i, plane_rows(plane - a, y - b), :]
            still.append(value)
            if c != 0:
                edge = edge_ref[i, pl.ds(CELLS + y - b, CELLS), :]
                value = settle(c, value, turn(edge, shift_to_end(c, plane - a), 1))
            out.append(value)
        return still, out

    def row_slice(plane, y):
        return pl.ds(plane * ROWS + CELLS + y, CELLS, stride=ROWS)

    def row_stream(ref, edge_ref, y):
        out = []
        for i, (a, b, c) in enumerate(DIRS):
            value = ref[i, row_slice(REACH - a, y - b), :]
            if c != 0:
                edge = jnp.broadcast_to(edge_ref[i, pl.ds(CELLS + y - b, 1), :], (CELLS, LANES))
                edge = pltpu.roll(
                    edge, shift_to_end(c, REACH - a), 1, stride=GROUP, stride_axis=0
                )
                value = settle(c, value, edge)
            out.append(value)
        return out

    def step_one(plane, y):
        rows = plane_rows(plane, y)
        post = collide(
            plane_stream(e_ref, ge_ref, plane, y)[1], e_ref[SOLID, rows, :] > 0.5, e_ref[JET, rows, :] > 0.5
        )
        for i in range(27):
            g_ref[i, rows, :] = post[i]

    def step_one_own(k, carry):
        step_one(REACH + 2 * k, 0)
        step_one(REACH + 2 * k + 1, 0)
        return carry

    def step_one_halo(k, carry):
        plane = k + 1 + CELLS * (k // 2)
        step_one(plane, -2)
        step_one(plane, 6)
        return carry

    lax.fori_loop(0, CELLS // 2, step_one_own, 0)
    lax.fori_loop(0, 4, step_one_halo, 0)
    for y in (-2, -1, CELLS, CELLS + 1):
        rows = row_slice(REACH, y)
        post = collide(row_stream(e_ref, ge_ref, y), e_ref[SOLID, rows, :] > 0.5, e_ref[JET, rows, :] > 0.5)
        for i in range(27):
            g_ref[i, rows, :] = post[i]

    def velocity(f, solid):
        density, first, second, third = moments(f)
        scale = (1.0 - solid) / density
        return first * scale, second * scale, third * scale

    def store_flow(rows, f):
        for c, value in enumerate(velocity(f, e_ref[SOLID, rows, :])):
            flow_ref[c, rows, :] = value

    def by_pair(values, c):
        return [[values[9 * a + 3 * b + c + 1] for b in range(3)] for a in range(3)]

    def step_two(plane, acc):
        still, f = plane_stream(g_ref, he_ref, plane, 0)
        rows = pl.ds(pl.multiple_of((plane - REACH) * CELLS, CELLS), CELLS)
        for i in range(27):
            adv_ref[i, rows, :] = f[i]
        store_flow(plane_rows(plane, 0), f)
        place = (lane // GROUP == LAST - plane) & ((slot == 2) | (slot == 3))
        out = []
        for total, down, up in zip(acc, face_sums(by_pair(still, -1)), face_sums(by_pair(still, 1))):
            mixed = turn(jnp.where(lane == 0, down, up), GROUP * (LAST - plane) + 3, 1)
            out.append(jnp.where(place, mixed, total))
        return tuple(out)

    def step_two_own(k, acc):
        return step_two(REACH + 2 * k + 1, step_two(REACH + 2 * k, acc))

    acc = lax.fori_loop(0, CELLS // 2, step_two_own, tuple(jnp.zeros((CELLS, LANES), jnp.float32) for _ in range(3)))
    save = pltpu.make_async_copy(adv_ref, adv_hbm, sem)
    save.start()
    for plane in (REACH - 1, REACH + CELLS):
        store_flow(plane_rows(plane, 0), plane_stream(g_ref, he_ref, plane, 0)[1])
    for y in (-1, CELLS):
        store_flow(row_slice(REACH, y), row_stream(g_ref, he_ref, y))
    f = edge_stream(he_ref, 0)
    sums = [face_sums(by_pair(f, c)) for c in (-1, 0, 1)]
    high = slot == 5
    density, first, second = [
        middle + jnp.where(high, down, up) + jnp.where(high, turn(total, 3, 1), turn(total, -1, 1))
        for down, middle, up, total in zip(sums[0], sums[1], sums[2], acc)
    ]
    scale = (1.0 - ge_ref[SOLID, pl.ds(CELLS, CELLS), :]) / density
    edge_flow = (first * scale, second * scale)

    acc = jnp.zeros((CELLS, LANES), jnp.float32)
    for x in range(CELLS):
        plane = x + REACH
        here = [flow_ref[c, plane_rows(plane, 0), :] for c in range(3)]

        def along_first(c):
            return 0.5 * (flow_ref[c, plane_rows(plane + 1, 0), :] - flow_ref[c, plane_rows(plane - 1, 0), :])

        def along_second(c):
            return 0.5 * (flow_ref[c, plane_rows(plane, 1), :] - flow_ref[c, plane_rows(plane, -1), :])

        def along_third(c):
            low = settle(1, here[c], turn(edge_flow[c], shift_to_end(1, plane), 1))
            high = settle(-1, here[c], turn(edge_flow[c], shift_to_end(-1, plane), 1))
            return 0.5 * (high - low)

        vort_first = along_second(2) - along_third(1)
        vort_second = along_third(0) - along_first(2)
        vort_third = along_first(1) - along_second(0)
        s_two = vort_first * vort_first + vort_second * vort_second + vort_third * vort_third
        solid_on = e_ref[SOLID, plane_rows(plane, 0), :] > 0.5
        ratio = s_two / (s_two + shade_scale)
        alpha = jnp.where(solid_on, solid_alpha, alpha_top * (1.0 - jnp.exp(-s_two / shade_scale)))
        red = jnp.where(solid_on, 0.6, 0.3 + 1.5 * ratio)
        green = jnp.where(solid_on, 0.6, 1.2 - 0.9 * ratio)
        blue = jnp.where(solid_on, 0.6, 0.8 + 0.4 * jnp.tanh(20.0 * here[0]))
        logs = jnp.log1p(-alpha)
        running = logs
        for step in (1, 2, 4, 8, 16, 32, 64):
            running = running + jnp.where(lane >= step, turn(running, step, 1), 0.0)
        weight = alpha * jnp.exp(running - logs)
        for ch, value in enumerate((red * weight, green * weight, blue * weight, logs)):
            total = jnp.sum(value, axis=1, keepdims=True)
            acc = jnp.where(lane // UP == ch * CELLS + x, total, acc)
    out_ref[...] = acc
    save.wait()


def last_kernel(slab_ref, rank_ref, out_ref):
    slabs = slab_ref[...]
    rank = rank_ref[...]
    channel = lanes_of(CELLS) // (CELLS * UP)
    logs = slabs
    for ch in range(3):
        logs = jnp.where(channel == ch, turn(slabs, (ch + 1) * CELLS * UP, 1), logs)
    front = jnp.zeros_like(slabs)
    for s in range(CELLS):
        front = front + jnp.where(rank[s : s + 1] < rank, logs[s : s + 1], 0.0)
    colour = jnp.sum(jnp.exp(front) * slabs, axis=0, keepdims=True)
    opacity = 1.0 - jnp.exp(jnp.sum(logs, axis=0, keepdims=True))
    row = jnp.where(channel[:1] == 3, opacity, colour)
    for ch in range(4):
        out_ref[ch] = jnp.broadcast_to(turn(row, -ch * CELLS * UP, 1)[:, : CELLS * UP], (UP, CELLS * UP))


def call(kernel, outs, scratch=(), in_hbm=False, first_out_hbm=False):
    shapes = tuple(jax.ShapeDtypeStruct(shape, jnp.float32) for shape in outs)
    extra = {}
    if in_hbm:
        extra["in_specs"] = [pl.BlockSpec(memory_space=pltpu.HBM)] * 3
    if first_out_hbm:
        spaces = [pltpu.HBM] + [pltpu.VMEM] * (len(outs) - 1)
        extra["out_specs"] = tuple(pl.BlockSpec(memory_space=space) for space in spaces)
    return pl.pallas_call(
        kernel,
        out_shape=shapes,
        scratch_shapes=scratch,
        compiler_params=pltpu.CompilerParams(vmem_limit_bytes=24 * 1024 * 1024),
        **extra,
    )


def both_ways(lo, hi, axis):
    count = lax.axis_size(axis)
    forward = [(i, (i + 1) % count) for i in range(count)]
    backward = [(target, source) for source, target in forward]
    return lax.ppermute(hi, axis, forward), lax.ppermute(lo, axis, backward)


def body(populations, solid_mask, jet_mask, visibility):
    cells = CELLS * CELLS
    f = populations.reshape(27, cells, LANES)
    solid = solid_mask.reshape(cells, LANES)
    jet = jet_mask.reshape(cells, LANES)
    x_shape = (X_COUNT, CELLS, LANES)
    post, lo, hi = call(
        first_kernel,
        ((29, cells, LANES), x_shape, x_shape),
        (
            pltpu.VMEM((27, cells, LANES), jnp.float32),
            pltpu.VMEM((cells, LANES), jnp.int32),
            pltpu.VMEM((cells, LANES), jnp.int32),
            pltpu.SemaphoreType.DMA((CELLS + 2,)),
        ),
        in_hbm=True,
    )(f, solid, jet)
    xlo, xhi = both_ways(lo, hi, "gx")
    y_shape = (Y_COUNT, LANES)
    lo, hi = call(second_kernel, (y_shape, y_shape))(post, xlo, xhi)
    ylo, yhi = both_ways(lo, hi, "gy")
    (main,) = call(faces_kernel, ((29, CELLS, LANES),))(post, xlo, xhi)
    half_shape = (HALF, 2 * CELLS, LANES)
    halo, face, lo, hi = call(
        third_kernel, ((29, (SPAN + 1) * CELLS, LANES), (29, 2 * CELLS, LANES), half_shape, half_shape)
    )(ylo, yhi, main)
    zlo, zhi = both_ways(lo, hi, "gz")
    height = SPAN * ROWS + CELLS
    (block,) = call(block_kernel, ((29, height, LANES),))(post, xlo, xhi, halo)
    advanced, slabs = call(
        fourth_kernel,
        ((27, cells, LANES), (CELLS, LANES)),
        (
            pltpu.VMEM((27, height, LANES), jnp.float32),
            pltpu.VMEM((29, 3 * CELLS, LANES), jnp.float32),
            pltpu.VMEM((27, 3 * CELLS, LANES), jnp.float32),
            pltpu.VMEM((3, height, LANES), jnp.float32),
            pltpu.VMEM((27, cells, LANES), jnp.float32),
            pltpu.SemaphoreType.DMA,
        ),
        first_out_hbm=True,
    )(block, face, zlo, zhi)
    slabs = lax.all_to_all(slabs, "gz", 0, 0, tiled=True)
    rank = jnp.broadcast_to(visibility[:, None], (CELLS, LANES))
    (image,) = call(last_kernel, ((4, UP, CELLS * UP),))(slabs, rank)
    return advanced.reshape(27, CELLS, CELLS, LANES), jnp.swapaxes(image, 1, 2)


def solution(mesh):
    return jax.shard_map(
        body,
        mesh=mesh,
        in_specs=(P(None, "gx", "gy", "gz"), P("gx", "gy", "gz"), P("gx", "gy", "gz"), P()),
        out_specs=(P(None, "gx", "gy", "gz"), P(None, "gx", ("gy", "gz"))),
        check_vma=False,
    )
```

```python
import jax
import jax.numpy as jnp
import numpy as np
from jax import lax
from jax.experimental import pallas as pl
from jax.experimental.pallas import tpu as pltpu
from jax.sharding import PartitionSpec as P

UP = 4
CELLS = 8
LANES = 128
REACH = 3
SPAN = CELLS + 2 * REACH
LAST = SPAN - 1
ROWS = 16
HALF = 15
GROUP = 8

omega_rate = 1.25
jet_speed = 0.12
alpha_top = 0.03
solid_alpha = 0.15
shade_scale = 0.002

DIRS = [(a, b, c) for a in (-1, 0, 1) for b in (-1, 0, 1) for c in (-1, 0, 1)]
WEIGHTS = [(8.0 / 27.0, 2.0 / 27.0, 1.0 / 54.0, 1.0 / 216.0)[abs(a) + abs(b) + abs(c)] for a, b, c in DIRS]
SOLID, JET = 27, 28
MASKS = (SOLID, JET)


def axis_list(axis, inward):
    out = []
    for dist, allowed in ((1, (-1, 0, 1)), (2, (0, inward)), (3, (inward,))):
        out += [(i, dist) for i in range(27) if DIRS[i][axis] in allowed]
    out += [(m, dist) for m in MASKS for dist in (1, 2)]
    return out


def held(key, x):
    dist, inward = (-x, 1) if x < 0 else (x - CELLS + 1, -1)
    if dist <= 0:
        return True
    return (key, dist) in axis_list(0, inward)


def corner_list(inward):
    out = []
    for key, dist in axis_list(1, inward):
        first, second = (0, 0) if key in MASKS else DIRS[key][:2]
        for x in (-3, -2, -1, 8, 9, 10):
            far = -(x + first) if x < 0 else x + first - CELLS + 1
            if held(key, x) and not (far >= 2 and dist - inward * second >= 2):
                out.append((key, dist, x))
    return out


X_COUNT = len(axis_list(0, 1))
Y_OWN = len(axis_list(1, 1)) * CELLS
Y_COUNT = Y_OWN + -(-len(corner_list(1)) // 8) * 8


def moments(f):
    third = None
    parts = []
    for a in range(3):
        row = []
        for b in range(3):
            lo, mid, hi = f[9 * a + 3 * b], f[9 * a + 3 * b + 1], f[9 * a + 3 * b + 2]
            row.append((lo + hi) + mid)
            diff = hi - lo
            third = diff if third is None else third + diff
        parts.append(row)
    sums = [(row[0] + row[2]) + row[1] for row in parts]
    second = (parts[0][2] - parts[0][0]) + (parts[1][2] - parts[1][0]) + (parts[2][2] - parts[2][0])
    return (sums[0] + sums[2]) + sums[1], sums[2] - sums[0], second, third


def collide(f, solid, jet):
    density, first, second, third = moments(f)
    scale = 1.0 / density
    ux = jnp.where(jet, jet_speed, first * scale)
    uy = jnp.where(jet, 0.0, second * scale)
    uz = jnp.where(jet, 0.0, third * scale)
    gain = jnp.where(jet, 1.0, omega_rate) * density
    keep = jnp.where(jet, 0.0, 1.0 - omega_rate)
    base = 1.0 - 1.5 * (ux * ux + uy * uy + uz * uz)
    strength = {w: gain * w for w in set(WEIGHTS)}
    post = [None] * 27
    comps = (ux, uy, uz)
    for i in range(14):
        w = strength[WEIGHTS[i]]
        if i == 13:
            post[i] = jnp.where(solid, f[i], w * base + keep * f[i])
            continue
        along = None
        for c, u in zip(DIRS[i], comps):
            if c == 0:
                continue
            if along is None:
                along = u if c > 0 else -u
            else:
                along = along + u if c > 0 else along - u
        even = w * (base + 4.5 * (along * along))
        odd = w * (3.0 * along)
        j = 26 - i
        post[i] = jnp.where(solid, f[j], (even + odd) + keep * f[i])
        post[j] = jnp.where(solid, f[i], (even - odd) + keep * f[j])
    return post


def lanes_of(rows):
    return lax.broadcasted_iota(jnp.int32, (rows, LANES), 1)


def turn(value, shift, axis):
    size = value.shape[axis]
    if isinstance(shift, int):
        shift = shift % size
        if shift == 0:
            return value
    return pltpu.roll(value, shift, axis)


def first_kernel(f_ref, mask_ref, p_ref, lo_ref, hi_ref):
    for k, key in enumerate(MASKS):
        p_ref[key] = mask_ref[k]
    for x in range(CELLS):
        rows = pl.ds(x * CELLS, CELLS)
        f = [f_ref[i, rows, :] for i in range(27)]
        post = collide(f, mask_ref[0, rows, :] > 0.5, mask_ref[1, rows, :] > 0.5)
        for i in range(27):
            p_ref[i, rows, :] = post[i]
    for k, (key, dist) in enumerate(axis_list(0, -1)):
        lo_ref[k] = p_ref[key, pl.ds((dist - 1) * CELLS, CELLS), :]
    for k, (key, dist) in enumerate(axis_list(0, 1)):
        hi_ref[k] = p_ref[key, pl.ds((CELLS - dist) * CELLS, CELLS), :]


LOW_AT = {entry: k for k, entry in enumerate(axis_list(0, 1))}
HIGH_AT = {entry: k for k, entry in enumerate(axis_list(0, -1))}


def plane_ref(key, x, p_ref, xlo_ref, xhi_ref):
    if x < 0:
        return xlo_ref.at[LOW_AT[(key, -x)]]
    if x >= CELLS:
        return xhi_ref.at[HIGH_AT[(key, x - CELLS + 1)]]
    return p_ref.at[key, pl.ds(x * CELLS, CELLS), :]


def second_kernel(p_ref, xlo_ref, xhi_ref, lo_ref, hi_ref):
    for inward, out_ref in ((-1, lo_ref), (1, hi_ref)):
        for k, (key, dist) in enumerate(axis_list(1, inward)):
            row = dist - 1 if inward < 0 else CELLS - dist
            out_ref[pl.ds(k * CELLS, CELLS), :] = p_ref[key, pl.ds(row, CELLS, stride=CELLS), :]
        for k, (key, dist, x) in enumerate(corner_list(inward)):
            row = dist - 1 if inward < 0 else CELLS - dist
            out_ref[pl.ds(Y_OWN + k, 1), :] = plane_ref(key, x, p_ref, xlo_ref, xhi_ref)[pl.ds(row, 1), :]


def pack(tiles):
    group = lanes_of(CELLS) // GROUP
    acc = [jnp.zeros((CELLS, LANES), jnp.float32)] * 29
    for place, shift, load in tiles:
        here = group == place % (LANES // GROUP)
        for key in range(29):
            value = load(key)
            if value is not None:
                acc[key] = jnp.where(here, turn(value, shift, 1), acc[key])
    return acc


def faces_kernel(p_ref, xlo_ref, xhi_ref, low_ref, high_ref):
    def load(key, plane):
        if held(key, plane - REACH):
            return plane_ref(key, plane - REACH, p_ref, xlo_ref, xhi_ref)[...]

    for out_ref, start in ((low_ref, 3), (high_ref, 5)):
        tiles = [
            (LAST - plane, GROUP * (LAST - plane) + start, lambda key, plane=plane: load(key, plane))
            for plane in range(SPAN)
        ]
        for key, value in enumerate(pack(tiles)):
            out_ref[key] = value


def pack_halo(h_ref, start):
    upper = lax.broadcasted_iota(jnp.int32, (CELLS, LANES), 0) < CELLS // 2
    tiles = [
        (
            LAST - tile,
            GROUP * (LAST - tile) + start,
            lambda key, tile=tile: h_ref[key, pl.ds(tile * CELLS, CELLS), :],
        )
        for tile in range(SPAN + 1)
    ]
    return [jnp.where(upper, turn(value, GROUP, 1), value) for value in pack(tiles)]


def third_kernel(ylo_ref, yhi_ref, main_ref, h_ref, z_ref, lo_ref, hi_ref):
    for inward, in_ref in ((1, ylo_ref), (-1, yhi_ref)):
        for k, (key, dist) in enumerate(axis_list(1, inward)):
            start = CELLS * REACH + CELLS - dist if inward > 0 else CELLS * (REACH + 1) + dist - 1
            h_ref[key, pl.ds(start, CELLS, stride=CELLS), :] = in_ref[pl.ds(k * CELLS, CELLS), :]
        for k, (key, dist, x) in enumerate(corner_list(inward)):
            plane = x + REACH
            row = CELLS * plane + CELLS - dist if inward > 0 else CELLS * (plane + 1) + dist - 1
            h_ref[key, pl.ds(row, 1), :] = in_ref[pl.ds(Y_OWN + k, 1), :]
    halo = pack_halo(h_ref, 3)
    early = lanes_of(CELLS) % GROUP < REACH
    for key in range(29):
        z_ref[key] = halo[key]
    for part, values in enumerate(([main_ref[key] for key in range(29)], halo)):
        rows = pl.ds(part * CELLS, CELLS)
        for out_ref, shift in ((lo_ref, -REACH), (hi_ref, REACH)):
            for k in range(HALF):
                value = values[k]
                if k + HALF < 29:
                    other = turn(values[k + HALF], shift, 1)
                    value = jnp.where(early, other, value) if shift < 0 else jnp.where(early, value, other)
                out_ref[k, rows, :] = value


def plane_rows(plane, y):
    return pl.ds(plane * ROWS + CELLS + y, CELLS)


def row_slice(plane, y):
    return pl.ds(plane * ROWS + CELLS + y, CELLS, stride=ROWS)


def velocity(f, solid):
    density, first, second, third = moments(f)
    scale = (1.0 - solid) / density
    return first * scale, second * scale, third * scale


def steps_kernel(p_ref, xlo_ref, xhi_ref, h_ref, adv_ref, flow_ref, high_ref, e_ref, g_ref):
    for plane in range(SPAN):
        for key in range(29):
            if held(key, plane - REACH):
                e_ref[key, plane_rows(plane, 0), :] = plane_ref(key, plane - REACH, p_ref, xlo_ref, xhi_ref)[...]
    for tile in range(SPAN + 1):
        for key in range(29):
            e_ref[key, pl.ds(tile * ROWS, CELLS), :] = h_ref[key, pl.ds(tile * CELLS, CELLS), :]

    def stream(ref, rows):
        out = [None] * 27
        for move in (-1, 1, 0):
            for i, (a, b, c) in enumerate(DIRS):
                if c == move:
                    out[i] = turn(ref[i, rows(a, b), :], c, 1)
        return out

    def plane_stream(ref, plane, y):
        return stream(ref, lambda a, b: plane_rows(plane - a, y - b))

    def row_stream(ref, y):
        return stream(ref, lambda a, b: row_slice(REACH - a, y - b))

    def settle(rows, f):
        post = collide(f, e_ref[SOLID, rows, :] > 0.5, e_ref[JET, rows, :] > 0.5)
        for i in range(27):
            g_ref[i, rows, :] = post[i]

    def step_one(plane, y):
        settle(plane_rows(plane, y), plane_stream(e_ref, plane, y))

    def step_one_own(k, carry):
        step_one(REACH + 2 * k, 0)
        step_one(REACH + 2 * k + 1, 0)
        return carry

    def step_one_halo(k, carry):
        plane = k + 1 + CELLS * (k // 2)
        step_one(plane, -2)
        step_one(plane, 6)
        return carry

    lax.fori_loop(0, CELLS // 2, step_one_own, 0)
    lax.fori_loop(0, 4, step_one_halo, 0)
    for y in (-2, -1, CELLS, CELLS + 1):
        settle(row_slice(REACH, y), row_stream(e_ref, y))

    def store_flow(rows, f):
        for c, value in enumerate(velocity(f, e_ref[SOLID, rows, :])):
            flow_ref[c, rows, :] = value

    def step_two(plane):
        f = plane_stream(g_ref, plane, 0)
        rows = pl.ds(pl.multiple_of((plane - REACH) * CELLS, CELLS), CELLS)
        for i in range(27):
            adv_ref[i, rows, :] = f[i]
        store_flow(plane_rows(plane, 0), f)

    def step_two_own(k, carry):
        step_two(REACH + 2 * k)
        step_two(REACH + 2 * k + 1)
        return carry

    lax.fori_loop(0, CELLS // 2, step_two_own, 0)
    for plane in (REACH - 1, REACH + CELLS):
        store_flow(plane_rows(plane, 0), plane_stream(g_ref, plane, 0))
    for y in (-1, CELLS):
        store_flow(row_slice(REACH, y), row_stream(g_ref, y))
    for key, value in enumerate(pack_halo(h_ref, 5)):
        high_ref[key] = value


def render_kernel(
    p_ref, adv_ref, flow_ref, lmain_ref, lhalo_ref, hmain_ref, hhalo_ref, zlo_ref, zhi_ref,
    adv_hbm, out_ref, low_ref, high_ref, lpost_ref, hpost_ref, done_ref, rim_ref, sem,
):
    lane = lanes_of(CELLS)
    slot = lane % GROUP
    ends = (lane < 2) | (lane >= LANES - 2)

    for part in range(2):
        rows = pl.ds(part * CELLS, CELLS)
        own_low, own_high = (lmain_ref, hmain_ref) if part == 0 else (lhalo_ref, hhalo_ref)
        low = [zlo_ref[key, rows, :] for key in range(HALF)]
        low += [turn(zlo_ref[key, rows, :], -REACH, 1) for key in range(29 - HALF)]
        high = [turn(zhi_ref[key, rows, :], 2, 1) for key in range(HALF)]
        high += [turn(zhi_ref[key, rows, :], REACH + 2, 1) for key in range(29 - HALF)]
        for key in range(29):
            first = jnp.where(slot < 3, low[key], own_low[key])
            second = jnp.where(slot >= 5, high[key], own_high[key])
            for start in (CELLS,) if part == 0 else (0, 2 * CELLS):
                low_ref[key, pl.ds(start, CELLS), :] = first
                high_ref[key, pl.ds(start, CELLS), :] = second

    def edge_stream(ref, rows):
        out = [None] * 27
        for a in (-1, 0, 1):
            for c in (-1, 0, 1):
                for b in (-1, 0, 1):
                    i = 9 * a + 3 * b + c + 13
                    out[i] = turn(ref[i, rows(b), :], c - GROUP * a, 1)
        return out

    for y in (-2, 6):
        for ref, post_ref in ((low_ref, lpost_ref), (high_ref, hpost_ref)):
            rows = pl.ds(CELLS + y, CELLS)
            f = edge_stream(ref, lambda b: pl.ds(CELLS + y - b, CELLS))
            post = collide(f, ref[SOLID, rows, :] > 0.5, ref[JET, rows, :] > 0.5)
            for i in range(27):
                post_ref[i, rows, :] = post[i]

    def join(low, high):
        return jnp.where(lanes_of(low.shape[0]) % GROUP < 3, turn(high, -2, 1), low)

    f_low = edge_stream(lpost_ref, lambda b: pl.ds(CELLS - b, CELLS))
    flow_low = velocity(f_low, low_ref[SOLID, pl.ds(CELLS, CELLS), :])
    f_high = edge_stream(hpost_ref, lambda b: pl.ds(CELLS - b, CELLS))
    flow_high = velocity(f_high, high_ref[SOLID, pl.ds(CELLS, CELLS), :])
    joined = [join(low, high) for low, high in zip(f_low, f_high)]
    for x in range(CELLS):
        rows = pl.ds(x * CELLS, CELLS)
        shift = -(GROUP * (LAST - REACH - x) + 3)
        for i in range(27):
            done_ref[i, rows, :] = jnp.where(ends, turn(joined[i], shift, 1), adv_ref[i, rows, :])
    save = pltpu.make_async_copy(done_ref, adv_hbm, sem)
    save.start()
    joined = [join(low, high) for low, high in zip(flow_low, flow_high)]
    for plane in range(REACH - 1, REACH + CELLS + 1):
        rows = plane_rows(plane, 0)
        shift = -(GROUP * (LAST - plane) + 3)
        for c in range(3):
            rim_ref[c, rows, :] = jnp.where(ends, turn(joined[c], shift, 1), flow_ref[c, rows, :])
    beside = pl.ds(CELLS - 1, 2, stride=CELLS + 1)
    side_low = velocity(
        edge_stream(lpost_ref, lambda b: pl.ds(CELLS - 1 - b, 2, stride=CELLS + 1)), low_ref[SOLID, beside, :]
    )
    side_high = velocity(
        edge_stream(hpost_ref, lambda b: pl.ds(CELLS - 1 - b, 2, stride=CELLS + 1)), high_ref[SOLID, beside, :]
    )
    for c in range(3):
        joined = join(side_low[c], side_high[c])
        for k, y in enumerate((-1, CELLS)):
            rows = row_slice(REACH, y)
            spread = pltpu.roll(
                jnp.broadcast_to(joined[k : k + 1], (CELLS, LANES)),
                LANES - (GROUP * (LAST - REACH) + 3),
                1,
                stride=GROUP,
                stride_axis=0,
            )
            rim_ref[c, rows, :] = jnp.where(ends, spread, flow_ref[c, rows, :])

    own = range(REACH, REACH + CELLS)

    def here(c):
        return [rim_ref[c, plane_rows(plane, 0), :] for plane in own]

    def along_first(c):
        return [
            0.5 * (rim_ref[c, plane_rows(plane + 1, 0), :] - rim_ref[c, plane_rows(plane - 1, 0), :]) for plane in own
        ]

    def along_second(c):
        return [0.5 * (rim_ref[c, plane_rows(plane, 1), :] - rim_ref[c, plane_rows(plane, -1), :]) for plane in own]

    def along_third(c):
        low = [turn(value, 1, 1) for value in here(c)]
        high = [turn(value, -1, 1) for value in here(c)]
        out = []
        for k, plane in enumerate(own):
            base = GROUP * (LAST - plane)
            first = jnp.where(lane == 0, turn(flow_low[c], -2 - base, 1), low[k])
            second = jnp.where(lane == LANES - 1, turn(flow_high[c], -6 - base, 1), high[k])
            out.append(0.5 * (second - first))
        return out

    def minus(first, second):
        return [a - b for a, b in zip(first, second)]

    vort = (
        minus(along_second(2), along_third(1)),
        minus(along_third(0), along_first(2)),
        minus(along_first(1), along_second(0)),
    )
    s_two = jnp.concatenate([a * a + b * b + c * c for a, b, c in zip(*vort)], axis=0)
    flow_first = jnp.concatenate(here(0), axis=0)
    solid_on = p_ref[SOLID] > 0.5
    ratio = s_two / (s_two + shade_scale)
    alpha = jnp.where(solid_on, solid_alpha, alpha_top * (1.0 - jnp.exp(-s_two / shade_scale)))
    red = jnp.where(solid_on, 0.6, 0.3 + 1.5 * ratio)
    green = jnp.where(solid_on, 0.6, 1.2 - 0.9 * ratio)
    blue = jnp.where(solid_on, 0.6, 0.8 + 0.4 * jnp.tanh(20.0 * flow_first))
    logs = jnp.log1p(-alpha)
    running = logs
    wide = lanes_of(CELLS * CELLS)
    for step in (1, 2, 4, 8, 16, 32, 64):
        running = running + jnp.where(wide >= step, turn(running, step, 1), 0.0)
    weight = alpha * jnp.exp(running - logs)
    acc = jnp.zeros((CELLS, LANES), jnp.float32)
    for ch, value in enumerate((red * weight, green * weight, blue * weight, logs)):
        total = jnp.sum(value, axis=1, keepdims=True)
        for x in range(CELLS):
            acc = jnp.where(lane // UP == ch * CELLS + x, total[x * CELLS : (x + 1) * CELLS], acc)
    out_ref[...] = acc
    save.wait()


def last_kernel(slab_ref, rank_ref, out_ref):
    slabs = slab_ref[...]
    rank = rank_ref[...]
    channel = lanes_of(CELLS) // (CELLS * UP)
    logs = slabs
    for ch in range(3):
        logs = jnp.where(channel == ch, turn(slabs, (ch + 1) * CELLS * UP, 1), logs)
    front = jnp.zeros_like(slabs)
    for s in range(CELLS):
        front = front + jnp.where(rank[s : s + 1] < rank, logs[s : s + 1], 0.0)
    colour = jnp.sum(jnp.exp(front) * slabs, axis=0, keepdims=True)
    opacity = 1.0 - jnp.exp(jnp.sum(logs, axis=0, keepdims=True))
    row = jnp.where(channel[:1] == 3, opacity, colour)
    for ch in range(4):
        out_ref[ch] = jnp.broadcast_to(turn(row, -ch * CELLS * UP, 1)[:, : CELLS * UP], (UP, CELLS * UP))


def call(kernel, outs, scratch=(), first_out_hbm=False):
    shapes = tuple(jax.ShapeDtypeStruct(shape, jnp.float32) for shape in outs)
    extra = {}
    if first_out_hbm:
        spaces = [pltpu.HBM] + [pltpu.VMEM] * (len(outs) - 1)
        extra["out_specs"] = tuple(pl.BlockSpec(memory_space=space) for space in spaces)
    return pl.pallas_call(
        kernel,
        out_shape=shapes,
        scratch_shapes=scratch,
        compiler_params=pltpu.CompilerParams(vmem_limit_bytes=24 * 1024 * 1024),
        **extra,
    )


def both_ways(lo, hi, axis):
    count = lax.axis_size(axis)
    forward = [(i, (i + 1) % count) for i in range(count)]
    backward = [(target, source) for source, target in forward]
    return lax.ppermute(hi, axis, forward), lax.ppermute(lo, axis, backward)


def body(populations, solid_mask, jet_mask, visibility):
    cells = CELLS * CELLS
    f = populations.reshape(27, cells, LANES)
    masks = jnp.stack([solid_mask, jet_mask]).astype(jnp.float32).reshape(2, cells, LANES)
    x_shape = (X_COUNT, CELLS, LANES)
    post, lo, hi = call(first_kernel, ((29, cells, LANES), x_shape, x_shape))(f, masks)
    xlo, xhi = both_ways(lo, hi, "gx")
    y_shape = (Y_COUNT, LANES)
    lo, hi = call(second_kernel, (y_shape, y_shape))(post, xlo, xhi)
    ylo, yhi = both_ways(lo, hi, "gy")
    tile_shape = (29, CELLS, LANES)
    low, high = call(faces_kernel, (tile_shape, tile_shape))(post, xlo, xhi)
    half_shape = (HALF, 2 * CELLS, LANES)
    halo, low_halo, lo, hi = call(
        third_kernel, ((29, (SPAN + 1) * CELLS, LANES), tile_shape, half_shape, half_shape)
    )(ylo, yhi, low)
    zlo, zhi = both_ways(lo, hi, "gz")
    height = SPAN * ROWS + CELLS
    moved, flow, high_halo = call(
        steps_kernel,
        ((27, cells, LANES), (3, height, LANES), tile_shape),
        (pltpu.VMEM((29, height, LANES), jnp.float32), pltpu.VMEM((27, height, LANES), jnp.float32)),
    )(post, xlo, xhi, halo)
    edge = pltpu.VMEM((29, 3 * CELLS, LANES), jnp.float32)
    edge_post = pltpu.VMEM((27, 3 * CELLS, LANES), jnp.float32)
    advanced, slabs = call(
        render_kernel,
        ((27, cells, LANES), (CELLS, LANES)),
        (
            edge,
            edge,
            edge_post,
            edge_post,
            pltpu.VMEM((27, cells, LANES), jnp.float32),
            pltpu.VMEM((3, height, LANES), jnp.float32),
            pltpu.SemaphoreType.DMA,
        ),
        first_out_hbm=True,
    )(post, moved, flow, low, low_halo, high, high_halo, zlo, zhi)
    slabs = lax.all_to_all(slabs, "gz", 0, 0, tiled=True)
    rank = jnp.broadcast_to(visibility[:, None], (CELLS, LANES))
    (image,) = call(last_kernel, ((4, UP, CELLS * UP),))(slabs, rank)
    return advanced.reshape(27, CELLS, CELLS, LANES), jnp.swapaxes(image, 1, 2)


def solution(mesh):
    return jax.shard_map(
        body,
        mesh=mesh,
        in_specs=(P(None, "gx", "gy", "gz"), P("gx", "gy", "gz"), P("gx", "gy", "gz"), P()),
        out_specs=(P(None, "gx", "gy", "gz"), P(None, "gx", ("gy", "gz"))),
        check_vma=False,
    )
```

```python
import jax
import jax.numpy as jnp
import numpy as np
from jax import lax
from jax.experimental import pallas as pl
from jax.experimental.pallas import tpu as pltpu
from jax.sharding import PartitionSpec as P

UP = 4
CELLS = 8
LANES = 128
REACH = 3
SPAN = CELLS + 2 * REACH
LAST = SPAN - 1
ROWS = 16
HALF = 15
GROUP = 8

omega_rate = 1.25
jet_speed = 0.12
alpha_top = 0.03
solid_alpha = 0.15
shade_scale = 0.002

DIRS = [(a, b, c) for a in (-1, 0, 1) for b in (-1, 0, 1) for c in (-1, 0, 1)]
WEIGHTS = [(8.0 / 27.0, 2.0 / 27.0, 1.0 / 54.0, 1.0 / 216.0)[abs(a) + abs(b) + abs(c)] for a, b, c in DIRS]
SOLID, JET = 27, 28
MASKS = (SOLID, JET)


def axis_list(axis, inward):
    out = []
    for dist, allowed in ((1, (-1, 0, 1)), (2, (0, inward)), (3, (inward,))):
        out += [(i, dist) for i in range(27) if DIRS[i][axis] in allowed]
    out += [(m, dist) for m in MASKS for dist in (1, 2)]
    return out


def held(key, x):
    dist, inward = (-x, 1) if x < 0 else (x - CELLS + 1, -1)
    if dist <= 0:
        return True
    return (key, dist) in axis_list(0, inward)


def corner_list(inward):
    out = []
    for key, dist in axis_list(1, inward):
        first, second = (0, 0) if key in MASKS else DIRS[key][:2]
        for x in (-3, -2, -1, 8, 9, 10):
            far = -(x + first) if x < 0 else x + first - CELLS + 1
            if held(key, x) and not (far >= 2 and dist - inward * second >= 2):
                out.append((key, dist, x))
    return out


X_COUNT = len(axis_list(0, 1))
Y_OWN = len(axis_list(1, 1)) * CELLS
Y_CORNER = -(-len(corner_list(1)) // 8) * 8


def moments(f):
    third = None
    parts = []
    for a in range(3):
        row = []
        for b in range(3):
            lo, mid, hi = f[9 * a + 3 * b], f[9 * a + 3 * b + 1], f[9 * a + 3 * b + 2]
            row.append((lo + hi) + mid)
            diff = hi - lo
            third = diff if third is None else third + diff
        parts.append(row)
    sums = [(row[0] + row[2]) + row[1] for row in parts]
    second = (parts[0][2] - parts[0][0]) + (parts[1][2] - parts[1][0]) + (parts[2][2] - parts[2][0])
    return (sums[0] + sums[2]) + sums[1], sums[2] - sums[0], second, third


def collide(f, solid, jet):
    density, first, second, third = moments(f)
    scale = 1.0 / density
    ux = jnp.where(jet, jet_speed, first * scale)
    uy = jnp.where(jet, 0.0, second * scale)
    uz = jnp.where(jet, 0.0, third * scale)
    gain = jnp.where(jet, 1.0, omega_rate) * density
    keep = jnp.where(jet, 0.0, 1.0 - omega_rate)
    base = 1.0 - 1.5 * (ux * ux + uy * uy + uz * uz)
    strength = {w: gain * w for w in set(WEIGHTS)}
    post = [None] * 27
    comps = (ux, uy, uz)
    for i in range(14):
        w = strength[WEIGHTS[i]]
        if i == 13:
            post[i] = jnp.where(solid, f[i], w * base + keep * f[i])
            continue
        along = None
        for c, u in zip(DIRS[i], comps):
            if c == 0:
                continue
            if along is None:
                along = u if c > 0 else -u
            else:
                along = along + u if c > 0 else along - u
        even = w * (base + 4.5 * (along * along))
        odd = w * (3.0 * along)
        j = 26 - i
        post[i] = jnp.where(solid, f[j], (even + odd) + keep * f[i])
        post[j] = jnp.where(solid, f[i], (even - odd) + keep * f[j])
    return post


def lanes_of(rows):
    return lax.broadcasted_iota(jnp.int32, (rows, LANES), 1)


def turn(value, shift, axis):
    size = value.shape[axis]
    if isinstance(shift, int):
        shift = shift % size
        if shift == 0:
            return value
    return pltpu.roll(value, shift, axis)


def first_kernel(f_ref, mask_ref, p_ref, lo_ref, hi_ref, ylo_ref, yhi_ref):
    for k, key in enumerate(MASKS):
        p_ref[key] = mask_ref[k]
    for x in range(CELLS):
        rows = pl.ds(x * CELLS, CELLS)
        f = [f_ref[i, rows, :] for i in range(27)]
        post = collide(f, mask_ref[0, rows, :] > 0.5, mask_ref[1, rows, :] > 0.5)
        for i in range(27):
            p_ref[i, rows, :] = post[i]
    for k, (key, dist) in enumerate(axis_list(0, -1)):
        lo_ref[k] = p_ref[key, pl.ds((dist - 1) * CELLS, CELLS), :]
    for k, (key, dist) in enumerate(axis_list(0, 1)):
        hi_ref[k] = p_ref[key, pl.ds((CELLS - dist) * CELLS, CELLS), :]
    for inward, out_ref in ((-1, ylo_ref), (1, yhi_ref)):
        for k, (key, dist) in enumerate(axis_list(1, inward)):
            row = dist - 1 if inward < 0 else CELLS - dist
            out_ref[pl.ds(k * CELLS, CELLS), :] = p_ref[key, pl.ds(row, CELLS, stride=CELLS), :]


LOW_AT = {entry: k for k, entry in enumerate(axis_list(0, 1))}
HIGH_AT = {entry: k for k, entry in enumerate(axis_list(0, -1))}


def plane_ref(key, x, p_ref, xlo_ref, xhi_ref):
    if x < 0:
        return xlo_ref.at[LOW_AT[(key, -x)]]
    if x >= CELLS:
        return xhi_ref.at[HIGH_AT[(key, x - CELLS + 1)]]
    return p_ref.at[key, pl.ds(x * CELLS, CELLS), :]


def second_kernel(xlo_ref, xhi_ref, lo_ref, hi_ref):
    for inward, out_ref in ((-1, lo_ref), (1, hi_ref)):
        for k, (key, dist, x) in enumerate(corner_list(inward)):
            row = dist - 1 if inward < 0 else CELLS - dist
            out_ref[pl.ds(k, 1), :] = plane_ref(key, x, None, xlo_ref, xhi_ref)[pl.ds(row, 1), :]


def pack(tiles):
    group = lanes_of(CELLS) // GROUP
    acc = [jnp.zeros((CELLS, LANES), jnp.float32)] * 29
    for place, shift, load in tiles:
        here = group == place % (LANES // GROUP)
        for key in range(29):
            value = load(key)
            if value is not None:
                acc[key] = jnp.where(here, turn(value, shift, 1), acc[key])
    return acc


def faces_kernel(p_ref, xlo_ref, xhi_ref, low_ref, high_ref):
    def load(key, plane):
        if held(key, plane - REACH):
            return plane_ref(key, plane - REACH, p_ref, xlo_ref, xhi_ref)[...]

    for out_ref, start in ((low_ref, 3), (high_ref, 5)):
        tiles = [
            (LAST - plane, GROUP * (LAST - plane) + start, lambda key, plane=plane: load(key, plane))
            for plane in range(SPAN)
        ]
        for key, value in enumerate(pack(tiles)):
            out_ref[key] = value


def pack_halo(h_ref, start):
    upper = lax.broadcasted_iota(jnp.int32, (CELLS, LANES), 0) < CELLS // 2
    tiles = [
        (
            LAST - tile,
            GROUP * (LAST - tile) + start,
            lambda key, tile=tile: h_ref[key, pl.ds(tile * CELLS, CELLS), :],
        )
        for tile in range(SPAN + 1)
    ]
    return [jnp.where(upper, turn(value, GROUP, 1), value) for value in pack(tiles)]


def third_kernel(ylo_ref, yhi_ref, clo_ref, chi_ref, main_ref, h_ref, z_ref, lo_ref, hi_ref):
    for inward, in_ref, corner_ref in ((1, ylo_ref, clo_ref), (-1, yhi_ref, chi_ref)):
        for k, (key, dist) in enumerate(axis_list(1, inward)):
            start = CELLS * REACH + CELLS - dist if inward > 0 else CELLS * (REACH + 1) + dist - 1
            h_ref[key, pl.ds(start, CELLS, stride=CELLS), :] = in_ref[pl.ds(k * CELLS, CELLS), :]
        for k, (key, dist, x) in enumerate(corner_list(inward)):
            plane = x + REACH
            row = CELLS * plane + CELLS - dist if inward > 0 else CELLS * (plane + 1) + dist - 1
            h_ref[key, pl.ds(row, 1), :] = corner_ref[pl.ds(k, 1), :]
    halo = pack_halo(h_ref, 3)
    early = lanes_of(CELLS) % GROUP < REACH
    for key in range(29):
        z_ref[key] = halo[key]
    for part, values in enumerate(([main_ref[key] for key in range(29)], halo)):
        rows = pl.ds(part * CELLS, CELLS)
        for out_ref, shift in ((lo_ref, -REACH), (hi_ref, REACH)):
            for k in range(HALF):
                value = values[k]
                if k + HALF < 29:
                    other = turn(values[k + HALF], shift, 1)
                    value = jnp.where(early, other, value) if shift < 0 else jnp.where(early, value, other)
                out_ref[k, rows, :] = value


def plane_rows(plane, y):
    return pl.ds(plane * ROWS + CELLS + y, CELLS)


def row_slice(plane, y):
    return pl.ds(plane * ROWS + CELLS + y, CELLS, stride=ROWS)


def velocity(f, solid):
    density, first, second, third = moments(f)
    scale = (1.0 - solid) / density
    return first * scale, second * scale, third * scale


def steps_kernel(p_ref, xlo_ref, xhi_ref, h_ref, adv_ref, flow_ref, high_ref, e_ref, g_ref):
    for plane in range(SPAN):
        for key in range(29):
            if held(key, plane - REACH):
                e_ref[key, plane_rows(plane, 0), :] = plane_ref(key, plane - REACH, p_ref, xlo_ref, xhi_ref)[...]
    for tile in range(SPAN + 1):
        for key in range(29):
            e_ref[key, pl.ds(tile * ROWS, CELLS), :] = h_ref[key, pl.ds(tile * CELLS, CELLS), :]

    def stream(ref, rows):
        out = [None] * 27
        for move in (-1, 1, 0):
            for i, (a, b, c) in enumerate(DIRS):
                if c == move:
                    out[i] = turn(ref[i, rows(a, b), :], c, 1)
        return out

    def plane_stream(ref, plane, y):
        return stream(ref, lambda a, b: plane_rows(plane - a, y - b))

    def row_stream(ref, y):
        return stream(ref, lambda a, b: row_slice(REACH - a, y - b))

    def settle(rows, f):
        post = collide(f, e_ref[SOLID, rows, :] > 0.5, e_ref[JET, rows, :] > 0.5)
        for i in range(27):
            g_ref[i, rows, :] = post[i]

    def step_one(plane, y):
        settle(plane_rows(plane, y), plane_stream(e_ref, plane, y))

    def step_one_own(k, carry):
        step_one(REACH + 2 * k, 0)
        step_one(REACH + 2 * k + 1, 0)
        return carry

    def step_one_halo(k, carry):
        plane = k + 1 + CELLS * (k // 2)
        step_one(plane, -2)
        step_one(plane, 6)
        return carry

    lax.fori_loop(0, CELLS // 2, step_one_own, 0)
    lax.fori_loop(0, 4, step_one_halo, 0)
    for y in (-2, -1, CELLS, CELLS + 1):
        settle(row_slice(REACH, y), row_stream(e_ref, y))

    def store_flow(rows, f):
        for c, value in enumerate(velocity(f, e_ref[SOLID, rows, :])):
            flow_ref[c, rows, :] = value

    def step_two(plane):
        f = plane_stream(g_ref, plane, 0)
        rows = pl.ds(pl.multiple_of((plane - REACH) * CELLS, CELLS), CELLS)
        for i in range(27):
            adv_ref[i, rows, :] = f[i]
        store_flow(plane_rows(plane, 0), f)

    def step_two_own(k, carry):
        step_two(REACH + 2 * k)
        step_two(REACH + 2 * k + 1)
        return carry

    lax.fori_loop(0, CELLS // 2, step_two_own, 0)
    for plane in (REACH - 1, REACH + CELLS):
        store_flow(plane_rows(plane, 0), plane_stream(g_ref, plane, 0))
    for y in (-1, CELLS):
        store_flow(row_slice(REACH, y), row_stream(g_ref, y))
    for key, value in enumerate(pack_halo(h_ref, 5)):
        high_ref[key] = value


def render_kernel(
    p_ref, adv_ref, flow_ref, lmain_ref, lhalo_ref, hmain_ref, hhalo_ref, zlo_ref, zhi_ref,
    adv_hbm, out_ref, low_ref, high_ref, lpost_ref, hpost_ref, done_ref, rim_ref, sem,
):
    lane = lanes_of(CELLS)
    slot = lane % GROUP
    ends = (lane < 2) | (lane >= LANES - 2)

    for part in range(2):
        rows = pl.ds(part * CELLS, CELLS)
        own_low, own_high = (lmain_ref, hmain_ref) if part == 0 else (lhalo_ref, hhalo_ref)
        low = [zlo_ref[key, rows, :] for key in range(HALF)]
        low += [turn(zlo_ref[key, rows, :], -REACH, 1) for key in range(29 - HALF)]
        high = [turn(zhi_ref[key, rows, :], 2, 1) for key in range(HALF)]
        high += [turn(zhi_ref[key, rows, :], REACH + 2, 1) for key in range(29 - HALF)]
        for key in range(29):
            first = jnp.where(slot < 3, low[key], own_low[key])
            second = jnp.where(slot >= 5, high[key], own_high[key])
            for start in (CELLS,) if part == 0 else (0, 2 * CELLS):
                low_ref[key, pl.ds(start, CELLS), :] = first
                high_ref[key, pl.ds(start, CELLS), :] = second

    def edge_stream(ref, rows):
        out = [None] * 27
        for a in (-1, 0, 1):
            for c in (-1, 0, 1):
                for b in (-1, 0, 1):
                    i = 9 * a + 3 * b + c + 13
                    out[i] = turn(ref[i, rows(b), :], c - GROUP * a, 1)
        return out

    for y in (-2, 6):
        for ref, post_ref in ((low_ref, lpost_ref), (high_ref, hpost_ref)):
            rows = pl.ds(CELLS + y, CELLS)
            f = edge_stream(ref, lambda b: pl.ds(CELLS + y - b, CELLS))
            post = collide(f, ref[SOLID, rows, :] > 0.5, ref[JET, rows, :] > 0.5)
            for i in range(27):
                post_ref[i, rows, :] = post[i]

    def join(low, high):
        return jnp.where(lanes_of(low.shape[0]) % GROUP < 3, turn(high, -2, 1), low)

    f_low = edge_stream(lpost_ref, lambda b: pl.ds(CELLS - b, CELLS))
    flow_low = velocity(f_low, low_ref[SOLID, pl.ds(CELLS, CELLS), :])
    f_high = edge_stream(hpost_ref, lambda b: pl.ds(CELLS - b, CELLS))
    flow_high = velocity(f_high, high_ref[SOLID, pl.ds(CELLS, CELLS), :])
    joined = [join(low, high) for low, high in zip(f_low, f_high)]
    for x in range(CELLS):
        rows = pl.ds(x * CELLS, CELLS)
        shift = -(GROUP * (LAST - REACH - x) + 3)
        for i in range(27):
            done_ref[i, rows, :] = jnp.where(ends, turn(joined[i], shift, 1), adv_ref[i, rows, :])
    save = pltpu.make_async_copy(done_ref, adv_hbm, sem)
    save.start()
    joined = [join(low, high) for low, high in zip(flow_low, flow_high)]
    for plane in range(REACH - 1, REACH + CELLS + 1):
        rows = plane_rows(plane, 0)
        shift = -(GROUP * (LAST - plane) + 3)
        for c in range(3):
            rim_ref[c, rows, :] = jnp.where(ends, turn(joined[c], shift, 1), flow_ref[c, rows, :])
    beside = pl.ds(CELLS - 1, 2, stride=CELLS + 1)
    side_low = velocity(
        edge_stream(lpost_ref, lambda b: pl.ds(CELLS - 1 - b, 2, stride=CELLS + 1)), low_ref[SOLID, beside, :]
    )
    side_high = velocity(
        edge_stream(hpost_ref, lambda b: pl.ds(CELLS - 1 - b, 2, stride=CELLS + 1)), high_ref[SOLID, beside, :]
    )
    for c in range(3):
        joined = join(side_low[c], side_high[c])
        for k, y in enumerate((-1, CELLS)):
            rows = row_slice(REACH, y)
            spread = pltpu.roll(
                jnp.broadcast_to(joined[k : k + 1], (CELLS, LANES)),
                LANES - (GROUP * (LAST - REACH) + 3),
                1,
                stride=GROUP,
                stride_axis=0,
            )
            rim_ref[c, rows, :] = jnp.where(ends, spread, flow_ref[c, rows, :])

    own = range(REACH, REACH + CELLS)

    def here(c):
        return [rim_ref[c, plane_rows(plane, 0), :] for plane in own]

    def along_first(c):
        return [
            0.5 * (rim_ref[c, plane_rows(plane + 1, 0), :] - rim_ref[c, plane_rows(plane - 1, 0), :]) for plane in own
        ]

    def along_second(c):
        return [0.5 * (rim_ref[c, plane_rows(plane, 1), :] - rim_ref[c, plane_rows(plane, -1), :]) for plane in own]

    def along_third(c):
        low = [turn(value, 1, 1) for value in here(c)]
        high = [turn(value, -1, 1) for value in here(c)]
        out = []
        for k, plane in enumerate(own):
            base = GROUP * (LAST - plane)
            first = jnp.where(lane == 0, turn(flow_low[c], -2 - base, 1), low[k])
            second = jnp.where(lane == LANES - 1, turn(flow_high[c], -6 - base, 1), high[k])
            out.append(0.5 * (second - first))
        return out

    def minus(first, second):
        return [a - b for a, b in zip(first, second)]

    vort = (
        minus(along_second(2), along_third(1)),
        minus(along_third(0), along_first(2)),
        minus(along_first(1), along_second(0)),
    )
    s_two = jnp.concatenate([a * a + b * b + c * c for a, b, c in zip(*vort)], axis=0)
    flow_first = jnp.concatenate(here(0), axis=0)
    solid_on = p_ref[SOLID] > 0.5
    ratio = s_two / (s_two + shade_scale)
    alpha = jnp.where(solid_on, solid_alpha, alpha_top * (1.0 - jnp.exp(-s_two / shade_scale)))
    red = jnp.where(solid_on, 0.6, 0.3 + 1.5 * ratio)
    green = jnp.where(solid_on, 0.6, 1.2 - 0.9 * ratio)
    blue = jnp.where(solid_on, 0.6, 0.8 + 0.4 * jnp.tanh(20.0 * flow_first))
    logs = jnp.log1p(-alpha)
    running = logs
    wide = lanes_of(CELLS * CELLS)
    for step in (1, 2, 4, 8, 16, 32, 64):
        running = running + jnp.where(wide >= step, turn(running, step, 1), 0.0)
    weight = alpha * jnp.exp(running - logs)
    acc = jnp.zeros((CELLS, LANES), jnp.float32)
    for ch, value in enumerate((red * weight, green * weight, blue * weight, logs)):
        total = jnp.sum(value, axis=1, keepdims=True)
        for x in range(CELLS):
            acc = jnp.where(lane // UP == ch * CELLS + x, total[x * CELLS : (x + 1) * CELLS], acc)
    out_ref[...] = acc
    save.wait()


def last_kernel(slab_ref, rank_ref, out_ref):
    slabs = slab_ref[...]
    rank = rank_ref[...]
    channel = lanes_of(CELLS) // (CELLS * UP)
    logs = slabs
    for ch in range(3):
        logs = jnp.where(channel == ch, turn(slabs, (ch + 1) * CELLS * UP, 1), logs)
    front = jnp.zeros_like(slabs)
    for s in range(CELLS):
        front = front + jnp.where(rank[s : s + 1] < rank, logs[s : s + 1], 0.0)
    colour = jnp.sum(jnp.exp(front) * slabs, axis=0, keepdims=True)
    opacity = 1.0 - jnp.exp(jnp.sum(logs, axis=0, keepdims=True))
    row = jnp.where(channel[:1] == 3, opacity, colour)
    for ch in range(4):
        out_ref[ch] = jnp.broadcast_to(turn(row, -ch * CELLS * UP, 1)[:, : CELLS * UP], (UP, CELLS * UP))


def call(kernel, outs, scratch=(), first_out_hbm=False):
    shapes = tuple(jax.ShapeDtypeStruct(shape, jnp.float32) for shape in outs)
    extra = {}
    if first_out_hbm:
        spaces = [pltpu.HBM] + [pltpu.VMEM] * (len(outs) - 1)
        extra["out_specs"] = tuple(pl.BlockSpec(memory_space=space) for space in spaces)
    return pl.pallas_call(
        kernel,
        out_shape=shapes,
        scratch_shapes=scratch,
        compiler_params=pltpu.CompilerParams(vmem_limit_bytes=24 * 1024 * 1024),
        **extra,
    )


def both_ways(lo, hi, axis):
    count = lax.axis_size(axis)
    forward = [(i, (i + 1) % count) for i in range(count)]
    backward = [(target, source) for source, target in forward]
    return lax.ppermute(hi, axis, forward), lax.ppermute(lo, axis, backward)


def body(populations, solid_mask, jet_mask, visibility):
    cells = CELLS * CELLS
    f = populations.reshape(27, cells, LANES)
    masks = jnp.stack([solid_mask, jet_mask]).astype(jnp.float32).reshape(2, cells, LANES)
    x_shape = (X_COUNT, CELLS, LANES)
    y_shape = (Y_OWN, LANES)
    post, lo, hi, down, up = call(first_kernel, ((29, cells, LANES), x_shape, x_shape, y_shape, y_shape))(f, masks)
    xlo, xhi = both_ways(lo, hi, "gx")
    ylo, yhi = both_ways(down, up, "gy")
    corner_shape = (Y_CORNER, LANES)
    lo, hi = call(second_kernel, (corner_shape, corner_shape))(xlo, xhi)
    clo, chi = both_ways(lo, hi, "gy")
    tile_shape = (29, CELLS, LANES)
    low, high = call(faces_kernel, (tile_shape, tile_shape))(post, xlo, xhi)
    half_shape = (HALF, 2 * CELLS, LANES)
    halo, low_halo, lo, hi = call(
        third_kernel, ((29, (SPAN + 1) * CELLS, LANES), tile_shape, half_shape, half_shape)
    )(ylo, yhi, clo, chi, low)
    zlo, zhi = both_ways(lo, hi, "gz")
    height = SPAN * ROWS + CELLS
    moved, flow, high_halo = call(
        steps_kernel,
        ((27, cells, LANES), (3, height, LANES), tile_shape),
        (pltpu.VMEM((29, height, LANES), jnp.float32), pltpu.VMEM((27, height, LANES), jnp.float32)),
    )(post, xlo, xhi, halo)
    edge = pltpu.VMEM((29, 3 * CELLS, LANES), jnp.float32)
    edge_post = pltpu.VMEM((27, 3 * CELLS, LANES), jnp.float32)
    advanced, slabs = call(
        render_kernel,
        ((27, cells, LANES), (CELLS, LANES)),
        (
            edge,
            edge,
            edge_post,
            edge_post,
            pltpu.VMEM((27, cells, LANES), jnp.float32),
            pltpu.VMEM((3, height, LANES), jnp.float32),
            pltpu.SemaphoreType.DMA,
        ),
        first_out_hbm=True,
    )(post, moved, flow, low, low_halo, high, high_halo, zlo, zhi)
    slabs = lax.all_to_all(slabs, "gz", 0, 0, tiled=True)
    rank = jnp.broadcast_to(visibility[:, None], (CELLS, LANES))
    (image,) = call(last_kernel, ((4, UP, CELLS * UP),))(slabs, rank)
    return advanced.reshape(27, CELLS, CELLS, LANES), jnp.swapaxes(image, 1, 2)


def solution(mesh):
    return jax.shard_map(
        body,
        mesh=mesh,
        in_specs=(P(None, "gx", "gy", "gz"), P("gx", "gy", "gz"), P("gx", "gy", "gz"), P()),
        out_specs=(P(None, "gx", "gy", "gz"), P(None, "gx", ("gy", "gz"))),
        check_vma=False,
    )
```

```python
import jax
import jax.numpy as jnp
import numpy as np
from jax import lax
from jax.experimental import pallas as pl
from jax.experimental.pallas import tpu as pltpu
from jax.sharding import PartitionSpec as P

UP = 4
CELLS = 8
LANES = 128
REACH = 3
SPAN = CELLS + 2 * REACH
LAST = SPAN - 1
ROWS = 16
HALF = 15
GROUP = 8

omega_rate = 1.25
jet_speed = 0.12
alpha_top = 0.03
solid_alpha = 0.15
shade_scale = 0.002

DIRS = [(a, b, c) for a in (-1, 0, 1) for b in (-1, 0, 1) for c in (-1, 0, 1)]
WEIGHTS = [(8.0 / 27.0, 2.0 / 27.0, 1.0 / 54.0, 1.0 / 216.0)[abs(a) + abs(b) + abs(c)] for a, b, c in DIRS]
SOLID, JET = 27, 28
MASKS = (SOLID, JET)


def axis_list(axis, inward):
    out = []
    for dist, allowed in ((1, (-1, 0, 1)), (2, (0, inward)), (3, (inward,))):
        out += [(i, dist) for i in range(27) if DIRS[i][axis] in allowed]
    out += [(m, dist) for m in MASKS for dist in (1, 2)]
    return out


def held(key, cell, axis=0):
    dist, inward = (-cell, 1) if cell < 0 else (cell - CELLS + 1, -1)
    if dist <= 0:
        return True
    return (key, dist) in axis_list(axis, inward)


def corner_list(inward):
    out = []
    for key, dist in axis_list(0, inward):
        first, second = (0, 0) if key in MASKS else DIRS[key][:2]
        for y in (-3, -2, -1, 8, 9, 10):
            far = -(y + second) if y < 0 else y + second - CELLS + 1
            if held(key, y, 1) and not (far >= 2 and dist - inward * first >= 2):
                out.append((key, dist, y))
    return out


X_COUNT = len(axis_list(0, 1))
CORNER = -(-len(corner_list(1)) // 8) * 8


def moments(f):
    third = None
    parts = []
    for a in range(3):
        row = []
        for b in range(3):
            lo, mid, hi = f[9 * a + 3 * b], f[9 * a + 3 * b + 1], f[9 * a + 3 * b + 2]
            row.append((lo + hi) + mid)
            diff = hi - lo
            third = diff if third is None else third + diff
        parts.append(row)
    sums = [(row[0] + row[2]) + row[1] for row in parts]
    second = (parts[0][2] - parts[0][0]) + (parts[1][2] - parts[1][0]) + (parts[2][2] - parts[2][0])
    return (sums[0] + sums[2]) + sums[1], sums[2] - sums[0], second, third


def collide(f, solid, jet):
    density, first, second, third = moments(f)
    scale = 1.0 / density
    ux = jnp.where(jet, jet_speed, first * scale)
    uy = jnp.where(jet, 0.0, second * scale)
    uz = jnp.where(jet, 0.0, third * scale)
    gain = jnp.where(jet, 1.0, omega_rate) * density
    keep = jnp.where(jet, 0.0, 1.0 - omega_rate)
    base = 1.0 - 1.5 * (ux * ux + uy * uy + uz * uz)
    strength = {w: gain * w for w in set(WEIGHTS)}
    post = [None] * 27
    comps = (ux, uy, uz)
    for i in range(14):
        w = strength[WEIGHTS[i]]
        if i == 13:
            post[i] = jnp.where(solid, f[i], w * base + keep * f[i])
            continue
        along = None
        for c, u in zip(DIRS[i], comps):
            if c == 0:
                continue
            if along is None:
                along = u if c > 0 else -u
            else:
                along = along + u if c > 0 else along - u
        even = w * (base + 4.5 * (along * along))
        odd = w * (3.0 * along)
        j = 26 - i
        post[i] = jnp.where(solid, f[j], (even + odd) + keep * f[i])
        post[j] = jnp.where(solid, f[i], (even - odd) + keep * f[j])
    return post


def lanes_of(rows):
    return lax.broadcasted_iota(jnp.int32, (rows, LANES), 1)


def turn(value, shift, axis):
    size = value.shape[axis]
    if isinstance(shift, int):
        shift = shift % size
        if shift == 0:
            return value
    return pltpu.roll(value, shift, axis)


def is_even(axis):
    return lax.axis_index(axis) % 2 == 0


def first_kernel(f_ref, mask_ref, p_ref, xa_ref, xb_ref, ya_ref, yb_ref):
    for k, key in enumerate(MASKS):
        p_ref[key] = mask_ref[k]
    for x in range(CELLS):
        rows = pl.ds(x * CELLS, CELLS)
        f = [f_ref[i, rows, :] for i in range(27)]
        post = collide(f, mask_ref[0, rows, :] > 0.5, mask_ref[1, rows, :] > 0.5)
        for i in range(27):
            p_ref[i, rows, :] = post[i]
    even = is_even("gx")
    for k, (low, high) in enumerate(zip(axis_list(0, -1), axis_list(0, 1))):
        lo = p_ref[low[0], pl.ds((low[1] - 1) * CELLS, CELLS), :]
        hi = p_ref[high[0], pl.ds((CELLS - high[1]) * CELLS, CELLS), :]
        xa_ref[k] = jnp.where(even, hi, lo)
        xb_ref[k] = jnp.where(even, lo, hi)
    even = is_even("gy")
    for k, (low, high) in enumerate(zip(axis_list(1, -1), axis_list(1, 1))):
        lo = p_ref[low[0], pl.ds(low[1] - 1, CELLS, stride=CELLS), :]
        hi = p_ref[high[0], pl.ds(CELLS - high[1], CELLS, stride=CELLS), :]
        ya_ref[k] = jnp.where(even, hi, lo)
        yb_ref[k] = jnp.where(even, lo, hi)


ENTRY = {(axis, inward): {e: k for k, e in enumerate(axis_list(axis, inward))} for axis in (0, 1) for inward in (1, -1)}


def from_pair(axis, inward, dist, key, a_ref, b_ref, even, rows=slice(None)):
    k = ENTRY[(axis, inward)][(key, dist)]
    if inward > 0:
        return jnp.where(even, b_ref[k, rows, :], a_ref[k, rows, :])
    return jnp.where(even, a_ref[k, rows, :], b_ref[k, rows, :])


def plane_value(key, x, p_ref, xa_ref, xb_ref, even):
    if x < 0:
        return from_pair(0, 1, -x, key, xa_ref, xb_ref, even)
    if x >= CELLS:
        return from_pair(0, -1, x - CELLS + 1, key, xa_ref, xb_ref, even)
    return p_ref[key, pl.ds(x * CELLS, CELLS), :]


def second_kernel(ya_ref, yb_ref, lo_ref, hi_ref):
    even = is_even("gy")
    for inward, out_ref in ((-1, lo_ref), (1, hi_ref)):
        for k, (key, dist, y) in enumerate(corner_list(inward)):
            row = pl.ds(dist - 1 if inward < 0 else CELLS - dist, 1)
            side, far = (1, -y) if y < 0 else (-1, y - CELLS + 1)
            out_ref[pl.ds(k, 1), :] = from_pair(1, side, far, key, ya_ref, yb_ref, even, row)


def pack(tiles):
    group = lanes_of(CELLS) // GROUP
    acc = [jnp.zeros((CELLS, LANES), jnp.float32)] * 29
    for place, shift, load in tiles:
        here = group == place % (LANES // GROUP)
        for key in range(29):
            value = load(key)
            if value is not None:
                acc[key] = jnp.where(here, turn(value, shift, 1), acc[key])
    return acc


def faces_kernel(p_ref, xa_ref, xb_ref, low_ref, high_ref):
    even = is_even("gx")

    def load(key, plane):
        if held(key, plane - REACH):
            return plane_value(key, plane - REACH, p_ref, xa_ref, xb_ref, even)

    for out_ref, start in ((low_ref, 3), (high_ref, 5)):
        tiles = [
            (LAST - plane, GROUP * (LAST - plane) + start, lambda key, plane=plane: load(key, plane))
            for plane in range(SPAN)
        ]
        for key, value in enumerate(pack(tiles)):
            out_ref[key] = value


def pack_halo(h_ref, start):
    upper = lax.broadcasted_iota(jnp.int32, (CELLS, LANES), 0) < CELLS // 2
    tiles = [
        (
            LAST - tile,
            GROUP * (LAST - tile) + start,
            lambda key, tile=tile: h_ref[key, pl.ds(tile * CELLS, CELLS), :],
        )
        for tile in range(SPAN + 1)
    ]
    return [jnp.where(upper, turn(value, GROUP, 1), value) for value in pack(tiles)]


def third_kernel(ya_ref, yb_ref, clo_ref, chi_ref, main_ref, h_ref, z_ref, lo_ref, hi_ref):
    even = is_even("gy")
    for inward in (1, -1):
        for key, dist in axis_list(1, inward):
            start = CELLS * REACH + CELLS - dist if inward > 0 else CELLS * (REACH + 1) + dist - 1
            h_ref[key, pl.ds(start, CELLS, stride=CELLS), :] = from_pair(1, inward, dist, key, ya_ref, yb_ref, even)
    for inward, corner_ref in ((1, clo_ref), (-1, chi_ref)):
        for k, (key, dist, y) in enumerate(corner_list(inward)):
            plane = REACH - dist if inward > 0 else REACH + CELLS - 1 + dist
            row = CELLS * plane + CELLS + y if y < 0 else CELLS * (plane + 1) + y - CELLS
            h_ref[key, pl.ds(row, 1), :] = corner_ref[pl.ds(k, 1), :]
    halo = pack_halo(h_ref, 3)
    early = lanes_of(CELLS) % GROUP < REACH
    for key in range(29):
        z_ref[key] = halo[key]
    for part, values in enumerate(([main_ref[key] for key in range(29)], halo)):
        rows = pl.ds(part * CELLS, CELLS)
        for out_ref, shift in ((lo_ref, -REACH), (hi_ref, REACH)):
            for k in range(HALF):
                value = values[k]
                if k + HALF < 29:
                    other = turn(values[k + HALF], shift, 1)
                    value = jnp.where(early, other, value) if shift < 0 else jnp.where(early, value, other)
                out_ref[k, rows, :] = value


def plane_rows(plane, y):
    return pl.ds(plane * ROWS + CELLS + y, CELLS)


def row_slice(plane, y):
    return pl.ds(plane * ROWS + CELLS + y, CELLS, stride=ROWS)


def velocity(f, solid):
    density, first, second, third = moments(f)
    scale = (1.0 - solid) / density
    return first * scale, second * scale, third * scale


def steps_kernel(p_ref, xa_ref, xb_ref, h_ref, adv_ref, flow_ref, high_ref, e_ref, g_ref):
    even = is_even("gx")
    for plane in range(SPAN):
        for key in range(29):
            if held(key, plane - REACH):
                e_ref[key, plane_rows(plane, 0), :] = plane_value(key, plane - REACH, p_ref, xa_ref, xb_ref, even)
    for tile in range(SPAN + 1):
        for key in range(29):
            e_ref[key, pl.ds(tile * ROWS, CELLS), :] = h_ref[key, pl.ds(tile * CELLS, CELLS), :]

    def stream(ref, rows):
        out = [None] * 27
        for move in (-1, 1, 0):
            for i, (a, b, c) in enumerate(DIRS):
                if c == move:
                    out[i] = turn(ref[i, rows(a, b), :], c, 1)
        return out

    def plane_stream(ref, plane, y):
        return stream(ref, lambda a, b: plane_rows(plane - a, y - b))

    def row_stream(ref, y):
        return stream(ref, lambda a, b: row_slice(REACH - a, y - b))

    def settle(rows, f):
        post = collide(f, e_ref[SOLID, rows, :] > 0.5, e_ref[JET, rows, :] > 0.5)
        for i in range(27):
            g_ref[i, rows, :] = post[i]

    def step_one(plane, y):
        settle(plane_rows(plane, y), plane_stream(e_ref, plane, y))

    def step_one_own(k, carry):
        step_one(REACH + 2 * k, 0)
        step_one(REACH + 2 * k + 1, 0)
        return carry

    def step_one_halo(k, carry):
        plane = k + 1 + CELLS * (k // 2)
        step_one(plane, -2)
        step_one(plane, 6)
        return carry

    lax.fori_loop(0, CELLS // 2, step_one_own, 0)
    lax.fori_loop(0, 4, step_one_halo, 0)
    for y in (-2, -1, CELLS, CELLS + 1):
        settle(row_slice(REACH, y), row_stream(e_ref, y))

    def store_flow(rows, f):
        for c, value in enumerate(velocity(f, e_ref[SOLID, rows, :])):
            flow_ref[c, rows, :] = value

    def step_two(plane):
        f = plane_stream(g_ref, plane, 0)
        rows = pl.ds(pl.multiple_of((plane - REACH) * CELLS, CELLS), CELLS)
        for i in range(27):
            adv_ref[i, rows, :] = f[i]
        store_flow(plane_rows(plane, 0), f)

    def step_two_own(k, carry):
        step_two(REACH + 2 * k)
        step_two(REACH + 2 * k + 1)
        return carry

    lax.fori_loop(0, CELLS // 2, step_two_own, 0)
    for plane in (REACH - 1, REACH + CELLS):
        store_flow(plane_rows(plane, 0), plane_stream(g_ref, plane, 0))
    for y in (-1, CELLS):
        store_flow(row_slice(REACH, y), row_stream(g_ref, y))
    for key, value in enumerate(pack_halo(h_ref, 5)):
        high_ref[key] = value


def render_kernel(
    p_ref, adv_ref, flow_ref, lmain_ref, lhalo_ref, hmain_ref, hhalo_ref, zlo_ref, zhi_ref,
    adv_hbm, out_ref, low_ref, high_ref, lpost_ref, hpost_ref, done_ref, rim_ref, sem,
):
    lane = lanes_of(CELLS)
    slot = lane % GROUP
    ends = (lane < 2) | (lane >= LANES - 2)

    for part in range(2):
        rows = pl.ds(part * CELLS, CELLS)
        own_low, own_high = (lmain_ref, hmain_ref) if part == 0 else (lhalo_ref, hhalo_ref)
        low = [zlo_ref[key, rows, :] for key in range(HALF)]
        low += [turn(zlo_ref[key, rows, :], -REACH, 1) for key in range(29 - HALF)]
        high = [turn(zhi_ref[key, rows, :], 2, 1) for key in range(HALF)]
        high += [turn(zhi_ref[key, rows, :], REACH + 2, 1) for key in range(29 - HALF)]
        for key in range(29):
            first = jnp.where(slot < 3, low[key], own_low[key])
            second = jnp.where(slot >= 5, high[key], own_high[key])
            for start in (CELLS,) if part == 0 else (0, 2 * CELLS):
                low_ref[key, pl.ds(start, CELLS), :] = first
                high_ref[key, pl.ds(start, CELLS), :] = second

    def edge_stream(ref, rows):
        out = [None] * 27
        for a in (-1, 0, 1):
            for c in (-1, 0, 1):
                for b in (-1, 0, 1):
                    i = 9 * a + 3 * b + c + 13
                    out[i] = turn(ref[i, rows(b), :], c - GROUP * a, 1)
        return out

    for y in (-2, 6):
        for ref, post_ref in ((low_ref, lpost_ref), (high_ref, hpost_ref)):
            rows = pl.ds(CELLS + y, CELLS)
            f = edge_stream(ref, lambda b: pl.ds(CELLS + y - b, CELLS))
            post = collide(f, ref[SOLID, rows, :] > 0.5, ref[JET, rows, :] > 0.5)
            for i in range(27):
                post_ref[i, rows, :] = post[i]

    def join(low, high):
        return jnp.where(lanes_of(low.shape[0]) % GROUP < 3, turn(high, -2, 1), low)

    f_low = edge_stream(lpost_ref, lambda b: pl.ds(CELLS - b, CELLS))
    flow_low = velocity(f_low, low_ref[SOLID, pl.ds(CELLS, CELLS), :])
    f_high = edge_stream(hpost_ref, lambda b: pl.ds(CELLS - b, CELLS))
    flow_high = velocity(f_high, high_ref[SOLID, pl.ds(CELLS, CELLS), :])
    joined = [join(low, high) for low, high in zip(f_low, f_high)]
    for x in range(CELLS):
        rows = pl.ds(x * CELLS, CELLS)
        shift = -(GROUP * (LAST - REACH - x) + 3)
        for i in range(27):
            done_ref[i, rows, :] = jnp.where(ends, turn(joined[i], shift, 1), adv_ref[i, rows, :])
    save = pltpu.make_async_copy(done_ref, adv_hbm, sem)
    save.start()
    joined = [join(low, high) for low, high in zip(flow_low, flow_high)]
    for plane in range(REACH - 1, REACH + CELLS + 1):
        rows = plane_rows(plane, 0)
        shift = -(GROUP * (LAST - plane) + 3)
        for c in range(3):
            rim_ref[c, rows, :] = jnp.where(ends, turn(joined[c], shift, 1), flow_ref[c, rows, :])
    beside = pl.ds(CELLS - 1, 2, stride=CELLS + 1)
    side_low = velocity(
        edge_stream(lpost_ref, lambda b: pl.ds(CELLS - 1 - b, 2, stride=CELLS + 1)), low_ref[SOLID, beside, :]
    )
    side_high = velocity(
        edge_stream(hpost_ref, lambda b: pl.ds(CELLS - 1 - b, 2, stride=CELLS + 1)), high_ref[SOLID, beside, :]
    )
    for c in range(3):
        joined = join(side_low[c], side_high[c])
        for k, y in enumerate((-1, CELLS)):
            rows = row_slice(REACH, y)
            spread = pltpu.roll(
                jnp.broadcast_to(joined[k : k + 1], (CELLS, LANES)),
                LANES - (GROUP * (LAST - REACH) + 3),
                1,
                stride=GROUP,
                stride_axis=0,
            )
            rim_ref[c, rows, :] = jnp.where(ends, spread, flow_ref[c, rows, :])

    own = range(REACH, REACH + CELLS)

    def here(c):
        return [rim_ref[c, plane_rows(plane, 0), :] for plane in own]

    def along_first(c):
        return [
            0.5 * (rim_ref[c, plane_rows(plane + 1, 0), :] - rim_ref[c, plane_rows(plane - 1, 0), :]) for plane in own
        ]

    def along_second(c):
        return [0.5 * (rim_ref[c, plane_rows(plane, 1), :] - rim_ref[c, plane_rows(plane, -1), :]) for plane in own]

    def along_third(c):
        low = [turn(value, 1, 1) for value in here(c)]
        high = [turn(value, -1, 1) for value in here(c)]
        out = []
        for k, plane in enumerate(own):
            base = GROUP * (LAST - plane)
            first = jnp.where(lane == 0, turn(flow_low[c], -2 - base, 1), low[k])
            second = jnp.where(lane == LANES - 1, turn(flow_high[c], -6 - base, 1), high[k])
            out.append(0.5 * (second - first))
        return out

    def minus(first, second):
        return [a - b for a, b in zip(first, second)]

    vort = (
        minus(along_second(2), along_third(1)),
        minus(along_third(0), along_first(2)),
        minus(along_first(1), along_second(0)),
    )
    s_two = jnp.concatenate([a * a + b * b + c * c for a, b, c in zip(*vort)], axis=0)
    flow_first = jnp.concatenate(here(0), axis=0)
    solid_on = p_ref[SOLID] > 0.5
    ratio = s_two / (s_two + shade_scale)
    alpha = jnp.where(solid_on, solid_alpha, alpha_top * (1.0 - jnp.exp(-s_two / shade_scale)))
    red = jnp.where(solid_on, 0.6, 0.3 + 1.5 * ratio)
    green = jnp.where(solid_on, 0.6, 1.2 - 0.9 * ratio)
    blue = jnp.where(solid_on, 0.6, 0.8 + 0.4 * jnp.tanh(20.0 * flow_first))
    logs = jnp.log1p(-alpha)
    running = logs
    wide = lanes_of(CELLS * CELLS)
    for step in (1, 2, 4, 8, 16, 32, 64):
        running = running + jnp.where(wide >= step, turn(running, step, 1), 0.0)
    weight = alpha * jnp.exp(running - logs)
    acc = jnp.zeros((CELLS, LANES), jnp.float32)
    for ch, value in enumerate((red * weight, green * weight, blue * weight, logs)):
        total = jnp.sum(value, axis=1, keepdims=True)
        for x in range(CELLS):
            acc = jnp.where(lane // UP == ch * CELLS + x, total[x * CELLS : (x + 1) * CELLS], acc)
    out_ref[...] = acc
    save.wait()


def last_kernel(slab_ref, rank_ref, out_ref):
    slabs = slab_ref[...]
    rank = rank_ref[...]
    channel = lanes_of(CELLS) // (CELLS * UP)
    logs = slabs
    for ch in range(3):
        logs = jnp.where(channel == ch, turn(slabs, (ch + 1) * CELLS * UP, 1), logs)
    front = jnp.zeros_like(slabs)
    for s in range(CELLS):
        front = front + jnp.where(rank[s : s + 1] < rank, logs[s : s + 1], 0.0)
    colour = jnp.sum(jnp.exp(front) * slabs, axis=0, keepdims=True)
    opacity = 1.0 - jnp.exp(jnp.sum(logs, axis=0, keepdims=True))
    row = jnp.where(channel[:1] == 3, opacity, colour)
    for ch in range(4):
        out_ref[ch] = jnp.broadcast_to(turn(row, -ch * CELLS * UP, 1)[:, : CELLS * UP], (UP, CELLS * UP))


def call(kernel, outs, scratch=(), first_out_hbm=False):
    shapes = tuple(jax.ShapeDtypeStruct(shape, jnp.float32) for shape in outs)
    extra = {}
    if first_out_hbm:
        spaces = [pltpu.HBM] + [pltpu.VMEM] * (len(outs) - 1)
        extra["out_specs"] = tuple(pl.BlockSpec(memory_space=space) for space in spaces)
    return pl.pallas_call(
        kernel,
        out_shape=shapes,
        scratch_shapes=scratch,
        compiler_params=pltpu.CompilerParams(vmem_limit_bytes=24 * 1024 * 1024),
        **extra,
    )


def both_ways(lo, hi, axis):
    count = lax.axis_size(axis)
    forward = [(i, (i + 1) % count) for i in range(count)]
    backward = [(target, source) for source, target in forward]
    return lax.ppermute(hi, axis, forward), lax.ppermute(lo, axis, backward)


def in_pairs(first, second, axis):
    count = lax.axis_size(axis)
    out = []
    for start, value in ((0, first), (1, second)):
        pairs = []
        for i in range(start, count + start, 2):
            left, right = i % count, (i + 1) % count
            pairs += [(left, right), (right, left)]
        out.append(lax.ppermute(value, axis, pairs))
    return out


def body(populations, solid_mask, jet_mask, visibility):
    cells = CELLS * CELLS
    f = populations.reshape(27, cells, LANES)
    masks = jnp.stack([solid_mask, jet_mask]).astype(jnp.float32).reshape(2, cells, LANES)
    send_shape = (X_COUNT, CELLS, LANES)
    post, xa, xb, ya, yb = call(first_kernel, ((29, cells, LANES),) + (send_shape,) * 4)(f, masks)
    ya, yb = in_pairs(ya, yb, "gy")
    xa, xb = in_pairs(xa, xb, "gx")
    corner_shape = (CORNER, LANES)
    lo, hi = call(second_kernel, (corner_shape, corner_shape))(ya, yb)
    clo, chi = both_ways(lo, hi, "gx")
    tile_shape = (29, CELLS, LANES)
    low, high = call(faces_kernel, (tile_shape, tile_shape))(post, xa, xb)
    half_shape = (HALF, 2 * CELLS, LANES)
    halo, low_halo, lo, hi = call(
        third_kernel, ((29, (SPAN + 1) * CELLS, LANES), tile_shape, half_shape, half_shape)
    )(ya, yb, clo, chi, low)
    zlo, zhi = both_ways(lo, hi, "gz")
    height = SPAN * ROWS + CELLS
    moved, flow, high_halo = call(
        steps_kernel,
        ((27, cells, LANES), (3, height, LANES), tile_shape),
        (pltpu.VMEM((29, height, LANES), jnp.float32), pltpu.VMEM((27, height, LANES), jnp.float32)),
    )(post, xa, xb, halo)
    edge = pltpu.VMEM((29, 3 * CELLS, LANES), jnp.float32)
    edge_post = pltpu.VMEM((27, 3 * CELLS, LANES), jnp.float32)
    advanced, slabs = call(
        render_kernel,
        ((27, cells, LANES), (CELLS, LANES)),
        (
            edge,
            edge,
            edge_post,
            edge_post,
            pltpu.VMEM((27, cells, LANES), jnp.float32),
            pltpu.VMEM((3, height, LANES), jnp.float32),
            pltpu.SemaphoreType.DMA,
        ),
        first_out_hbm=True,
    )(post, moved, flow, low, low_halo, high, high_halo, zlo, zhi)
    slabs = lax.all_to_all(slabs, "gz", 0, 0, tiled=True)
    rank = jnp.broadcast_to(visibility[:, None], (CELLS, LANES))
    (image,) = call(last_kernel, ((4, UP, CELLS * UP),))(slabs, rank)
    return advanced.reshape(27, CELLS, CELLS, LANES), jnp.swapaxes(image, 1, 2)


def solution(mesh):
    return jax.shard_map(
        body,
        mesh=mesh,
        in_specs=(P(None, "gx", "gy", "gz"), P("gx", "gy", "gz"), P("gx", "gy", "gz"), P()),
        out_specs=(P(None, "gx", "gy", "gz"), P(None, "gx", ("gy", "gz"))),
        check_vma=False,
    )
```

```python
import jax
import jax.numpy as jnp
import numpy as np
from jax import lax
from jax.experimental import pallas as pl
from jax.experimental.pallas import tpu as pltpu
from jax.sharding import PartitionSpec as P

UP = 4
CELLS = 8
LANES = 128
REACH = 3
SPAN = CELLS + 2 * REACH
LAST = SPAN - 1
ROWS = 16
HALF = 15
GROUP = 8

omega_rate = 1.25
jet_speed = 0.12
alpha_top = 0.03
solid_alpha = 0.15
shade_scale = 0.002

DIRS = [(a, b, c) for a in (-1, 0, 1) for b in (-1, 0, 1) for c in (-1, 0, 1)]
WEIGHTS = [(8.0 / 27.0, 2.0 / 27.0, 1.0 / 54.0, 1.0 / 216.0)[abs(a) + abs(b) + abs(c)] for a, b, c in DIRS]
SOLID, JET = 27, 28
MASKS = (SOLID, JET)


def axis_list(axis, inward):
    out = []
    for dist, allowed in ((1, (-1, 0, 1)), (2, (0, inward)), (3, (inward,))):
        out += [(i, dist) for i in range(27) if DIRS[i][axis] in allowed]
    out += [(m, dist) for m in MASKS for dist in (1, 2)]
    return out


def held(key, cell, axis=0):
    dist, inward = (-cell, 1) if cell < 0 else (cell - CELLS + 1, -1)
    if dist <= 0:
        return True
    return (key, dist) in axis_list(axis, inward)


def corner_list(inward):
    out = []
    for key, dist in axis_list(0, inward):
        first, second = (0, 0) if key in MASKS else DIRS[key][:2]
        for y in (-3, -2, -1, 8, 9, 10):
            far = -(y + second) if y < 0 else y + second - CELLS + 1
            if held(key, y, 1) and not (far >= 2 and dist - inward * first >= 2):
                out.append((key, dist, y))
    return out


X_COUNT = len(axis_list(0, 1))
CORNER = -(-len(corner_list(1)) // 8) * 8


def moments(f):
    third = None
    parts = []
    for a in range(3):
        row = []
        for b in range(3):
            lo, mid, hi = f[9 * a + 3 * b], f[9 * a + 3 * b + 1], f[9 * a + 3 * b + 2]
            row.append((lo + hi) + mid)
            diff = hi - lo
            third = diff if third is None else third + diff
        parts.append(row)
    sums = [(row[0] + row[2]) + row[1] for row in parts]
    second = (parts[0][2] - parts[0][0]) + (parts[1][2] - parts[1][0]) + (parts[2][2] - parts[2][0])
    return (sums[0] + sums[2]) + sums[1], sums[2] - sums[0], second, third


def collide(f, solid, jet):
    density, first, second, third = moments(f)
    scale = 1.0 / density
    ux = jnp.where(jet, jet_speed, first * scale)
    uy = jnp.where(jet, 0.0, second * scale)
    uz = jnp.where(jet, 0.0, third * scale)
    gain = jnp.where(jet, 1.0, omega_rate) * density
    keep = jnp.where(jet, 0.0, 1.0 - omega_rate)
    base = 1.0 - 1.5 * (ux * ux + uy * uy + uz * uz)
    strength = {w: gain * w for w in set(WEIGHTS)}
    post = [None] * 27
    comps = (ux, uy, uz)
    for i in range(14):
        w = strength[WEIGHTS[i]]
        if i == 13:
            post[i] = jnp.where(solid, f[i], w * base + keep * f[i])
            continue
        along = None
        for c, u in zip(DIRS[i], comps):
            if c == 0:
                continue
            if along is None:
                along = u if c > 0 else -u
            else:
                along = along + u if c > 0 else along - u
        even = w * (base + 4.5 * (along * along))
        odd = w * (3.0 * along)
        j = 26 - i
        post[i] = jnp.where(solid, f[j], (even + odd) + keep * f[i])
        post[j] = jnp.where(solid, f[i], (even - odd) + keep * f[j])
    return post


def lanes_of(rows):
    return lax.broadcasted_iota(jnp.int32, (rows, LANES), 1)


def turn(value, shift, axis):
    size = value.shape[axis]
    if isinstance(shift, int):
        shift = shift % size
        if shift == 0:
            return value
    return pltpu.roll(value, shift, axis)


def is_even(axis):
    return lax.axis_index(axis) % 2 == 0


def first_kernel(f_hbm, solid_hbm, jet_hbm, p_ref, xa_ref, xb_ref, ya_ref, yb_ref, f_ref, solid_ref, jet_ref, sems):
    masks = [
        pltpu.make_async_copy(solid_hbm, solid_ref, sems.at[CELLS]),
        pltpu.make_async_copy(jet_hbm, jet_ref, sems.at[CELLS + 1]),
    ]
    copies = []
    for x in range(CELLS):
        rows = pl.ds(x * CELLS, CELLS)
        copies.append(pltpu.make_async_copy(f_hbm.at[:, rows, :], f_ref.at[:, rows, :], sems.at[x]))
    for copy in masks + copies:
        copy.start()
    for copy in masks:
        copy.wait()
    p_ref[SOLID] = solid_ref[...].astype(jnp.float32)
    p_ref[JET] = jet_ref[...].astype(jnp.float32)
    for x in range(CELLS):
        copies[x].wait()
        rows = pl.ds(x * CELLS, CELLS)
        f = [f_ref[i, rows, :] for i in range(27)]
        post = collide(f, solid_ref[rows, :] == 1, jet_ref[rows, :] == 1)
        for i in range(27):
            p_ref[i, rows, :] = post[i]
    even = is_even("gx")
    for k, (low, high) in enumerate(zip(axis_list(0, -1), axis_list(0, 1))):
        lo = p_ref[low[0], pl.ds((low[1] - 1) * CELLS, CELLS), :]
        hi = p_ref[high[0], pl.ds((CELLS - high[1]) * CELLS, CELLS), :]
        xa_ref[k] = jnp.where(even, hi, lo)
        xb_ref[k] = jnp.where(even, lo, hi)
    even = is_even("gy")
    for k, (low, high) in enumerate(zip(axis_list(1, -1), axis_list(1, 1))):
        lo = p_ref[low[0], pl.ds(low[1] - 1, CELLS, stride=CELLS), :]
        hi = p_ref[high[0], pl.ds(CELLS - high[1], CELLS, stride=CELLS), :]
        ya_ref[k] = jnp.where(even, hi, lo)
        yb_ref[k] = jnp.where(even, lo, hi)


ENTRY = {(axis, inward): {e: k for k, e in enumerate(axis_list(axis, inward))} for axis in (0, 1) for inward in (1, -1)}


def from_pair(axis, inward, dist, key, a_ref, b_ref, even, rows=slice(None)):
    k = ENTRY[(axis, inward)][(key, dist)]
    if inward > 0:
        return jnp.where(even, b_ref[k, rows, :], a_ref[k, rows, :])
    return jnp.where(even, a_ref[k, rows, :], b_ref[k, rows, :])


def plane_value(key, x, p_ref, xa_ref, xb_ref, even):
    if x < 0:
        return from_pair(0, 1, -x, key, xa_ref, xb_ref, even)
    if x >= CELLS:
        return from_pair(0, -1, x - CELLS + 1, key, xa_ref, xb_ref, even)
    return p_ref[key, pl.ds(x * CELLS, CELLS), :]


def second_kernel(ya_ref, yb_ref, lo_ref, hi_ref):
    even = is_even("gy")
    for inward, out_ref in ((-1, lo_ref), (1, hi_ref)):
        for k, (key, dist, y) in enumerate(corner_list(inward)):
            row = pl.ds(dist - 1 if inward < 0 else CELLS - dist, 1)
            side, far = (1, -y) if y < 0 else (-1, y - CELLS + 1)
            out_ref[pl.ds(k, 1), :] = from_pair(1, side, far, key, ya_ref, yb_ref, even, row)


def pack(tiles):
    group = lanes_of(CELLS) // GROUP
    acc = [jnp.zeros((CELLS, LANES), jnp.float32)] * 29
    for place, shift, load in tiles:
        here = group == place % (LANES // GROUP)
        for key in range(29):
            value = load(key)
            if value is not None:
                acc[key] = jnp.where(here, turn(value, shift, 1), acc[key])
    return acc


def faces_kernel(p_ref, xa_ref, xb_ref, low_ref, high_ref):
    even = is_even("gx")

    def load(key, plane):
        if held(key, plane - REACH):
            return plane_value(key, plane - REACH, p_ref, xa_ref, xb_ref, even)

    for out_ref, start in ((low_ref, 3), (high_ref, 5)):
        tiles = [
            (LAST - plane, GROUP * (LAST - plane) + start, lambda key, plane=plane: load(key, plane))
            for plane in range(SPAN)
        ]
        for key, value in enumerate(pack(tiles)):
            out_ref[key] = value


def pack_halo(h_ref, start):
    upper = lax.broadcasted_iota(jnp.int32, (CELLS, LANES), 0) < CELLS // 2
    tiles = [
        (
            LAST - tile,
            GROUP * (LAST - tile) + start,
            lambda key, tile=tile: h_ref[key, pl.ds(tile * CELLS, CELLS), :],
        )
        for tile in range(SPAN + 1)
    ]
    return [jnp.where(upper, turn(value, GROUP, 1), value) for value in pack(tiles)]


def third_kernel(ya_ref, yb_ref, clo_ref, chi_ref, main_ref, h_ref, z_ref, lo_ref, hi_ref):
    even = is_even("gy")
    for inward in (1, -1):
        for key, dist in axis_list(1, inward):
            start = CELLS * REACH + CELLS - dist if inward > 0 else CELLS * (REACH + 1) + dist - 1
            h_ref[key, pl.ds(start, CELLS, stride=CELLS), :] = from_pair(1, inward, dist, key, ya_ref, yb_ref, even)
    for inward, corner_ref in ((1, clo_ref), (-1, chi_ref)):
        for k, (key, dist, y) in enumerate(corner_list(inward)):
            plane = REACH - dist if inward > 0 else REACH + CELLS - 1 + dist
            row = CELLS * plane + CELLS + y if y < 0 else CELLS * (plane + 1) + y - CELLS
            h_ref[key, pl.ds(row, 1), :] = corner_ref[pl.ds(k, 1), :]
    halo = pack_halo(h_ref, 3)
    early = lanes_of(CELLS) % GROUP < REACH
    for key in range(29):
        z_ref[key] = halo[key]
    for part, values in enumerate(([main_ref[key] for key in range(29)], halo)):
        rows = pl.ds(part * CELLS, CELLS)
        for out_ref, shift in ((lo_ref, -REACH), (hi_ref, REACH)):
            for k in range(HALF):
                value = values[k]
                if k + HALF < 29:
                    other = turn(values[k + HALF], shift, 1)
                    value = jnp.where(early, other, value) if shift < 0 else jnp.where(early, value, other)
                out_ref[k, rows, :] = value


def plane_rows(plane, y):
    return pl.ds(plane * ROWS + CELLS + y, CELLS)


def row_slice(plane, y):
    return pl.ds(plane * ROWS + CELLS + y, CELLS, stride=ROWS)


def velocity(f, solid):
    density, first, second, third = moments(f)
    scale = (1.0 - solid) / density
    return first * scale, second * scale, third * scale


def steps_kernel(p_ref, xa_ref, xb_ref, h_ref, adv_ref, flow_ref, high_ref, e_ref, g_ref):
    even = is_even("gx")
    for plane in range(SPAN):
        for key in range(29):
            if held(key, plane - REACH):
                e_ref[key, plane_rows(plane, 0), :] = plane_value(key, plane - REACH, p_ref, xa_ref, xb_ref, even)
    for tile in range(SPAN + 1):
        for key in range(29):
            e_ref[key, pl.ds(tile * ROWS, CELLS), :] = h_ref[key, pl.ds(tile * CELLS, CELLS), :]

    def stream(ref, rows):
        out = [None] * 27
        for move in (-1, 1, 0):
            for i, (a, b, c) in enumerate(DIRS):
                if c == move:
                    out[i] = turn(ref[i, rows(a, b), :], c, 1)
        return out

    def plane_stream(ref, plane, y):
        return stream(ref, lambda a, b: plane_rows(plane - a, y - b))

    def row_stream(ref, y):
        return stream(ref, lambda a, b: row_slice(REACH - a, y - b))

    def settle(rows, f):
        post = collide(f, e_ref[SOLID, rows, :] > 0.5, e_ref[JET, rows, :] > 0.5)
        for i in range(27):
            g_ref[i, rows, :] = post[i]

    def step_one(plane, y):
        settle(plane_rows(plane, y), plane_stream(e_ref, plane, y))

    def step_one_own(k, carry):
        step_one(REACH + 2 * k, 0)
        step_one(REACH + 2 * k + 1, 0)
        return carry

    def step_one_halo(k, carry):
        plane = k + 1 + CELLS * (k // 2)
        step_one(plane, -2)
        step_one(plane, 6)
        return carry

    lax.fori_loop(0, CELLS // 2, step_one_own, 0)
    lax.fori_loop(0, 4, step_one_halo, 0)
    for y in (-2, -1, CELLS, CELLS + 1):
        settle(row_slice(REACH, y), row_stream(e_ref, y))

    def store_flow(rows, f):
        for c, value in enumerate(velocity(f, e_ref[SOLID, rows, :])):
            flow_ref[c, rows, :] = value

    def step_two(plane):
        f = plane_stream(g_ref, plane, 0)
        rows = pl.ds(pl.multiple_of((plane - REACH) * CELLS, CELLS), CELLS)
        for i in range(27):
            adv_ref[i, rows, :] = f[i]
        store_flow(plane_rows(plane, 0), f)

    def step_two_own(k, carry):
        step_two(REACH + 2 * k)
        step_two(REACH + 2 * k + 1)
        return carry

    lax.fori_loop(0, CELLS // 2, step_two_own, 0)
    for plane in (REACH - 1, REACH + CELLS):
        store_flow(plane_rows(plane, 0), plane_stream(g_ref, plane, 0))
    for y in (-1, CELLS):
        store_flow(row_slice(REACH, y), row_stream(g_ref, y))
    for key, value in enumerate(pack_halo(h_ref, 5)):
        high_ref[key] = value


def render_kernel(
    p_ref, adv_ref, flow_ref, lmain_ref, lhalo_ref, hmain_ref, hhalo_ref, zlo_ref, zhi_ref,
    adv_hbm, out_ref, low_ref, high_ref, lpost_ref, hpost_ref, done_ref, rim_ref, sem,
):
    lane = lanes_of(CELLS)
    slot = lane % GROUP
    ends = (lane < 2) | (lane >= LANES - 2)

    for part in range(2):
        rows = pl.ds(part * CELLS, CELLS)
        own_low, own_high = (lmain_ref, hmain_ref) if part == 0 else (lhalo_ref, hhalo_ref)
        low = [zlo_ref[key, rows, :] for key in range(HALF)]
        low += [turn(zlo_ref[key, rows, :], -REACH, 1) for key in range(29 - HALF)]
        high = [turn(zhi_ref[key, rows, :], 2, 1) for key in range(HALF)]
        high += [turn(zhi_ref[key, rows, :], REACH + 2, 1) for key in range(29 - HALF)]
        for key in range(29):
            first = jnp.where(slot < 3, low[key], own_low[key])
            second = jnp.where(slot >= 5, high[key], own_high[key])
            for start in (CELLS,) if part == 0 else (0, 2 * CELLS):
                low_ref[key, pl.ds(start, CELLS), :] = first
                high_ref[key, pl.ds(start, CELLS), :] = second

    def edge_stream(ref, rows):
        out = [None] * 27
        for a in (-1, 0, 1):
            for c in (-1, 0, 1):
                for b in (-1, 0, 1):
                    i = 9 * a + 3 * b + c + 13
                    out[i] = turn(ref[i, rows(b), :], c - GROUP * a, 1)
        return out

    for y in (-2, 6):
        for ref, post_ref in ((low_ref, lpost_ref), (high_ref, hpost_ref)):
            rows = pl.ds(CELLS + y, CELLS)
            f = edge_stream(ref, lambda b: pl.ds(CELLS + y - b, CELLS))
            post = collide(f, ref[SOLID, rows, :] > 0.5, ref[JET, rows, :] > 0.5)
            for i in range(27):
                post_ref[i, rows, :] = post[i]

    def join(low, high):
        return jnp.where(lanes_of(low.shape[0]) % GROUP < 3, turn(high, -2, 1), low)

    f_low = edge_stream(lpost_ref, lambda b: pl.ds(CELLS - b, CELLS))
    flow_low = velocity(f_low, low_ref[SOLID, pl.ds(CELLS, CELLS), :])
    f_high = edge_stream(hpost_ref, lambda b: pl.ds(CELLS - b, CELLS))
    flow_high = velocity(f_high, high_ref[SOLID, pl.ds(CELLS, CELLS), :])
    joined = [join(low, high) for low, high in zip(f_low, f_high)]
    for x in range(CELLS):
        rows = pl.ds(x * CELLS, CELLS)
        shift = -(GROUP * (LAST - REACH - x) + 3)
        for i in range(27):
            done_ref[i, rows, :] = jnp.where(ends, turn(joined[i], shift, 1), adv_ref[i, rows, :])
    save = pltpu.make_async_copy(done_ref, adv_hbm, sem)
    save.start()
    joined = [join(low, high) for low, high in zip(flow_low, flow_high)]
    for plane in range(REACH - 1, REACH + CELLS + 1):
        rows = plane_rows(plane, 0)
        shift = -(GROUP * (LAST - plane) + 3)
        for c in range(3):
            rim_ref[c, rows, :] = jnp.where(ends, turn(joined[c], shift, 1), flow_ref[c, rows, :])
    beside = pl.ds(CELLS - 1, 2, stride=CELLS + 1)
    side_low = velocity(
        edge_stream(lpost_ref, lambda b: pl.ds(CELLS - 1 - b, 2, stride=CELLS + 1)), low_ref[SOLID, beside, :]
    )
    side_high = velocity(
        edge_stream(hpost_ref, lambda b: pl.ds(CELLS - 1 - b, 2, stride=CELLS + 1)), high_ref[SOLID, beside, :]
    )
    for c in range(3):
        joined = join(side_low[c], side_high[c])
        for k, y in enumerate((-1, CELLS)):
            rows = row_slice(REACH, y)
            spread = pltpu.roll(
                jnp.broadcast_to(joined[k : k + 1], (CELLS, LANES)),
                LANES - (GROUP * (LAST - REACH) + 3),
                1,
                stride=GROUP,
                stride_axis=0,
            )
            rim_ref[c, rows, :] = jnp.where(ends, spread, flow_ref[c, rows, :])

    own = range(REACH, REACH + CELLS)

    def here(c):
        return [rim_ref[c, plane_rows(plane, 0), :] for plane in own]

    def along_first(c):
        return [
            0.5 * (rim_ref[c, plane_rows(plane + 1, 0), :] - rim_ref[c, plane_rows(plane - 1, 0), :]) for plane in own
        ]

    def along_second(c):
        return [0.5 * (rim_ref[c, plane_rows(plane, 1), :] - rim_ref[c, plane_rows(plane, -1), :]) for plane in own]

    def along_third(c):
        low = [turn(value, 1, 1) for value in here(c)]
        high = [turn(value, -1, 1) for value in here(c)]
        out = []
        for k, plane in enumerate(own):
            base = GROUP * (LAST - plane)
            first = jnp.where(lane == 0, turn(flow_low[c], -2 - base, 1), low[k])
            second = jnp.where(lane == LANES - 1, turn(flow_high[c], -6 - base, 1), high[k])
            out.append(0.5 * (second - first))
        return out

    def minus(first, second):
        return [a - b for a, b in zip(first, second)]

    vort = (
        minus(along_second(2), along_third(1)),
        minus(along_third(0), along_first(2)),
        minus(along_first(1), along_second(0)),
    )
    s_two = jnp.concatenate([a * a + b * b + c * c for a, b, c in zip(*vort)], axis=0)
    flow_first = jnp.concatenate(here(0), axis=0)
    solid_on = p_ref[SOLID] > 0.5
    ratio = s_two / (s_two + shade_scale)
    alpha = jnp.where(solid_on, solid_alpha, alpha_top * (1.0 - jnp.exp(-s_two / shade_scale)))
    red = jnp.where(solid_on, 0.6, 0.3 + 1.5 * ratio)
    green = jnp.where(solid_on, 0.6, 1.2 - 0.9 * ratio)
    blue = jnp.where(solid_on, 0.6, 0.8 + 0.4 * jnp.tanh(20.0 * flow_first))
    logs = jnp.log1p(-alpha)
    running = logs
    wide = lanes_of(CELLS * CELLS)
    for step in (1, 2, 4, 8, 16, 32, 64):
        running = running + jnp.where(wide >= step, turn(running, step, 1), 0.0)
    weight = alpha * jnp.exp(running - logs)
    acc = jnp.zeros((CELLS, LANES), jnp.float32)
    for ch, value in enumerate((red * weight, green * weight, blue * weight, logs)):
        total = jnp.sum(value, axis=1, keepdims=True)
        for x in range(CELLS):
            acc = jnp.where(lane // UP == ch * CELLS + x, total[x * CELLS : (x + 1) * CELLS], acc)
    out_ref[...] = acc
    save.wait()


def last_kernel(slab_ref, rank_ref, out_ref):
    slabs = slab_ref[...]
    rank = rank_ref[...]
    channel = lanes_of(CELLS) // (CELLS * UP)
    logs = slabs
    for ch in range(3):
        logs = jnp.where(channel == ch, turn(slabs, (ch + 1) * CELLS * UP, 1), logs)
    front = jnp.zeros_like(slabs)
    for s in range(CELLS):
        front = front + jnp.where(rank[s : s + 1] < rank, logs[s : s + 1], 0.0)
    colour = jnp.sum(jnp.exp(front) * slabs, axis=0, keepdims=True)
    opacity = 1.0 - jnp.exp(jnp.sum(logs, axis=0, keepdims=True))
    row = jnp.where(channel[:1] == 3, opacity, colour)
    for ch in range(4):
        out_ref[ch] = jnp.broadcast_to(turn(row, -ch * CELLS * UP, 1)[:, : CELLS * UP], (UP, CELLS * UP))


def call(kernel, outs, scratch=(), first_out_hbm=False, in_hbm=False):
    shapes = tuple(jax.ShapeDtypeStruct(shape, jnp.float32) for shape in outs)
    extra = {}
    if in_hbm:
        extra["in_specs"] = [pl.BlockSpec(memory_space=pltpu.HBM)] * 3
    if first_out_hbm:
        spaces = [pltpu.HBM] + [pltpu.VMEM] * (len(outs) - 1)
        extra["out_specs"] = tuple(pl.BlockSpec(memory_space=space) for space in spaces)
    return pl.pallas_call(
        kernel,
        out_shape=shapes,
        scratch_shapes=scratch,
        compiler_params=pltpu.CompilerParams(vmem_limit_bytes=24 * 1024 * 1024),
        **extra,
    )


def both_ways(lo, hi, axis):
    count = lax.axis_size(axis)
    forward = [(i, (i + 1) % count) for i in range(count)]
    backward = [(target, source) for source, target in forward]
    return lax.ppermute(hi, axis, forward), lax.ppermute(lo, axis, backward)


def in_pairs(first, second, axis):
    count = lax.axis_size(axis)
    out = []
    for start, value in ((0, first), (1, second)):
        pairs = []
        for i in range(start, count + start, 2):
            left, right = i % count, (i + 1) % count
            pairs += [(left, right), (right, left)]
        out.append(lax.ppermute(value, axis, pairs))
    return out


def body(populations, solid_mask, jet_mask, visibility):
    cells = CELLS * CELLS
    f = populations.reshape(27, cells, LANES)
    solid = solid_mask.reshape(cells, LANES)
    jet = jet_mask.reshape(cells, LANES)
    f, solid, jet = [pltpu.with_memory_space_constraint(value, pltpu.HBM) for value in (f, solid, jet)]
    send_shape = (X_COUNT, CELLS, LANES)
    post, xa, xb, ya, yb = call(
        first_kernel,
        ((29, cells, LANES),) + (send_shape,) * 4,
        (
            pltpu.VMEM((27, cells, LANES), jnp.float32),
            pltpu.VMEM((cells, LANES), jnp.int32),
            pltpu.VMEM((cells, LANES), jnp.int32),
            pltpu.SemaphoreType.DMA((CELLS + 2,)),
        ),
        in_hbm=True,
    )(f, solid, jet)
    xa, xb = in_pairs(xa, xb, "gx")
    ya, yb = in_pairs(ya, yb, "gy")
    xa, xb, ya, yb = lax.optimization_barrier((xa, xb, ya, yb))
    corner_shape = (CORNER, LANES)
    lo, hi = call(second_kernel, (corner_shape, corner_shape))(ya, yb)
    clo, chi = both_ways(lo, hi, "gx")
    tile_shape = (29, CELLS, LANES)
    low, high = call(faces_kernel, (tile_shape, tile_shape))(post, xa, xb)
    half_shape = (HALF, 2 * CELLS, LANES)
    halo, low_halo, lo, hi = call(
        third_kernel, ((29, (SPAN + 1) * CELLS, LANES), tile_shape, half_shape, half_shape)
    )(ya, yb, clo, chi, low)
    zlo, zhi = both_ways(lo, hi, "gz")
    height = SPAN * ROWS + CELLS
    moved, flow, high_halo = call(
        steps_kernel,
        ((27, cells, LANES), (3, height, LANES), tile_shape),
        (pltpu.VMEM((29, height, LANES), jnp.float32), pltpu.VMEM((27, height, LANES), jnp.float32)),
    )(post, xa, xb, halo)
    edge = pltpu.VMEM((29, 3 * CELLS, LANES), jnp.float32)
    edge_post = pltpu.VMEM((27, 3 * CELLS, LANES), jnp.float32)
    advanced, slabs = call(
        render_kernel,
        ((27, cells, LANES), (CELLS, LANES)),
        (
            edge,
            edge,
            edge_post,
            edge_post,
            pltpu.VMEM((27, cells, LANES), jnp.float32),
            pltpu.VMEM((3, height, LANES), jnp.float32),
            pltpu.SemaphoreType.DMA,
        ),
        first_out_hbm=True,
    )(post, moved, flow, low, low_halo, high, high_halo, zlo, zhi)
    slabs = lax.all_to_all(slabs, "gz", 0, 0, tiled=True)
    rank = jnp.broadcast_to(visibility[:, None], (CELLS, LANES))
    (image,) = call(last_kernel, ((4, UP, CELLS * UP),))(slabs, rank)
    return advanced.reshape(27, CELLS, CELLS, LANES), jnp.swapaxes(image, 1, 2)


def solution(mesh):
    return jax.shard_map(
        body,
        mesh=mesh,
        in_specs=(P(None, "gx", "gy", "gz"), P("gx", "gy", "gz"), P("gx", "gy", "gz"), P()),
        out_specs=(P(None, "gx", "gy", "gz"), P(None, "gx", ("gy", "gz"))),
        check_vma=False,
    )
```

```python
import jax
import jax.numpy as jnp
import numpy as np
from jax import lax
from jax.experimental import pallas as pl
from jax.experimental.pallas import tpu as pltpu
from jax.sharding import PartitionSpec as P

UP = 4
CELLS = 8
LANES = 128
REACH = 3
SPAN = CELLS + 2 * REACH
LAST = SPAN - 1
ROWS = 16
HALF = 15
GROUP = 8

omega_rate = 1.25
jet_speed = 0.12
alpha_top = 0.03
solid_alpha = 0.15
shade_scale = 0.002

DIRS = [(a, b, c) for a in (-1, 0, 1) for b in (-1, 0, 1) for c in (-1, 0, 1)]
WEIGHTS = [(8.0 / 27.0, 2.0 / 27.0, 1.0 / 54.0, 1.0 / 216.0)[abs(a) + abs(b) + abs(c)] for a, b, c in DIRS]
SOLID, JET = 27, 28
MASKS = (SOLID, JET)


def axis_list(axis, inward):
    out = []
    for dist, allowed in ((1, (-1, 0, 1)), (2, (0, inward)), (3, (inward,))):
        out += [(i, dist) for i in range(27) if DIRS[i][axis] in allowed]
    out += [(m, dist) for m in MASKS for dist in (1, 2)]
    return out


def held(key, x):
    dist, inward = (-x, 1) if x < 0 else (x - CELLS + 1, -1)
    if dist <= 0:
        return True
    return (key, dist) in axis_list(0, inward)


def corner_list(inward):
    out = []
    for key, dist in axis_list(1, inward):
        first, second = (0, 0) if key in MASKS else DIRS[key][:2]
        for x in (-3, -2, -1, 8, 9, 10):
            far = -(x + first) if x < 0 else x + first - CELLS + 1
            if held(key, x) and not (far >= 2 and dist - inward * second >= 2):
                out.append((key, dist, x))
    return out


X_COUNT = len(axis_list(0, 1))
Y_OWN = len(axis_list(1, 1)) * CELLS
Y_CORNER = -(-len(corner_list(1)) // 8) * 8


def moments(f):
    third = None
    parts = []
    for a in range(3):
        row = []
        for b in range(3):
            lo, mid, hi = f[9 * a + 3 * b], f[9 * a + 3 * b + 1], f[9 * a + 3 * b + 2]
            row.append((lo + hi) + mid)
            diff = hi - lo
            third = diff if third is None else third + diff
        parts.append(row)
    sums = [(row[0] + row[2]) + row[1] for row in parts]
    second = (parts[0][2] - parts[0][0]) + (parts[1][2] - parts[1][0]) + (parts[2][2] - parts[2][0])
    return (sums[0] + sums[2]) + sums[1], sums[2] - sums[0], second, third


def collide(f, solid, jet):
    density, first, second, third = moments(f)
    scale = 1.0 / density
    ux = jnp.where(jet, jet_speed, first * scale)
    uy = jnp.where(jet, 0.0, second * scale)
    uz = jnp.where(jet, 0.0, third * scale)
    gain = jnp.where(jet, 1.0, omega_rate) * density
    keep = jnp.where(jet, 0.0, 1.0 - omega_rate)
    base = 1.0 - 1.5 * (ux * ux + uy * uy + uz * uz)
    strength = {w: gain * w for w in set(WEIGHTS)}
    post = [None] * 27
    comps = (ux, uy, uz)
    for i in range(14):
        w = strength[WEIGHTS[i]]
        if i == 13:
            post[i] = jnp.where(solid, f[i], w * base + keep * f[i])
            continue
        along = None
        for c, u in zip(DIRS[i], comps):
            if c == 0:
                continue
            if along is None:
                along = u if c > 0 else -u
            else:
                along = along + u if c > 0 else along - u
        even = w * (base + 4.5 * (along * along))
        odd = w * (3.0 * along)
        j = 26 - i
        post[i] = jnp.where(solid, f[j], (even + odd) + keep * f[i])
        post[j] = jnp.where(solid, f[i], (even - odd) + keep * f[j])
    return post


def lanes_of(rows):
    return lax.broadcasted_iota(jnp.int32, (rows, LANES), 1)


def turn(value, shift, axis):
    size = value.shape[axis]
    if isinstance(shift, int):
        shift = shift % size
        if shift == 0:
            return value
    return pltpu.roll(value, shift, axis)


def first_kernel(
    f_hbm, solid_hbm, jet_hbm, p_ref, lo_ref, hi_ref, ylo_ref, yhi_ref, f_ref, solid_ref, jet_ref, sems
):
    masks = [
        pltpu.make_async_copy(solid_hbm, solid_ref, sems.at[CELLS]),
        pltpu.make_async_copy(jet_hbm, jet_ref, sems.at[CELLS + 1]),
    ]
    copies = []
    for x in range(CELLS):
        rows = pl.ds(x * CELLS, CELLS)
        copies.append(pltpu.make_async_copy(f_hbm.at[:, rows, :], f_ref.at[:, rows, :], sems.at[x]))
    for copy in masks + copies:
        copy.start()
    for copy in masks:
        copy.wait()
    p_ref[SOLID] = solid_ref[...].astype(jnp.float32)
    p_ref[JET] = jet_ref[...].astype(jnp.float32)
    for x in range(CELLS):
        copies[x].wait()
        rows = pl.ds(x * CELLS, CELLS)
        f = [f_ref[i, rows, :] for i in range(27)]
        post = collide(f, solid_ref[rows, :] == 1, jet_ref[rows, :] == 1)
        for i in range(27):
            p_ref[i, rows, :] = post[i]
    for k, (key, dist) in enumerate(axis_list(0, -1)):
        lo_ref[k] = p_ref[key, pl.ds((dist - 1) * CELLS, CELLS), :]
    for k, (key, dist) in enumerate(axis_list(0, 1)):
        hi_ref[k] = p_ref[key, pl.ds((CELLS - dist) * CELLS, CELLS), :]
    for inward, out_ref in ((-1, ylo_ref), (1, yhi_ref)):
        for k, (key, dist) in enumerate(axis_list(1, inward)):
            row = dist - 1 if inward < 0 else CELLS - dist
            out_ref[pl.ds(k * CELLS, CELLS), :] = p_ref[key, pl.ds(row, CELLS, stride=CELLS), :]


LOW_AT = {entry: k for k, entry in enumerate(axis_list(0, 1))}
HIGH_AT = {entry: k for k, entry in enumerate(axis_list(0, -1))}


def plane_ref(key, x, p_ref, xlo_ref, xhi_ref):
    if x < 0:
        return xlo_ref.at[LOW_AT[(key, -x)]]
    if x >= CELLS:
        return xhi_ref.at[HIGH_AT[(key, x - CELLS + 1)]]
    return p_ref.at[key, pl.ds(x * CELLS, CELLS), :]


def second_kernel(xlo_ref, xhi_ref, lo_ref, hi_ref):
    for inward, out_ref in ((-1, lo_ref), (1, hi_ref)):
        for k, (key, dist, x) in enumerate(corner_list(inward)):
            row = dist - 1 if inward < 0 else CELLS - dist
            out_ref[pl.ds(k, 1), :] = plane_ref(key, x, None, xlo_ref, xhi_ref)[pl.ds(row, 1), :]


def pack(tiles):
    group = lanes_of(CELLS) // GROUP
    acc = [jnp.zeros((CELLS, LANES), jnp.float32)] * 29
    for place, shift, load in tiles:
        here = group == place % (LANES // GROUP)
        for key in range(29):
            value = load(key)
            if value is not None:
                acc[key] = jnp.where(here, turn(value, shift, 1), acc[key])
    return acc


def faces_kernel(p_ref, xlo_ref, xhi_ref, low_ref, high_ref):
    def load(key, plane):
        if held(key, plane - REACH):
            return plane_ref(key, plane - REACH, p_ref, xlo_ref, xhi_ref)[...]

    for out_ref, start in ((low_ref, 3), (high_ref, 5)):
        tiles = [
            (LAST - plane, GROUP * (LAST - plane) + start, lambda key, plane=plane: load(key, plane))
            for plane in range(SPAN)
        ]
        for key, value in enumerate(pack(tiles)):
            out_ref[key] = value


def pack_halo(h_ref, start):
    upper = lax.broadcasted_iota(jnp.int32, (CELLS, LANES), 0) < CELLS // 2
    tiles = [
        (
            LAST - tile,
            GROUP * (LAST - tile) + start,
            lambda key, tile=tile: h_ref[key, pl.ds(tile * CELLS, CELLS), :],
        )
        for tile in range(SPAN + 1)
    ]
    return [jnp.where(upper, turn(value, GROUP, 1), value) for value in pack(tiles)]


def third_kernel(ylo_ref, yhi_ref, clo_ref, chi_ref, main_ref, h_ref, z_ref, lo_ref, hi_ref):
    for inward, in_ref, corner_ref in ((1, ylo_ref, clo_ref), (-1, yhi_ref, chi_ref)):
        for k, (key, dist) in enumerate(axis_list(1, inward)):
            start = CELLS * REACH + CELLS - dist if inward > 0 else CELLS * (REACH + 1) + dist - 1
            h_ref[key, pl.ds(start, CELLS, stride=CELLS), :] = in_ref[pl.ds(k * CELLS, CELLS), :]
        for k, (key, dist, x) in enumerate(corner_list(inward)):
            plane = x + REACH
            row = CELLS * plane + CELLS - dist if inward > 0 else CELLS * (plane + 1) + dist - 1
            h_ref[key, pl.ds(row, 1), :] = corner_ref[pl.ds(k, 1), :]
    halo = pack_halo(h_ref, 3)
    early = lanes_of(CELLS) % GROUP < REACH
    for key in range(29):
        z_ref[key] = halo[key]
    for part, values in enumerate(([main_ref[key] for key in range(29)], halo)):
        rows = pl.ds(part * CELLS, CELLS)
        for out_ref, shift in ((lo_ref, -REACH), (hi_ref, REACH)):
            for k in range(HALF):
                value = values[k]
                if k + HALF < 29:
                    other = turn(values[k + HALF], shift, 1)
                    value = jnp.where(early, other, value) if shift < 0 else jnp.where(early, value, other)
                out_ref[k, rows, :] = value


def plane_rows(plane, y):
    return pl.ds(plane * ROWS + CELLS + y, CELLS)


def row_slice(plane, y):
    return pl.ds(plane * ROWS + CELLS + y, CELLS, stride=ROWS)


def velocity(f, solid):
    density, first, second, third = moments(f)
    scale = (1.0 - solid) / density
    return first * scale, second * scale, third * scale


def steps_kernel(p_ref, xlo_ref, xhi_ref, h_ref, adv_ref, flow_ref, high_ref, e_ref, g_ref):
    for plane in range(SPAN):
        for key in range(29):
            if held(key, plane - REACH):
                e_ref[key, plane_rows(plane, 0), :] = plane_ref(key, plane - REACH, p_ref, xlo_ref, xhi_ref)[...]
    for tile in range(SPAN + 1):
        for key in range(29):
            e_ref[key, pl.ds(tile * ROWS, CELLS), :] = h_ref[key, pl.ds(tile * CELLS, CELLS), :]

    def stream(ref, rows):
        out = [None] * 27
        for move in (-1, 1, 0):
            for i, (a, b, c) in enumerate(DIRS):
                if c == move:
                    out[i] = turn(ref[i, rows(a, b), :], c, 1)
        return out

    def plane_stream(ref, plane, y):
        return stream(ref, lambda a, b: plane_rows(plane - a, y - b))

    def row_stream(ref, y):
        return stream(ref, lambda a, b: row_slice(REACH - a, y - b))

    def settle(rows, f):
        post = collide(f, e_ref[SOLID, rows, :] > 0.5, e_ref[JET, rows, :] > 0.5)
        for i in range(27):
            g_ref[i, rows, :] = post[i]

    def step_one(plane, y):
        settle(plane_rows(plane, y), plane_stream(e_ref, plane, y))

    def step_one_own(k, carry):
        step_one(REACH + 2 * k, 0)
        step_one(REACH + 2 * k + 1, 0)
        return carry

    def step_one_halo(k, carry):
        plane = k + 1 + CELLS * (k // 2)
        step_one(plane, -2)
        step_one(plane, 6)
        return carry

    lax.fori_loop(0, CELLS // 2, step_one_own, 0)
    lax.fori_loop(0, 4, step_one_halo, 0)
    for y in (-2, -1, CELLS, CELLS + 1):
        settle(row_slice(REACH, y), row_stream(e_ref, y))

    def store_flow(rows, f):
        for c, value in enumerate(velocity(f, e_ref[SOLID, rows, :])):
            flow_ref[c, rows, :] = value

    def step_two(plane):
        f = plane_stream(g_ref, plane, 0)
        rows = pl.ds(pl.multiple_of((plane - REACH) * CELLS, CELLS), CELLS)
        for i in range(27):
            adv_ref[i, rows, :] = f[i]
        store_flow(plane_rows(plane, 0), f)

    def step_two_own(k, carry):
        step_two(REACH + 2 * k)
        step_two(REACH + 2 * k + 1)
        return carry

    lax.fori_loop(0, CELLS // 2, step_two_own, 0)
    for plane in (REACH - 1, REACH + CELLS):
        store_flow(plane_rows(plane, 0), plane_stream(g_ref, plane, 0))
    for y in (-1, CELLS):
        store_flow(row_slice(REACH, y), row_stream(g_ref, y))
    for key, value in enumerate(pack_halo(h_ref, 5)):
        high_ref[key] = value


def render_kernel(
    p_ref, adv_ref, flow_ref, lmain_ref, lhalo_ref, hmain_ref, hhalo_ref, zlo_ref, zhi_ref,
    adv_hbm, out_ref, low_ref, high_ref, lpost_ref, hpost_ref, done_ref, rim_ref, sem,
):
    lane = lanes_of(CELLS)
    slot = lane % GROUP
    ends = (lane < 2) | (lane >= LANES - 2)

    for part in range(2):
        rows = pl.ds(part * CELLS, CELLS)
        own_low, own_high = (lmain_ref, hmain_ref) if part == 0 else (lhalo_ref, hhalo_ref)
        low = [zlo_ref[key, rows, :] for key in range(HALF)]
        low += [turn(zlo_ref[key, rows, :], -REACH, 1) for key in range(29 - HALF)]
        high = [turn(zhi_ref[key, rows, :], 2, 1) for key in range(HALF)]
        high += [turn(zhi_ref[key, rows, :], REACH + 2, 1) for key in range(29 - HALF)]
        for key in range(29):
            first = jnp.where(slot < 3, low[key], own_low[key])
            second = jnp.where(slot >= 5, high[key], own_high[key])
            for start in (CELLS,) if part == 0 else (0, 2 * CELLS):
                low_ref[key, pl.ds(start, CELLS), :] = first
                high_ref[key, pl.ds(start, CELLS), :] = second

    def edge_stream(ref, rows):
        out = [None] * 27
        for a in (-1, 0, 1):
            for c in (-1, 0, 1):
                for b in (-1, 0, 1):
                    i = 9 * a + 3 * b + c + 13
                    out[i] = turn(ref[i, rows(b), :], c - GROUP * a, 1)
        return out

    for y in (-2, 6):
        for ref, post_ref in ((low_ref, lpost_ref), (high_ref, hpost_ref)):
            rows = pl.ds(CELLS + y, CELLS)
            f = edge_stream(ref, lambda b: pl.ds(CELLS + y - b, CELLS))
            post = collide(f, ref[SOLID, rows, :] > 0.5, ref[JET, rows, :] > 0.5)
            for i in range(27):
                post_ref[i, rows, :] = post[i]

    def join(low, high):
        return jnp.where(lanes_of(low.shape[0]) % GROUP < 3, turn(high, -2, 1), low)

    f_low = edge_stream(lpost_ref, lambda b: pl.ds(CELLS - b, CELLS))
    flow_low = velocity(f_low, low_ref[SOLID, pl.ds(CELLS, CELLS), :])
    f_high = edge_stream(hpost_ref, lambda b: pl.ds(CELLS - b, CELLS))
    flow_high = velocity(f_high, high_ref[SOLID, pl.ds(CELLS, CELLS), :])
    joined = [join(low, high) for low, high in zip(f_low, f_high)]
    for x in range(CELLS):
        rows = pl.ds(x * CELLS, CELLS)
        shift = -(GROUP * (LAST - REACH - x) + 3)
        for i in range(27):
            done_ref[i, rows, :] = jnp.where(ends, turn(joined[i], shift, 1), adv_ref[i, rows, :])
    save = pltpu.make_async_copy(done_ref, adv_hbm, sem)
    save.start()
    joined = [join(low, high) for low, high in zip(flow_low, flow_high)]
    for plane in range(REACH - 1, REACH + CELLS + 1):
        rows = plane_rows(plane, 0)
        shift = -(GROUP * (LAST - plane) + 3)
        for c in range(3):
            rim_ref[c, rows, :] = jnp.where(ends, turn(joined[c], shift, 1), flow_ref[c, rows, :])
    beside = pl.ds(CELLS - 1, 2, stride=CELLS + 1)
    side_low = velocity(
        edge_stream(lpost_ref, lambda b: pl.ds(CELLS - 1 - b, 2, stride=CELLS + 1)), low_ref[SOLID, beside, :]
    )
    side_high = velocity(
        edge_stream(hpost_ref, lambda b: pl.ds(CELLS - 1 - b, 2, stride=CELLS + 1)), high_ref[SOLID, beside, :]
    )
    for c in range(3):
        joined = join(side_low[c], side_high[c])
        for k, y in enumerate((-1, CELLS)):
            rows = row_slice(REACH, y)
            spread = pltpu.roll(
                jnp.broadcast_to(joined[k : k + 1], (CELLS, LANES)),
                LANES - (GROUP * (LAST - REACH) + 3),
                1,
                stride=GROUP,
                stride_axis=0,
            )
            rim_ref[c, rows, :] = jnp.where(ends, spread, flow_ref[c, rows, :])

    own = range(REACH, REACH + CELLS)

    def here(c):
        return [rim_ref[c, plane_rows(plane, 0), :] for plane in own]

    def along_first(c):
        return [
            0.5 * (rim_ref[c, plane_rows(plane + 1, 0), :] - rim_ref[c, plane_rows(plane - 1, 0), :]) for plane in own
        ]

    def along_second(c):
        return [0.5 * (rim_ref[c, plane_rows(plane, 1), :] - rim_ref[c, plane_rows(plane, -1), :]) for plane in own]

    def along_third(c):
        low = [turn(value, 1, 1) for value in here(c)]
        high = [turn(value, -1, 1) for value in here(c)]
        out = []
        for k, plane in enumerate(own):
            base = GROUP * (LAST - plane)
            first = jnp.where(lane == 0, turn(flow_low[c], -2 - base, 1), low[k])
            second = jnp.where(lane == LANES - 1, turn(flow_high[c], -6 - base, 1), high[k])
            out.append(0.5 * (second - first))
        return out

    def minus(first, second):
        return [a - b for a, b in zip(first, second)]

    vort = (
        minus(along_second(2), along_third(1)),
        minus(along_third(0), along_first(2)),
        minus(along_first(1), along_second(0)),
    )
    s_two = jnp.concatenate([a * a + b * b + c * c for a, b, c in zip(*vort)], axis=0)
    flow_first = jnp.concatenate(here(0), axis=0)
    solid_on = p_ref[SOLID] > 0.5
    ratio = s_two / (s_two + shade_scale)
    alpha = jnp.where(solid_on, solid_alpha, alpha_top * (1.0 - jnp.exp(-s_two / shade_scale)))
    red = jnp.where(solid_on, 0.6, 0.3 + 1.5 * ratio)
    green = jnp.where(solid_on, 0.6, 1.2 - 0.9 * ratio)
    blue = jnp.where(solid_on, 0.6, 0.8 + 0.4 * jnp.tanh(20.0 * flow_first))
    logs = jnp.log1p(-alpha)
    running = logs
    wide = lanes_of(CELLS * CELLS)
    for step in (1, 2, 4, 8, 16, 32, 64):
        running = running + jnp.where(wide >= step, turn(running, step, 1), 0.0)
    weight = alpha * jnp.exp(running - logs)
    acc = jnp.zeros((CELLS, LANES), jnp.float32)
    for ch, value in enumerate((red * weight, green * weight, blue * weight, logs)):
        total = jnp.sum(value, axis=1, keepdims=True)
        for x in range(CELLS):
            acc = jnp.where(lane // UP == ch * CELLS + x, total[x * CELLS : (x + 1) * CELLS], acc)
    out_ref[...] = acc
    save.wait()


def last_kernel(slab_ref, rank_ref, out_ref):
    slabs = slab_ref[...]
    rank = rank_ref[...]
    channel = lanes_of(CELLS) // (CELLS * UP)
    logs = slabs
    for ch in range(3):
        logs = jnp.where(channel == ch, turn(slabs, (ch + 1) * CELLS * UP, 1), logs)
    front = jnp.zeros_like(slabs)
    for s in range(CELLS):
        front = front + jnp.where(rank[s : s + 1] < rank, logs[s : s + 1], 0.0)
    colour = jnp.sum(jnp.exp(front) * slabs, axis=0, keepdims=True)
    opacity = 1.0 - jnp.exp(jnp.sum(logs, axis=0, keepdims=True))
    row = jnp.where(channel[:1] == 3, opacity, colour)
    for ch in range(4):
        out_ref[ch] = jnp.broadcast_to(turn(row, -ch * CELLS * UP, 1)[:, : CELLS * UP], (UP, CELLS * UP))


def call(kernel, outs, scratch=(), first_out_hbm=False, in_hbm=False):
    shapes = tuple(jax.ShapeDtypeStruct(shape, jnp.float32) for shape in outs)
    extra = {}
    if in_hbm:
        extra["in_specs"] = [pl.BlockSpec(memory_space=pltpu.HBM)] * 3
    if first_out_hbm:
        spaces = [pltpu.HBM] + [pltpu.VMEM] * (len(outs) - 1)
        extra["out_specs"] = tuple(pl.BlockSpec(memory_space=space) for space in spaces)
    return pl.pallas_call(
        kernel,
        out_shape=shapes,
        scratch_shapes=scratch,
        compiler_params=pltpu.CompilerParams(vmem_limit_bytes=24 * 1024 * 1024),
        **extra,
    )


def both_ways(lo, hi, axis):
    count = lax.axis_size(axis)
    forward = [(i, (i + 1) % count) for i in range(count)]
    backward = [(target, source) for source, target in forward]
    return lax.ppermute(hi, axis, forward), lax.ppermute(lo, axis, backward)


def body(populations, solid_mask, jet_mask, visibility):
    cells = CELLS * CELLS
    f = populations.reshape(27, cells, LANES)
    solid = solid_mask.reshape(cells, LANES)
    jet = jet_mask.reshape(cells, LANES)
    f, solid, jet = [pltpu.with_memory_space_constraint(value, pltpu.HBM) for value in (f, solid, jet)]
    x_shape = (X_COUNT, CELLS, LANES)
    y_shape = (Y_OWN, LANES)
    post, lo, hi, down, up = call(
        first_kernel,
        ((29, cells, LANES), x_shape, x_shape, y_shape, y_shape),
        (
            pltpu.VMEM((27, cells, LANES), jnp.float32),
            pltpu.VMEM((cells, LANES), jnp.int32),
            pltpu.VMEM((cells, LANES), jnp.int32),
            pltpu.SemaphoreType.DMA((CELLS + 2,)),
        ),
        in_hbm=True,
    )(f, solid, jet)
    xlo, xhi = both_ways(lo, hi, "gx")
    ylo, yhi = both_ways(down, up, "gy")
    corner_shape = (Y_CORNER, LANES)
    lo, hi = call(second_kernel, (corner_shape, corner_shape))(xlo, xhi)
    clo, chi = both_ways(lo, hi, "gy")
    tile_shape = (29, CELLS, LANES)
    low, high = call(faces_kernel, (tile_shape, tile_shape))(post, xlo, xhi)
    half_shape = (HALF, 2 * CELLS, LANES)
    halo, low_halo, lo, hi = call(
        third_kernel, ((29, (SPAN + 1) * CELLS, LANES), tile_shape, half_shape, half_shape)
    )(ylo, yhi, clo, chi, low)
    zlo, zhi = both_ways(lo, hi, "gz")
    height = SPAN * ROWS + CELLS
    moved, flow, high_halo = call(
        steps_kernel,
        ((27, cells, LANES), (3, height, LANES), tile_shape),
        (pltpu.VMEM((29, height, LANES), jnp.float32), pltpu.VMEM((27, height, LANES), jnp.float32)),
    )(post, xlo, xhi, halo)
    edge = pltpu.VMEM((29, 3 * CELLS, LANES), jnp.float32)
    edge_post = pltpu.VMEM((27, 3 * CELLS, LANES), jnp.float32)
    advanced, slabs = call(
        render_kernel,
        ((27, cells, LANES), (CELLS, LANES)),
        (
            edge,
            edge,
            edge_post,
            edge_post,
            pltpu.VMEM((27, cells, LANES), jnp.float32),
            pltpu.VMEM((3, height, LANES), jnp.float32),
            pltpu.SemaphoreType.DMA,
        ),
        first_out_hbm=True,
    )(post, moved, flow, low, low_halo, high, high_halo, zlo, zhi)
    slabs = lax.all_to_all(slabs, "gz", 0, 0, tiled=True)
    rank = jnp.broadcast_to(visibility[:, None], (CELLS, LANES))
    (image,) = call(last_kernel, ((4, UP, CELLS * UP),))(slabs, rank)
    return advanced.reshape(27, CELLS, CELLS, LANES), jnp.swapaxes(image, 1, 2)


def solution(mesh):
    return jax.shard_map(
        body,
        mesh=mesh,
        in_specs=(P(None, "gx", "gy", "gz"), P("gx", "gy", "gz"), P("gx", "gy", "gz"), P()),
        out_specs=(P(None, "gx", "gy", "gz"), P(None, "gx", ("gy", "gz"))),
        check_vma=False,
    )
```

```python
import jax
import jax.numpy as jnp
import numpy as np
from jax import lax
from jax.experimental import pallas as pl
from jax.experimental.pallas import tpu as pltpu
from jax.sharding import PartitionSpec as P

UP = 4
CELLS = 8
LANES = 128
REACH = 3
SPAN = CELLS + 2 * REACH
LAST = SPAN - 1
ROWS = 16
HALF = 15
GROUP = 8

omega_rate = 1.25
jet_speed = 0.12
alpha_top = 0.03
solid_alpha = 0.15
shade_scale = 0.002

DIRS = [(a, b, c) for a in (-1, 0, 1) for b in (-1, 0, 1) for c in (-1, 0, 1)]
WEIGHTS = [(8.0 / 27.0, 2.0 / 27.0, 1.0 / 54.0, 1.0 / 216.0)[abs(a) + abs(b) + abs(c)] for a, b, c in DIRS]
SOLID, JET = 27, 28
MASKS = (SOLID, JET)


def axis_list(axis, inward):
    out = []
    for dist, allowed in ((1, (-1, 0, 1)), (2, (0, inward)), (3, (inward,))):
        out += [(i, dist) for i in range(27) if DIRS[i][axis] in allowed]
    out += [(m, dist) for m in MASKS for dist in (1, 2)]
    return out


def held(key, x):
    dist, inward = (-x, 1) if x < 0 else (x - CELLS + 1, -1)
    if dist <= 0:
        return True
    return (key, dist) in axis_list(0, inward)


def corner_list(inward):
    out = []
    for key, dist in axis_list(1, inward):
        first, second = (0, 0) if key in MASKS else DIRS[key][:2]
        for x in (-3, -2, -1, 8, 9, 10):
            far = -(x + first) if x < 0 else x + first - CELLS + 1
            if held(key, x) and not (far >= 2 and dist - inward * second >= 2):
                out.append((key, dist, x))
    return out


X_COUNT = len(axis_list(0, 1))
Y_OWN = len(axis_list(1, 1)) * CELLS
Y_CORNER = -(-len(corner_list(1)) // 8) * 8


def moments(f):
    third = None
    parts = []
    for a in range(3):
        row = []
        for b in range(3):
            lo, mid, hi = f[9 * a + 3 * b], f[9 * a + 3 * b + 1], f[9 * a + 3 * b + 2]
            row.append((lo + hi) + mid)
            diff = hi - lo
            third = diff if third is None else third + diff
        parts.append(row)
    sums = [(row[0] + row[2]) + row[1] for row in parts]
    second = (parts[0][2] - parts[0][0]) + (parts[1][2] - parts[1][0]) + (parts[2][2] - parts[2][0])
    return (sums[0] + sums[2]) + sums[1], sums[2] - sums[0], second, third


def collide(f, solid, jet):
    density, first, second, third = moments(f)
    scale = 1.0 / density
    ux = jnp.where(jet, jet_speed, first * scale)
    uy = jnp.where(jet, 0.0, second * scale)
    uz = jnp.where(jet, 0.0, third * scale)
    gain = jnp.where(jet, 1.0, omega_rate) * density
    keep = jnp.where(jet, 0.0, 1.0 - omega_rate)
    base = 1.0 - 1.5 * (ux * ux + uy * uy + uz * uz)
    strength = {w: gain * w for w in set(WEIGHTS)}
    post = [None] * 27
    comps = (ux, uy, uz)
    for i in range(14):
        w = strength[WEIGHTS[i]]
        if i == 13:
            post[i] = jnp.where(solid, f[i], w * base + keep * f[i])
            continue
        along = None
        for c, u in zip(DIRS[i], comps):
            if c == 0:
                continue
            if along is None:
                along = u if c > 0 else -u
            else:
                along = along + u if c > 0 else along - u
        even = w * (base + 4.5 * (along * along))
        odd = w * (3.0 * along)
        j = 26 - i
        post[i] = jnp.where(solid, f[j], (even + odd) + keep * f[i])
        post[j] = jnp.where(solid, f[i], (even - odd) + keep * f[j])
    return post


def lanes_of(rows):
    return lax.broadcasted_iota(jnp.int32, (rows, LANES), 1)


def turn(value, shift, axis):
    size = value.shape[axis]
    if isinstance(shift, int):
        shift = shift % size
        if shift == 0:
            return value
    return pltpu.roll(value, shift, axis)


def first_kernel(
    f_hbm, solid_hbm, jet_hbm, p_ref, lo_ref, hi_ref, ylo_ref, yhi_ref, f_ref, solid_ref, jet_ref, sems
):
    masks = [
        pltpu.make_async_copy(solid_hbm, solid_ref, sems.at[CELLS]),
        pltpu.make_async_copy(jet_hbm, jet_ref, sems.at[CELLS + 1]),
    ]
    copies = []
    for x in range(CELLS):
        rows = pl.ds(x * CELLS, CELLS)
        copies.append(pltpu.make_async_copy(f_hbm.at[:, rows, :], f_ref.at[:, rows, :], sems.at[x]))
    for copy in masks + copies:
        copy.start()
    for copy in masks:
        copy.wait()
    p_ref[SOLID] = solid_ref[...].astype(jnp.float32)
    p_ref[JET] = jet_ref[...].astype(jnp.float32)
    for x in range(CELLS):
        copies[x].wait()
        rows = pl.ds(x * CELLS, CELLS)
        f = [f_ref[i, rows, :] for i in range(27)]
        post = collide(f, solid_ref[rows, :] == 1, jet_ref[rows, :] == 1)
        for i in range(27):
            p_ref[i, rows, :] = post[i]
    for k, (key, dist) in enumerate(axis_list(0, -1)):
        lo_ref[k] = p_ref[key, pl.ds((dist - 1) * CELLS, CELLS), :]
    for k, (key, dist) in enumerate(axis_list(0, 1)):
        hi_ref[k] = p_ref[key, pl.ds((CELLS - dist) * CELLS, CELLS), :]
    for inward, out_ref in ((-1, ylo_ref), (1, yhi_ref)):
        for k, (key, dist) in enumerate(axis_list(1, inward)):
            row = dist - 1 if inward < 0 else CELLS - dist
            out_ref[pl.ds(k * CELLS, CELLS), :] = p_ref[key, pl.ds(row, CELLS, stride=CELLS), :]


LOW_AT = {entry: k for k, entry in enumerate(axis_list(0, 1))}
HIGH_AT = {entry: k for k, entry in enumerate(axis_list(0, -1))}


def plane_ref(key, x, p_ref, xlo_ref, xhi_ref):
    if x < 0:
        return xlo_ref.at[LOW_AT[(key, -x)]]
    if x >= CELLS:
        return xhi_ref.at[HIGH_AT[(key, x - CELLS + 1)]]
    return p_ref.at[key, pl.ds(x * CELLS, CELLS), :]


def is_even(axis):
    return lax.axis_index(axis) % 2 == 0


def second_kernel(xlo_ref, xhi_ref, a_ref, b_ref):
    even = is_even("gy")
    rows = []
    for inward in (-1, 1):
        out = []
        for key, dist, x in corner_list(inward):
            row = dist - 1 if inward < 0 else CELLS - dist
            out.append(plane_ref(key, x, None, xlo_ref, xhi_ref)[pl.ds(row, 1), :])
        rows.append(out)
    for k, (lo, hi) in enumerate(zip(*rows)):
        a_ref[pl.ds(k, 1), :] = jnp.where(even, hi, lo)
        b_ref[pl.ds(k, 1), :] = jnp.where(even, lo, hi)


def pack(tiles):
    group = lanes_of(CELLS) // GROUP
    acc = [jnp.zeros((CELLS, LANES), jnp.float32)] * 29
    for place, shift, load in tiles:
        here = group == place % (LANES // GROUP)
        for key in range(29):
            value = load(key)
            if value is not None:
                acc[key] = jnp.where(here, turn(value, shift, 1), acc[key])
    return acc


def faces_kernel(p_ref, xlo_ref, xhi_ref, low_ref, high_ref):
    def load(key, plane):
        if held(key, plane - REACH):
            return plane_ref(key, plane - REACH, p_ref, xlo_ref, xhi_ref)[...]

    for out_ref, start in ((low_ref, 3), (high_ref, 5)):
        tiles = [
            (LAST - plane, GROUP * (LAST - plane) + start, lambda key, plane=plane: load(key, plane))
            for plane in range(SPAN)
        ]
        for key, value in enumerate(pack(tiles)):
            out_ref[key] = value


def pack_halo(h_ref, start):
    upper = lax.broadcasted_iota(jnp.int32, (CELLS, LANES), 0) < CELLS // 2
    tiles = [
        (
            LAST - tile,
            GROUP * (LAST - tile) + start,
            lambda key, tile=tile: h_ref[key, pl.ds(tile * CELLS, CELLS), :],
        )
        for tile in range(SPAN + 1)
    ]
    return [jnp.where(upper, turn(value, GROUP, 1), value) for value in pack(tiles)]


def third_kernel(ylo_ref, yhi_ref, ca_ref, cb_ref, main_ref, h_ref, z_ref, lo_ref, hi_ref):
    even = is_even("gy")
    for inward, in_ref in ((1, ylo_ref), (-1, yhi_ref)):
        for k, (key, dist) in enumerate(axis_list(1, inward)):
            start = CELLS * REACH + CELLS - dist if inward > 0 else CELLS * (REACH + 1) + dist - 1
            h_ref[key, pl.ds(start, CELLS, stride=CELLS), :] = in_ref[pl.ds(k * CELLS, CELLS), :]
        for k, (key, dist, x) in enumerate(corner_list(inward)):
            plane = x + REACH
            row = CELLS * plane + CELLS - dist if inward > 0 else CELLS * (plane + 1) + dist - 1
            one, two = (cb_ref, ca_ref) if inward > 0 else (ca_ref, cb_ref)
            h_ref[key, pl.ds(row, 1), :] = jnp.where(even, one[pl.ds(k, 1), :], two[pl.ds(k, 1), :])
    halo = pack_halo(h_ref, 3)
    early = lanes_of(CELLS) % GROUP < REACH
    for key in range(29):
        z_ref[key] = halo[key]
    for part, values in enumerate(([main_ref[key] for key in range(29)], halo)):
        rows = pl.ds(part * CELLS, CELLS)
        for out_ref, shift in ((lo_ref, -REACH), (hi_ref, REACH)):
            for k in range(HALF):
                value = values[k]
                if k + HALF < 29:
                    other = turn(values[k + HALF], shift, 1)
                    value = jnp.where(early, other, value) if shift < 0 else jnp.where(early, value, other)
                out_ref[k, rows, :] = value


def plane_rows(plane, y):
    return pl.ds(plane * ROWS + CELLS + y, CELLS)


def row_slice(plane, y):
    return pl.ds(plane * ROWS + CELLS + y, CELLS, stride=ROWS)


def velocity(f, solid):
    density, first, second, third = moments(f)
    scale = (1.0 - solid) / density
    return first * scale, second * scale, third * scale


def steps_kernel(p_ref, xlo_ref, xhi_ref, h_ref, adv_ref, flow_ref, high_ref, e_ref, g_ref):
    for plane in range(SPAN):
        for key in range(29):
            if held(key, plane - REACH):
                e_ref[key, plane_rows(plane, 0), :] = plane_ref(key, plane - REACH, p_ref, xlo_ref, xhi_ref)[...]
    for tile in range(SPAN + 1):
        for key in range(29):
            e_ref[key, pl.ds(tile * ROWS, CELLS), :] = h_ref[key, pl.ds(tile * CELLS, CELLS), :]

    def stream(ref, rows):
        out = [None] * 27
        for move in (-1, 1, 0):
            for i, (a, b, c) in enumerate(DIRS):
                if c == move:
                    out[i] = turn(ref[i, rows(a, b), :], c, 1)
        return out

    def plane_stream(ref, plane, y):
        return stream(ref, lambda a, b: plane_rows(plane - a, y - b))

    def row_stream(ref, y):
        return stream(ref, lambda a, b: row_slice(REACH - a, y - b))

    def settle(rows, f):
        post = collide(f, e_ref[SOLID, rows, :] > 0.5, e_ref[JET, rows, :] > 0.5)
        for i in range(27):
            g_ref[i, rows, :] = post[i]

    def step_one(plane, y):
        settle(plane_rows(plane, y), plane_stream(e_ref, plane, y))

    def step_one_own(k, carry):
        step_one(REACH + 2 * k, 0)
        step_one(REACH + 2 * k + 1, 0)
        return carry

    def step_one_halo(k, carry):
        plane = k + 1 + CELLS * (k // 2)
        step_one(plane, -2)
        step_one(plane, 6)
        return carry

    lax.fori_loop(0, CELLS // 2, step_one_own, 0)
    lax.fori_loop(0, 4, step_one_halo, 0)
    for y in (-2, -1, CELLS, CELLS + 1):
        settle(row_slice(REACH, y), row_stream(e_ref, y))

    def store_flow(rows, f):
        for c, value in enumerate(velocity(f, e_ref[SOLID, rows, :])):
            flow_ref[c, rows, :] = value

    def step_two(plane):
        f = plane_stream(g_ref, plane, 0)
        rows = pl.ds(pl.multiple_of((plane - REACH) * CELLS, CELLS), CELLS)
        for i in range(27):
            adv_ref[i, rows, :] = f[i]
        store_flow(plane_rows(plane, 0), f)

    def step_two_own(k, carry):
        step_two(REACH + 2 * k)
        step_two(REACH + 2 * k + 1)
        return carry

    lax.fori_loop(0, CELLS // 2, step_two_own, 0)
    for plane in (REACH - 1, REACH + CELLS):
        store_flow(plane_rows(plane, 0), plane_stream(g_ref, plane, 0))
    for y in (-1, CELLS):
        store_flow(row_slice(REACH, y), row_stream(g_ref, y))
    for key, value in enumerate(pack_halo(h_ref, 5)):
        high_ref[key] = value


def render_kernel(
    p_ref, adv_ref, flow_ref, lmain_ref, lhalo_ref, hmain_ref, hhalo_ref, zlo_ref, zhi_ref,
    adv_hbm, out_ref, low_ref, high_ref, lpost_ref, hpost_ref, done_ref, rim_ref, sem,
):
    lane = lanes_of(CELLS)
    slot = lane % GROUP
    ends = (lane < 2) | (lane >= LANES - 2)

    for part in range(2):
        rows = pl.ds(part * CELLS, CELLS)
        own_low, own_high = (lmain_ref, hmain_ref) if part == 0 else (lhalo_ref, hhalo_ref)
        low = [zlo_ref[key, rows, :] for key in range(HALF)]
        low += [turn(zlo_ref[key, rows, :], -REACH, 1) for key in range(29 - HALF)]
        high = [turn(zhi_ref[key, rows, :], 2, 1) for key in range(HALF)]
        high += [turn(zhi_ref[key, rows, :], REACH + 2, 1) for key in range(29 - HALF)]
        for key in range(29):
            first = jnp.where(slot < 3, low[key], own_low[key])
            second = jnp.where(slot >= 5, high[key], own_high[key])
            for start in (CELLS,) if part == 0 else (0, 2 * CELLS):
                low_ref[key, pl.ds(start, CELLS), :] = first
                high_ref[key, pl.ds(start, CELLS), :] = second

    def edge_stream(ref, rows):
        out = [None] * 27
        for a in (-1, 0, 1):
            for c in (-1, 0, 1):
                for b in (-1, 0, 1):
                    i = 9 * a + 3 * b + c + 13
                    out[i] = turn(ref[i, rows(b), :], c - GROUP * a, 1)
        return out

    for y in (-2, 6):
        for ref, post_ref in ((low_ref, lpost_ref), (high_ref, hpost_ref)):
            rows = pl.ds(CELLS + y, CELLS)
            f = edge_stream(ref, lambda b: pl.ds(CELLS + y - b, CELLS))
            post = collide(f, ref[SOLID, rows, :] > 0.5, ref[JET, rows, :] > 0.5)
            for i in range(27):
                post_ref[i, rows, :] = post[i]

    def join(low, high):
        return jnp.where(lanes_of(low.shape[0]) % GROUP < 3, turn(high, -2, 1), low)

    f_low = edge_stream(lpost_ref, lambda b: pl.ds(CELLS - b, CELLS))
    flow_low = velocity(f_low, low_ref[SOLID, pl.ds(CELLS, CELLS), :])
    f_high = edge_stream(hpost_ref, lambda b: pl.ds(CELLS - b, CELLS))
    flow_high = velocity(f_high, high_ref[SOLID, pl.ds(CELLS, CELLS), :])
    joined = [join(low, high) for low, high in zip(f_low, f_high)]
    for x in range(CELLS):
        rows = pl.ds(x * CELLS, CELLS)
        shift = -(GROUP * (LAST - REACH - x) + 3)
        for i in range(27):
            done_ref[i, rows, :] = jnp.where(ends, turn(joined[i], shift, 1), adv_ref[i, rows, :])
    save = pltpu.make_async_copy(done_ref, adv_hbm, sem)
    save.start()
    joined = [join(low, high) for low, high in zip(flow_low, flow_high)]
    for plane in range(REACH - 1, REACH + CELLS + 1):
        rows = plane_rows(plane, 0)
        shift = -(GROUP * (LAST - plane) + 3)
        for c in range(3):
            rim_ref[c, rows, :] = jnp.where(ends, turn(joined[c], shift, 1), flow_ref[c, rows, :])
    beside = pl.ds(CELLS - 1, 2, stride=CELLS + 1)
    side_low = velocity(
        edge_stream(lpost_ref, lambda b: pl.ds(CELLS - 1 - b, 2, stride=CELLS + 1)), low_ref[SOLID, beside, :]
    )
    side_high = velocity(
        edge_stream(hpost_ref, lambda b: pl.ds(CELLS - 1 - b, 2, stride=CELLS + 1)), high_ref[SOLID, beside, :]
    )
    for c in range(3):
        joined = join(side_low[c], side_high[c])
        for k, y in enumerate((-1, CELLS)):
            rows = row_slice(REACH, y)
            spread = pltpu.roll(
                jnp.broadcast_to(joined[k : k + 1], (CELLS, LANES)),
                LANES - (GROUP * (LAST - REACH) + 3),
                1,
                stride=GROUP,
                stride_axis=0,
            )
            rim_ref[c, rows, :] = jnp.where(ends, spread, flow_ref[c, rows, :])

    own = range(REACH, REACH + CELLS)

    def here(c):
        return [rim_ref[c, plane_rows(plane, 0), :] for plane in own]

    def along_first(c):
        return [
            0.5 * (rim_ref[c, plane_rows(plane + 1, 0), :] - rim_ref[c, plane_rows(plane - 1, 0), :]) for plane in own
        ]

    def along_second(c):
        return [0.5 * (rim_ref[c, plane_rows(plane, 1), :] - rim_ref[c, plane_rows(plane, -1), :]) for plane in own]

    def along_third(c):
        low = [turn(value, 1, 1) for value in here(c)]
        high = [turn(value, -1, 1) for value in here(c)]
        out = []
        for k, plane in enumerate(own):
            base = GROUP * (LAST - plane)
            first = jnp.where(lane == 0, turn(flow_low[c], -2 - base, 1), low[k])
            second = jnp.where(lane == LANES - 1, turn(flow_high[c], -6 - base, 1), high[k])
            out.append(0.5 * (second - first))
        return out

    def minus(first, second):
        return [a - b for a, b in zip(first, second)]

    vort = (
        minus(along_second(2), along_third(1)),
        minus(along_third(0), along_first(2)),
        minus(along_first(1), along_second(0)),
    )
    s_two = jnp.concatenate([a * a + b * b + c * c for a, b, c in zip(*vort)], axis=0)
    flow_first = jnp.concatenate(here(0), axis=0)
    solid_on = p_ref[SOLID] > 0.5
    ratio = s_two / (s_two + shade_scale)
    alpha = jnp.where(solid_on, solid_alpha, alpha_top * (1.0 - jnp.exp(-s_two / shade_scale)))
    red = jnp.where(solid_on, 0.6, 0.3 + 1.5 * ratio)
    green = jnp.where(solid_on, 0.6, 1.2 - 0.9 * ratio)
    blue = jnp.where(solid_on, 0.6, 0.8 + 0.4 * jnp.tanh(20.0 * flow_first))
    logs = jnp.log1p(-alpha)
    running = logs
    wide = lanes_of(CELLS * CELLS)
    for step in (1, 2, 4, 8, 16, 32, 64):
        running = running + jnp.where(wide >= step, turn(running, step, 1), 0.0)
    weight = alpha * jnp.exp(running - logs)
    acc = jnp.zeros((CELLS, LANES), jnp.float32)
    for ch, value in enumerate((red * weight, green * weight, blue * weight, logs)):
        total = jnp.sum(value, axis=1, keepdims=True)
        for x in range(CELLS):
            acc = jnp.where(lane // UP == ch * CELLS + x, total[x * CELLS : (x + 1) * CELLS], acc)
    out_ref[...] = acc
    save.wait()


def last_kernel(slab_ref, rank_ref, out_ref):
    slabs = slab_ref[...]
    rank = rank_ref[...]
    channel = lanes_of(CELLS) // (CELLS * UP)
    logs = slabs
    for ch in range(3):
        logs = jnp.where(channel == ch, turn(slabs, (ch + 1) * CELLS * UP, 1), logs)
    front = jnp.zeros_like(slabs)
    for s in range(CELLS):
        front = front + jnp.where(rank[s : s + 1] < rank, logs[s : s + 1], 0.0)
    colour = jnp.sum(jnp.exp(front) * slabs, axis=0, keepdims=True)
    opacity = 1.0 - jnp.exp(jnp.sum(logs, axis=0, keepdims=True))
    row = jnp.where(channel[:1] == 3, opacity, colour)
    for ch in range(4):
        out_ref[ch] = jnp.broadcast_to(turn(row, -ch * CELLS * UP, 1)[:, : CELLS * UP], (UP, CELLS * UP))


def call(kernel, outs, scratch=(), first_out_hbm=False, in_hbm=False):
    shapes = tuple(jax.ShapeDtypeStruct(shape, jnp.float32) for shape in outs)
    extra = {}
    if in_hbm:
        extra["in_specs"] = [pl.BlockSpec(memory_space=pltpu.HBM)] * 3
    if first_out_hbm:
        spaces = [pltpu.HBM] + [pltpu.VMEM] * (len(outs) - 1)
        extra["out_specs"] = tuple(pl.BlockSpec(memory_space=space) for space in spaces)
    return pl.pallas_call(
        kernel,
        out_shape=shapes,
        scratch_shapes=scratch,
        compiler_params=pltpu.CompilerParams(vmem_limit_bytes=24 * 1024 * 1024),
        **extra,
    )


def both_ways(lo, hi, axis):
    count = lax.axis_size(axis)
    forward = [(i, (i + 1) % count) for i in range(count)]
    backward = [(target, source) for source, target in forward]
    return lax.ppermute(hi, axis, forward), lax.ppermute(lo, axis, backward)


def in_pairs(first, second, axis):
    count = lax.axis_size(axis)
    out = []
    for start, value in ((0, first), (1, second)):
        pairs = []
        for i in range(start, count + start, 2):
            left, right = i % count, (i + 1) % count
            pairs += [(left, right), (right, left)]
        out.append(lax.ppermute(value, axis, pairs))
    return out


def body(populations, solid_mask, jet_mask, visibility):
    cells = CELLS * CELLS
    f = populations.reshape(27, cells, LANES)
    solid = solid_mask.reshape(cells, LANES)
    jet = jet_mask.reshape(cells, LANES)
    f, solid, jet = [pltpu.with_memory_space_constraint(value, pltpu.HBM) for value in (f, solid, jet)]
    x_shape = (X_COUNT, CELLS, LANES)
    y_shape = (Y_OWN, LANES)
    post, lo, hi, down, up = call(
        first_kernel,
        ((29, cells, LANES), x_shape, x_shape, y_shape, y_shape),
        (
            pltpu.VMEM((27, cells, LANES), jnp.float32),
            pltpu.VMEM((cells, LANES), jnp.int32),
            pltpu.VMEM((cells, LANES), jnp.int32),
            pltpu.SemaphoreType.DMA((CELLS + 2,)),
        ),
        in_hbm=True,
    )(f, solid, jet)
    xlo, xhi = both_ways(lo, hi, "gx")
    ylo, yhi = both_ways(down, up, "gy")
    corner_shape = (Y_CORNER, LANES)
    first, second = call(second_kernel, (corner_shape, corner_shape))(xlo, xhi)
    first, second = in_pairs(first, second, "gy")
    tile_shape = (29, CELLS, LANES)
    low, high = call(faces_kernel, (tile_shape, tile_shape))(post, xlo, xhi)
    half_shape = (HALF, 2 * CELLS, LANES)
    halo, low_halo, lo, hi = call(
        third_kernel, ((29, (SPAN + 1) * CELLS, LANES), tile_shape, half_shape, half_shape)
    )(ylo, yhi, first, second, low)
    zlo, zhi = both_ways(lo, hi, "gz")
    height = SPAN * ROWS + CELLS
    moved, flow, high_halo = call(
        steps_kernel,
        ((27, cells, LANES), (3, height, LANES), tile_shape),
        (pltpu.VMEM((29, height, LANES), jnp.float32), pltpu.VMEM((27, height, LANES), jnp.float32)),
    )(post, xlo, xhi, halo)
    edge = pltpu.VMEM((29, 3 * CELLS, LANES), jnp.float32)
    edge_post = pltpu.VMEM((27, 3 * CELLS, LANES), jnp.float32)
    advanced, slabs = call(
        render_kernel,
        ((27, cells, LANES), (CELLS, LANES)),
        (
            edge,
            edge,
            edge_post,
            edge_post,
            pltpu.VMEM((27, cells, LANES), jnp.float32),
            pltpu.VMEM((3, height, LANES), jnp.float32),
            pltpu.SemaphoreType.DMA,
        ),
        first_out_hbm=True,
    )(post, moved, flow, low, low_halo, high, high_halo, zlo, zhi)
    slabs = lax.all_to_all(slabs, "gz", 0, 0, tiled=True)
    rank = jnp.broadcast_to(visibility[:, None], (CELLS, LANES))
    (image,) = call(last_kernel, ((4, UP, CELLS * UP),))(slabs, rank)
    return advanced.reshape(27, CELLS, CELLS, LANES), jnp.swapaxes(image, 1, 2)


def solution(mesh):
    return jax.shard_map(
        body,
        mesh=mesh,
        in_specs=(P(None, "gx", "gy", "gz"), P("gx", "gy", "gz"), P("gx", "gy", "gz"), P()),
        out_specs=(P(None, "gx", "gy", "gz"), P(None, "gx", ("gy", "gz"))),
        check_vma=False,
    )
```

```python
import jax
import jax.numpy as jnp
import numpy as np
from jax import lax
from jax.experimental import pallas as pl
from jax.experimental.pallas import tpu as pltpu
from jax.sharding import PartitionSpec as P

UP = 4
CELLS = 8
LANES = 128
REACH = 3
SPAN = CELLS + 2 * REACH
LAST = SPAN - 1
ROWS = 16
HALF = 15
GROUP = 8

omega_rate = 1.25
jet_speed = 0.12
alpha_top = 0.03
solid_alpha = 0.15
shade_scale = 0.002

DIRS = [(a, b, c) for a in (-1, 0, 1) for b in (-1, 0, 1) for c in (-1, 0, 1)]
WEIGHTS = [(8.0 / 27.0, 2.0 / 27.0, 1.0 / 54.0, 1.0 / 216.0)[abs(a) + abs(b) + abs(c)] for a, b, c in DIRS]
SOLID, JET = 27, 28
MASKS = (SOLID, JET)


def axis_list(axis, inward):
    out = []
    for dist, allowed in ((1, (-1, 0, 1)), (2, (0, inward)), (3, (inward,))):
        out += [(i, dist) for i in range(27) if DIRS[i][axis] in allowed]
    out += [(m, dist) for m in MASKS for dist in (1, 2)]
    return out


def held(key, x):
    dist, inward = (-x, 1) if x < 0 else (x - CELLS + 1, -1)
    if dist <= 0:
        return True
    return (key, dist) in axis_list(0, inward)


def corner_list(inward):
    out = []
    for key, dist in axis_list(1, inward):
        first, second = (0, 0) if key in MASKS else DIRS[key][:2]
        for x in (-3, -2, -1, 8, 9, 10):
            far = -(x + first) if x < 0 else x + first - CELLS + 1
            if held(key, x) and not (far >= 2 and dist - inward * second >= 2):
                out.append((key, dist, x))
    return out


X_COUNT = len(axis_list(0, 1))
Y_CORNER = -(-len(corner_list(1)) // 8) * 8


def moments(f):
    third = None
    parts = []
    for a in range(3):
        row = []
        for b in range(3):
            lo, mid, hi = f[9 * a + 3 * b], f[9 * a + 3 * b + 1], f[9 * a + 3 * b + 2]
            row.append((lo + hi) + mid)
            diff = hi - lo
            third = diff if third is None else third + diff
        parts.append(row)
    sums = [(row[0] + row[2]) + row[1] for row in parts]
    second = (parts[0][2] - parts[0][0]) + (parts[1][2] - parts[1][0]) + (parts[2][2] - parts[2][0])
    return (sums[0] + sums[2]) + sums[1], sums[2] - sums[0], second, third


def collide(f, solid, jet):
    density, first, second, third = moments(f)
    scale = 1.0 / density
    ux = jnp.where(jet, jet_speed, first * scale)
    uy = jnp.where(jet, 0.0, second * scale)
    uz = jnp.where(jet, 0.0, third * scale)
    gain = jnp.where(jet, 1.0, omega_rate) * density
    keep = jnp.where(jet, 0.0, 1.0 - omega_rate)
    base = 1.0 - 1.5 * (ux * ux + uy * uy + uz * uz)
    strength = {w: gain * w for w in set(WEIGHTS)}
    post = [None] * 27
    comps = (ux, uy, uz)
    for i in range(14):
        w = strength[WEIGHTS[i]]
        if i == 13:
            post[i] = jnp.where(solid, f[i], w * base + keep * f[i])
            continue
        along = None
        for c, u in zip(DIRS[i], comps):
            if c == 0:
                continue
            if along is None:
                along = u if c > 0 else -u
            else:
                along = along + u if c > 0 else along - u
        even = w * (base + 4.5 * (along * along))
        odd = w * (3.0 * along)
        j = 26 - i
        post[i] = jnp.where(solid, f[j], (even + odd) + keep * f[i])
        post[j] = jnp.where(solid, f[i], (even - odd) + keep * f[j])
    return post


def lanes_of(rows):
    return lax.broadcasted_iota(jnp.int32, (rows, LANES), 1)


def turn(value, shift, axis):
    size = value.shape[axis]
    if isinstance(shift, int):
        shift = shift % size
        if shift == 0:
            return value
    return pltpu.roll(value, shift, axis)


def is_even(axis):
    return lax.axis_index(axis) % 2 == 0


def first_kernel(f_hbm, solid_hbm, jet_hbm, p_ref, xa_ref, xb_ref, ya_ref, yb_ref, f_ref, solid_ref, jet_ref, sems):
    masks = [
        pltpu.make_async_copy(solid_hbm, solid_ref, sems.at[CELLS]),
        pltpu.make_async_copy(jet_hbm, jet_ref, sems.at[CELLS + 1]),
    ]
    copies = []
    for x in range(CELLS):
        rows = pl.ds(x * CELLS, CELLS)
        copies.append(pltpu.make_async_copy(f_hbm.at[:, rows, :], f_ref.at[:, rows, :], sems.at[x]))
    for copy in masks + copies:
        copy.start()
    for copy in masks:
        copy.wait()
    p_ref[SOLID] = solid_ref[...].astype(jnp.float32)
    p_ref[JET] = jet_ref[...].astype(jnp.float32)
    for x in range(CELLS):
        copies[x].wait()
        rows = pl.ds(x * CELLS, CELLS)
        f = [f_ref[i, rows, :] for i in range(27)]
        post = collide(f, solid_ref[rows, :] == 1, jet_ref[rows, :] == 1)
        for i in range(27):
            p_ref[i, rows, :] = post[i]
    even = is_even("gx")
    for k, (low, high) in enumerate(zip(axis_list(0, -1), axis_list(0, 1))):
        lo = p_ref[low[0], pl.ds((low[1] - 1) * CELLS, CELLS), :]
        hi = p_ref[high[0], pl.ds((CELLS - high[1]) * CELLS, CELLS), :]
        xa_ref[k] = jnp.where(even, hi, lo)
        xb_ref[k] = jnp.where(even, lo, hi)
    even = is_even("gy")
    for k, (low, high) in enumerate(zip(axis_list(1, -1), axis_list(1, 1))):
        lo = p_ref[low[0], pl.ds(low[1] - 1, CELLS, stride=CELLS), :]
        hi = p_ref[high[0], pl.ds(CELLS - high[1], CELLS, stride=CELLS), :]
        ya_ref[k] = jnp.where(even, hi, lo)
        yb_ref[k] = jnp.where(even, lo, hi)


ENTRY = {(axis, inward): {e: k for k, e in enumerate(axis_list(axis, inward))} for axis in (0, 1) for inward in (1, -1)}


def from_pair(axis, inward, dist, key, a_ref, b_ref, even, rows=slice(None)):
    k = ENTRY[(axis, inward)][(key, dist)]
    if inward > 0:
        return jnp.where(even, b_ref[k, rows, :], a_ref[k, rows, :])
    return jnp.where(even, a_ref[k, rows, :], b_ref[k, rows, :])


def plane_value(key, x, p_ref, xa_ref, xb_ref, even):
    if x < 0:
        return from_pair(0, 1, -x, key, xa_ref, xb_ref, even)
    if x >= CELLS:
        return from_pair(0, -1, x - CELLS + 1, key, xa_ref, xb_ref, even)
    return p_ref[key, pl.ds(x * CELLS, CELLS), :]


def second_kernel(xa_ref, xb_ref, lo_ref, hi_ref):
    even = is_even("gx")
    for inward, out_ref in ((-1, lo_ref), (1, hi_ref)):
        for k, (key, dist, x) in enumerate(corner_list(inward)):
            row = pl.ds(dist - 1 if inward < 0 else CELLS - dist, 1)
            side, far = (1, -x) if x < 0 else (-1, x - CELLS + 1)
            out_ref[pl.ds(k, 1), :] = from_pair(0, side, far, key, xa_ref, xb_ref, even, row)


def pack(tiles):
    group = lanes_of(CELLS) // GROUP
    acc = [jnp.zeros((CELLS, LANES), jnp.float32)] * 29
    for place, shift, load in tiles:
        here = group == place % (LANES // GROUP)
        for key in range(29):
            value = load(key)
            if value is not None:
                acc[key] = jnp.where(here, turn(value, shift, 1), acc[key])
    return acc


def faces_kernel(p_ref, xa_ref, xb_ref, low_ref, high_ref):
    even = is_even("gx")

    def load(key, plane):
        if held(key, plane - REACH):
            return plane_value(key, plane - REACH, p_ref, xa_ref, xb_ref, even)

    for out_ref, start in ((low_ref, 3), (high_ref, 5)):
        tiles = [
            (LAST - plane, GROUP * (LAST - plane) + start, lambda key, plane=plane: load(key, plane))
            for plane in range(SPAN)
        ]
        for key, value in enumerate(pack(tiles)):
            out_ref[key] = value


def pack_halo(h_ref, start):
    upper = lax.broadcasted_iota(jnp.int32, (CELLS, LANES), 0) < CELLS // 2
    tiles = [
        (
            LAST - tile,
            GROUP * (LAST - tile) + start,
            lambda key, tile=tile: h_ref[key, pl.ds(tile * CELLS, CELLS), :],
        )
        for tile in range(SPAN + 1)
    ]
    return [jnp.where(upper, turn(value, GROUP, 1), value) for value in pack(tiles)]


def third_kernel(ya_ref, yb_ref, clo_ref, chi_ref, main_ref, h_ref, z_ref, lo_ref, hi_ref):
    even = is_even("gy")
    for inward, corner_ref in ((1, clo_ref), (-1, chi_ref)):
        for k, (key, dist) in enumerate(axis_list(1, inward)):
            start = CELLS * REACH + CELLS - dist if inward > 0 else CELLS * (REACH + 1) + dist - 1
            h_ref[key, pl.ds(start, CELLS, stride=CELLS), :] = from_pair(1, inward, dist, key, ya_ref, yb_ref, even)
        for k, (key, dist, x) in enumerate(corner_list(inward)):
            plane = x + REACH
            row = CELLS * plane + CELLS - dist if inward > 0 else CELLS * (plane + 1) + dist - 1
            h_ref[key, pl.ds(row, 1), :] = corner_ref[pl.ds(k, 1), :]
    halo = pack_halo(h_ref, 3)
    early = lanes_of(CELLS) % GROUP < REACH
    for key in range(29):
        z_ref[key] = halo[key]
    for part, values in enumerate(([main_ref[key] for key in range(29)], halo)):
        rows = pl.ds(part * CELLS, CELLS)
        for out_ref, shift in ((lo_ref, -REACH), (hi_ref, REACH)):
            for k in range(HALF):
                value = values[k]
                if k + HALF < 29:
                    other = turn(values[k + HALF], shift, 1)
                    value = jnp.where(early, other, value) if shift < 0 else jnp.where(early, value, other)
                out_ref[k, rows, :] = value


def plane_rows(plane, y):
    return pl.ds(plane * ROWS + CELLS + y, CELLS)


def row_slice(plane, y):
    return pl.ds(plane * ROWS + CELLS + y, CELLS, stride=ROWS)


def velocity(f, solid):
    density, first, second, third = moments(f)
    scale = (1.0 - solid) / density
    return first * scale, second * scale, third * scale


def steps_kernel(p_ref, xa_ref, xb_ref, h_ref, adv_ref, flow_ref, high_ref, e_ref, g_ref):
    even = is_even("gx")
    for plane in range(SPAN):
        for key in range(29):
            if held(key, plane - REACH):
                e_ref[key, plane_rows(plane, 0), :] = plane_value(key, plane - REACH, p_ref, xa_ref, xb_ref, even)
    for tile in range(SPAN + 1):
        for key in range(29):
            e_ref[key, pl.ds(tile * ROWS, CELLS), :] = h_ref[key, pl.ds(tile * CELLS, CELLS), :]

    def stream(ref, rows):
        out = [None] * 27
        for move in (-1, 1, 0):
            for i, (a, b, c) in enumerate(DIRS):
                if c == move:
                    out[i] = turn(ref[i, rows(a, b), :], c, 1)
        return out

    def plane_stream(ref, plane, y):
        return stream(ref, lambda a, b: plane_rows(plane - a, y - b))

    def row_stream(ref, y):
        return stream(ref, lambda a, b: row_slice(REACH - a, y - b))

    def settle(rows, f):
        post = collide(f, e_ref[SOLID, rows, :] > 0.5, e_ref[JET, rows, :] > 0.5)
        for i in range(27):
            g_ref[i, rows, :] = post[i]

    def step_one(plane, y):
        settle(plane_rows(plane, y), plane_stream(e_ref, plane, y))

    def step_one_own(k, carry):
        step_one(REACH + 2 * k, 0)
        step_one(REACH + 2 * k + 1, 0)
        return carry

    def step_one_halo(k, carry):
        plane = k + 1 + CELLS * (k // 2)
        step_one(plane, -2)
        step_one(plane, 6)
        return carry

    lax.fori_loop(0, CELLS // 2, step_one_own, 0)
    lax.fori_loop(0, 4, step_one_halo, 0)
    for y in (-2, -1, CELLS, CELLS + 1):
        settle(row_slice(REACH, y), row_stream(e_ref, y))

    def store_flow(rows, f):
        for c, value in enumerate(velocity(f, e_ref[SOLID, rows, :])):
            flow_ref[c, rows, :] = value

    def step_two(plane):
        f = plane_stream(g_ref, plane, 0)
        rows = pl.ds(pl.multiple_of((plane - REACH) * CELLS, CELLS), CELLS)
        for i in range(27):
            adv_ref[i, rows, :] = f[i]
        store_flow(plane_rows(plane, 0), f)

    def step_two_own(k, carry):
        step_two(REACH + 2 * k)
        step_two(REACH + 2 * k + 1)
        return carry

    lax.fori_loop(0, CELLS // 2, step_two_own, 0)
    for plane in (REACH - 1, REACH + CELLS):
        store_flow(plane_rows(plane, 0), plane_stream(g_ref, plane, 0))
    for y in (-1, CELLS):
        store_flow(row_slice(REACH, y), row_stream(g_ref, y))
    for key, value in enumerate(pack_halo(h_ref, 5)):
        high_ref[key] = value


def render_kernel(
    p_ref, adv_ref, flow_ref, lmain_ref, lhalo_ref, hmain_ref, hhalo_ref, zlo_ref, zhi_ref,
    adv_hbm, out_ref, low_ref, high_ref, lpost_ref, hpost_ref, done_ref, rim_ref, sem,
):
    lane = lanes_of(CELLS)
    slot = lane % GROUP
    ends = (lane < 2) | (lane >= LANES - 2)

    for part in range(2):
        rows = pl.ds(part * CELLS, CELLS)
        own_low, own_high = (lmain_ref, hmain_ref) if part == 0 else (lhalo_ref, hhalo_ref)
        low = [zlo_ref[key, rows, :] for key in range(HALF)]
        low += [turn(zlo_ref[key, rows, :], -REACH, 1) for key in range(29 - HALF)]
        high = [turn(zhi_ref[key, rows, :], 2, 1) for key in range(HALF)]
        high += [turn(zhi_ref[key, rows, :], REACH + 2, 1) for key in range(29 - HALF)]
        for key in range(29):
            first = jnp.where(slot < 3, low[key], own_low[key])
            second = jnp.where(slot >= 5, high[key], own_high[key])
            for start in (CELLS,) if part == 0 else (0, 2 * CELLS):
                low_ref[key, pl.ds(start, CELLS), :] = first
                high_ref[key, pl.ds(start, CELLS), :] = second

    def edge_stream(ref, rows):
        out = [None] * 27
        for a in (-1, 0, 1):
            for c in (-1, 0, 1):
                for b in (-1, 0, 1):
                    i = 9 * a + 3 * b + c + 13
                    out[i] = turn(ref[i, rows(b), :], c - GROUP * a, 1)
        return out

    for y in (-2, 6):
        for ref, post_ref in ((low_ref, lpost_ref), (high_ref, hpost_ref)):
            rows = pl.ds(CELLS + y, CELLS)
            f = edge_stream(ref, lambda b: pl.ds(CELLS + y - b, CELLS))
            post = collide(f, ref[SOLID, rows, :] > 0.5, ref[JET, rows, :] > 0.5)
            for i in range(27):
                post_ref[i, rows, :] = post[i]

    def join(low, high):
        return jnp.where(lanes_of(low.shape[0]) % GROUP < 3, turn(high, -2, 1), low)

    f_low = edge_stream(lpost_ref, lambda b: pl.ds(CELLS - b, CELLS))
    flow_low = velocity(f_low, low_ref[SOLID, pl.ds(CELLS, CELLS), :])
    f_high = edge_stream(hpost_ref, lambda b: pl.ds(CELLS - b, CELLS))
    flow_high = velocity(f_high, high_ref[SOLID, pl.ds(CELLS, CELLS), :])
    joined = [join(low, high) for low, high in zip(f_low, f_high)]
    for x in range(CELLS):
        rows = pl.ds(x * CELLS, CELLS)
        shift = -(GROUP * (LAST - REACH - x) + 3)
        for i in range(27):
            done_ref[i, rows, :] = jnp.where(ends, turn(joined[i], shift, 1), adv_ref[i, rows, :])
    save = pltpu.make_async_copy(done_ref, adv_hbm, sem)
    save.start()
    joined = [join(low, high) for low, high in zip(flow_low, flow_high)]
    for plane in range(REACH - 1, REACH + CELLS + 1):
        rows = plane_rows(plane, 0)
        shift = -(GROUP * (LAST - plane) + 3)
        for c in range(3):
            rim_ref[c, rows, :] = jnp.where(ends, turn(joined[c], shift, 1), flow_ref[c, rows, :])
    beside = pl.ds(CELLS - 1, 2, stride=CELLS + 1)
    side_low = velocity(
        edge_stream(lpost_ref, lambda b: pl.ds(CELLS - 1 - b, 2, stride=CELLS + 1)), low_ref[SOLID, beside, :]
    )
    side_high = velocity(
        edge_stream(hpost_ref, lambda b: pl.ds(CELLS - 1 - b, 2, stride=CELLS + 1)), high_ref[SOLID, beside, :]
    )
    for c in range(3):
        joined = join(side_low[c], side_high[c])
        for k, y in enumerate((-1, CELLS)):
            rows = row_slice(REACH, y)
            spread = pltpu.roll(
                jnp.broadcast_to(joined[k : k + 1], (CELLS, LANES)),
                LANES - (GROUP * (LAST - REACH) + 3),
                1,
                stride=GROUP,
                stride_axis=0,
            )
            rim_ref[c, rows, :] = jnp.where(ends, spread, flow_ref[c, rows, :])

    own = range(REACH, REACH + CELLS)

    def here(c):
        return [rim_ref[c, plane_rows(plane, 0), :] for plane in own]

    def along_first(c):
        return [
            0.5 * (rim_ref[c, plane_rows(plane + 1, 0), :] - rim_ref[c, plane_rows(plane - 1, 0), :]) for plane in own
        ]

    def along_second(c):
        return [0.5 * (rim_ref[c, plane_rows(plane, 1), :] - rim_ref[c, plane_rows(plane, -1), :]) for plane in own]

    def along_third(c):
        low = [turn(value, 1, 1) for value in here(c)]
        high = [turn(value, -1, 1) for value in here(c)]
        out = []
        for k, plane in enumerate(own):
            base = GROUP * (LAST - plane)
            first = jnp.where(lane == 0, turn(flow_low[c], -2 - base, 1), low[k])
            second = jnp.where(lane == LANES - 1, turn(flow_high[c], -6 - base, 1), high[k])
            out.append(0.5 * (second - first))
        return out

    def minus(first, second):
        return [a - b for a, b in zip(first, second)]

    vort = (
        minus(along_second(2), along_third(1)),
        minus(along_third(0), along_first(2)),
        minus(along_first(1), along_second(0)),
    )
    s_two = jnp.concatenate([a * a + b * b + c * c for a, b, c in zip(*vort)], axis=0)
    flow_first = jnp.concatenate(here(0), axis=0)
    solid_on = p_ref[SOLID] > 0.5
    ratio = s_two / (s_two + shade_scale)
    alpha = jnp.where(solid_on, solid_alpha, alpha_top * (1.0 - jnp.exp(-s_two / shade_scale)))
    red = jnp.where(solid_on, 0.6, 0.3 + 1.5 * ratio)
    green = jnp.where(solid_on, 0.6, 1.2 - 0.9 * ratio)
    blue = jnp.where(solid_on, 0.6, 0.8 + 0.4 * jnp.tanh(20.0 * flow_first))
    logs = jnp.log1p(-alpha)
    running = logs
    wide = lanes_of(CELLS * CELLS)
    for step in (1, 2, 4, 8, 16, 32, 64):
        running = running + jnp.where(wide >= step, turn(running, step, 1), 0.0)
    weight = alpha * jnp.exp(running - logs)
    acc = jnp.zeros((CELLS, LANES), jnp.float32)
    for ch, value in enumerate((red * weight, green * weight, blue * weight, logs)):
        total = jnp.sum(value, axis=1, keepdims=True)
        for x in range(CELLS):
            acc = jnp.where(lane // UP == ch * CELLS + x, total[x * CELLS : (x + 1) * CELLS], acc)
    out_ref[...] = acc
    save.wait()


def last_kernel(slab_ref, rank_ref, out_ref):
    slabs = slab_ref[...]
    rank = rank_ref[...]
    channel = lanes_of(CELLS) // (CELLS * UP)
    logs = slabs
    for ch in range(3):
        logs = jnp.where(channel == ch, turn(slabs, (ch + 1) * CELLS * UP, 1), logs)
    front = jnp.zeros_like(slabs)
    for s in range(CELLS):
        front = front + jnp.where(rank[s : s + 1] < rank, logs[s : s + 1], 0.0)
    colour = jnp.sum(jnp.exp(front) * slabs, axis=0, keepdims=True)
    opacity = 1.0 - jnp.exp(jnp.sum(logs, axis=0, keepdims=True))
    row = jnp.where(channel[:1] == 3, opacity, colour)
    for ch in range(4):
        out_ref[ch] = jnp.broadcast_to(turn(row, -ch * CELLS * UP, 1)[:, : CELLS * UP], (UP, CELLS * UP))


def call(kernel, outs, scratch=(), first_out_hbm=False, in_hbm=False):
    shapes = tuple(jax.ShapeDtypeStruct(shape, jnp.float32) for shape in outs)
    extra = {}
    if in_hbm:
        extra["in_specs"] = [pl.BlockSpec(memory_space=pltpu.HBM)] * 3
    if first_out_hbm:
        spaces = [pltpu.HBM] + [pltpu.VMEM] * (len(outs) - 1)
        extra["out_specs"] = tuple(pl.BlockSpec(memory_space=space) for space in spaces)
    return pl.pallas_call(
        kernel,
        out_shape=shapes,
        scratch_shapes=scratch,
        compiler_params=pltpu.CompilerParams(vmem_limit_bytes=24 * 1024 * 1024),
        **extra,
    )


def both_ways(lo, hi, axis):
    count = lax.axis_size(axis)
    forward = [(i, (i + 1) % count) for i in range(count)]
    backward = [(target, source) for source, target in forward]
    return lax.ppermute(hi, axis, forward), lax.ppermute(lo, axis, backward)


def in_pairs(first, second, axis):
    count = lax.axis_size(axis)
    out = []
    for start, value in ((0, first), (1, second)):
        pairs = []
        for i in range(start, count + start, 2):
            left, right = i % count, (i + 1) % count
            pairs += [(left, right), (right, left)]
        out.append(lax.ppermute(value, axis, pairs))
    return out


def body(populations, solid_mask, jet_mask, visibility):
    cells = CELLS * CELLS
    f = populations.reshape(27, cells, LANES)
    solid = solid_mask.reshape(cells, LANES)
    jet = jet_mask.reshape(cells, LANES)
    f, solid, jet = [pltpu.with_memory_space_constraint(value, pltpu.HBM) for value in (f, solid, jet)]
    send_shape = (X_COUNT, CELLS, LANES)
    post, xa, xb, ya, yb = call(
        first_kernel,
        ((29, cells, LANES),) + (send_shape,) * 4,
        (
            pltpu.VMEM((27, cells, LANES), jnp.float32),
            pltpu.VMEM((cells, LANES), jnp.int32),
            pltpu.VMEM((cells, LANES), jnp.int32),
            pltpu.SemaphoreType.DMA((CELLS + 2,)),
        ),
        in_hbm=True,
    )(f, solid, jet)
    xa, xb = in_pairs(xa, xb, "gx")
    ya, yb = in_pairs(ya, yb, "gy")
    corner_shape = (Y_CORNER, LANES)
    lo, hi = call(second_kernel, (corner_shape, corner_shape))(xa, xb)
    clo, chi = both_ways(lo, hi, "gy")
    tile_shape = (29, CELLS, LANES)
    low, high = call(faces_kernel, (tile_shape, tile_shape))(post, xa, xb)
    half_shape = (HALF, 2 * CELLS, LANES)
    halo, low_halo, lo, hi = call(
        third_kernel, ((29, (SPAN + 1) * CELLS, LANES), tile_shape, half_shape, half_shape)
    )(ya, yb, clo, chi, low)
    zlo, zhi = both_ways(lo, hi, "gz")
    height = SPAN * ROWS + CELLS
    moved, flow, high_halo = call(
        steps_kernel,
        ((27, cells, LANES), (3, height, LANES), tile_shape),
        (pltpu.VMEM((29, height, LANES), jnp.float32), pltpu.VMEM((27, height, LANES), jnp.float32)),
    )(post, xa, xb, halo)
    edge = pltpu.VMEM((29, 3 * CELLS, LANES), jnp.float32)
    edge_post = pltpu.VMEM((27, 3 * CELLS, LANES), jnp.float32)
    advanced, slabs = call(
        render_kernel,
        ((27, cells, LANES), (CELLS, LANES)),
        (
            edge,
            edge,
            edge_post,
            edge_post,
            pltpu.VMEM((27, cells, LANES), jnp.float32),
            pltpu.VMEM((3, height, LANES), jnp.float32),
            pltpu.SemaphoreType.DMA,
        ),
        first_out_hbm=True,
    )(post, moved, flow, low, low_halo, high, high_halo, zlo, zhi)
    slabs = lax.all_to_all(slabs, "gz", 0, 0, tiled=True)
    rank = jnp.broadcast_to(visibility[:, None], (CELLS, LANES))
    (image,) = call(last_kernel, ((4, UP, CELLS * UP),))(slabs, rank)
    return advanced.reshape(27, CELLS, CELLS, LANES), jnp.swapaxes(image, 1, 2)


def solution(mesh):
    return jax.shard_map(
        body,
        mesh=mesh,
        in_specs=(P(None, "gx", "gy", "gz"), P("gx", "gy", "gz"), P("gx", "gy", "gz"), P()),
        out_specs=(P(None, "gx", "gy", "gz"), P(None, "gx", ("gy", "gz"))),
        check_vma=False,
    )
```

```python
import jax
import jax.numpy as jnp
import numpy as np
from jax import lax
from jax.experimental import pallas as pl
from jax.experimental.pallas import tpu as pltpu
from jax.sharding import PartitionSpec as P

UP = 4
CELLS = 8
LANES = 128
REACH = 3
SPAN = CELLS + 2 * REACH
LAST = SPAN - 1
ROWS = 16
HALF = 15
GROUP = 8

omega_rate = 1.25
jet_speed = 0.12
alpha_top = 0.03
solid_alpha = 0.15
shade_scale = 0.002

DIRS = [(a, b, c) for a in (-1, 0, 1) for b in (-1, 0, 1) for c in (-1, 0, 1)]
WEIGHTS = [(8.0 / 27.0, 2.0 / 27.0, 1.0 / 54.0, 1.0 / 216.0)[abs(a) + abs(b) + abs(c)] for a, b, c in DIRS]
SOLID, JET = 27, 28
MASKS = (SOLID, JET)


def axis_list(axis, inward):
    out = []
    for dist, allowed in ((1, (-1, 0, 1)), (2, (0, inward)), (3, (inward,))):
        out += [(i, dist) for i in range(27) if DIRS[i][axis] in allowed]
    out += [(m, dist) for m in MASKS for dist in (1, 2)]
    return out


def held(key, x):
    dist, inward = (-x, 1) if x < 0 else (x - CELLS + 1, -1)
    if dist <= 0:
        return True
    return (key, dist) in axis_list(0, inward)


def corner_list(inward):
    out = []
    for key, dist in axis_list(1, inward):
        first, second = (0, 0) if key in MASKS else DIRS[key][:2]
        for x in (-3, -2, -1, 8, 9, 10):
            far = -(x + first) if x < 0 else x + first - CELLS + 1
            if held(key, x) and not (far >= 2 and dist - inward * second >= 2):
                out.append((key, dist, x))
    return out


X_COUNT = len(axis_list(0, 1))
Y_OWN = len(axis_list(1, 1)) * CELLS
Y_CORNER = -(-len(corner_list(1)) // 8) * 8


def moments(f):
    third = None
    parts = []
    for a in range(3):
        row = []
        for b in range(3):
            lo, mid, hi = f[9 * a + 3 * b], f[9 * a + 3 * b + 1], f[9 * a + 3 * b + 2]
            row.append((lo + hi) + mid)
            diff = hi - lo
            third = diff if third is None else third + diff
        parts.append(row)
    sums = [(row[0] + row[2]) + row[1] for row in parts]
    second = (parts[0][2] - parts[0][0]) + (parts[1][2] - parts[1][0]) + (parts[2][2] - parts[2][0])
    return (sums[0] + sums[2]) + sums[1], sums[2] - sums[0], second, third


def collide(f, solid, jet):
    density, first, second, third = moments(f)
    scale = 1.0 / density
    ux = jnp.where(jet, jet_speed, first * scale)
    uy = jnp.where(jet, 0.0, second * scale)
    uz = jnp.where(jet, 0.0, third * scale)
    gain = jnp.where(jet, 1.0, omega_rate) * density
    keep = jnp.where(jet, 0.0, 1.0 - omega_rate)
    base = 1.0 - 1.5 * (ux * ux + uy * uy + uz * uz)
    strength = {w: gain * w for w in set(WEIGHTS)}
    post = [None] * 27
    comps = (ux, uy, uz)
    for i in range(14):
        w = strength[WEIGHTS[i]]
        if i == 13:
            post[i] = jnp.where(solid, f[i], w * base + keep * f[i])
            continue
        along = None
        for c, u in zip(DIRS[i], comps):
            if c == 0:
                continue
            if along is None:
                along = u if c > 0 else -u
            else:
                along = along + u if c > 0 else along - u
        even = w * (base + 4.5 * (along * along))
        odd = w * (3.0 * along)
        j = 26 - i
        post[i] = jnp.where(solid, f[j], (even + odd) + keep * f[i])
        post[j] = jnp.where(solid, f[i], (even - odd) + keep * f[j])
    return post


def lanes_of(rows):
    return lax.broadcasted_iota(jnp.int32, (rows, LANES), 1)


def turn(value, shift, axis):
    size = value.shape[axis]
    if isinstance(shift, int):
        shift = shift % size
        if shift == 0:
            return value
    return pltpu.roll(value, shift, axis)


def is_even(axis):
    return lax.axis_index(axis) % 2 == 0


def first_kernel(
    f_hbm, solid_hbm, jet_hbm, p_ref, lo_ref, hi_ref, ya_ref, yb_ref, f_ref, solid_ref, jet_ref, sems
):
    masks = [
        pltpu.make_async_copy(solid_hbm, solid_ref, sems.at[CELLS]),
        pltpu.make_async_copy(jet_hbm, jet_ref, sems.at[CELLS + 1]),
    ]
    copies = []
    for x in range(CELLS):
        rows = pl.ds(x * CELLS, CELLS)
        copies.append(pltpu.make_async_copy(f_hbm.at[:, rows, :], f_ref.at[:, rows, :], sems.at[x]))
    for copy in masks + copies:
        copy.start()
    for copy in masks:
        copy.wait()
    p_ref[SOLID] = solid_ref[...].astype(jnp.float32)
    p_ref[JET] = jet_ref[...].astype(jnp.float32)
    for x in range(CELLS):
        copies[x].wait()
        rows = pl.ds(x * CELLS, CELLS)
        f = [f_ref[i, rows, :] for i in range(27)]
        post = collide(f, solid_ref[rows, :] == 1, jet_ref[rows, :] == 1)
        for i in range(27):
            p_ref[i, rows, :] = post[i]
    for k, (key, dist) in enumerate(axis_list(0, -1)):
        lo_ref[k] = p_ref[key, pl.ds((dist - 1) * CELLS, CELLS), :]
    for k, (key, dist) in enumerate(axis_list(0, 1)):
        hi_ref[k] = p_ref[key, pl.ds((CELLS - dist) * CELLS, CELLS), :]
    even = is_even("gy")
    for k, (low, high) in enumerate(zip(axis_list(1, -1), axis_list(1, 1))):
        rows = pl.ds(k * CELLS, CELLS)
        lo = p_ref[low[0], pl.ds(low[1] - 1, CELLS, stride=CELLS), :]
        hi = p_ref[high[0], pl.ds(CELLS - high[1], CELLS, stride=CELLS), :]
        ya_ref[rows, :] = jnp.where(even, hi, lo)
        yb_ref[rows, :] = jnp.where(even, lo, hi)


LOW_AT = {entry: k for k, entry in enumerate(axis_list(0, 1))}
HIGH_AT = {entry: k for k, entry in enumerate(axis_list(0, -1))}


def plane_ref(key, x, p_ref, xlo_ref, xhi_ref):
    if x < 0:
        return xlo_ref.at[LOW_AT[(key, -x)]]
    if x >= CELLS:
        return xhi_ref.at[HIGH_AT[(key, x - CELLS + 1)]]
    return p_ref.at[key, pl.ds(x * CELLS, CELLS), :]


def second_kernel(xlo_ref, xhi_ref, lo_ref, hi_ref):
    for inward, out_ref in ((-1, lo_ref), (1, hi_ref)):
        for k, (key, dist, x) in enumerate(corner_list(inward)):
            row = dist - 1 if inward < 0 else CELLS - dist
            out_ref[pl.ds(k, 1), :] = plane_ref(key, x, None, xlo_ref, xhi_ref)[pl.ds(row, 1), :]


def pack(tiles):
    group = lanes_of(CELLS) // GROUP
    acc = [jnp.zeros((CELLS, LANES), jnp.float32)] * 29
    for place, shift, load in tiles:
        here = group == place % (LANES // GROUP)
        for key in range(29):
            value = load(key)
            if value is not None:
                acc[key] = jnp.where(here, turn(value, shift, 1), acc[key])
    return acc


def faces_kernel(p_ref, xlo_ref, xhi_ref, low_ref, high_ref):
    def load(key, plane):
        if held(key, plane - REACH):
            return plane_ref(key, plane - REACH, p_ref, xlo_ref, xhi_ref)[...]

    for out_ref, start in ((low_ref, 3), (high_ref, 5)):
        tiles = [
            (LAST - plane, GROUP * (LAST - plane) + start, lambda key, plane=plane: load(key, plane))
            for plane in range(SPAN)
        ]
        for key, value in enumerate(pack(tiles)):
            out_ref[key] = value


def pack_halo(h_ref, start):
    upper = lax.broadcasted_iota(jnp.int32, (CELLS, LANES), 0) < CELLS // 2
    tiles = [
        (
            LAST - tile,
            GROUP * (LAST - tile) + start,
            lambda key, tile=tile: h_ref[key, pl.ds(tile * CELLS, CELLS), :],
        )
        for tile in range(SPAN + 1)
    ]
    return [jnp.where(upper, turn(value, GROUP, 1), value) for value in pack(tiles)]


def third_kernel(ya_ref, yb_ref, clo_ref, chi_ref, main_ref, h_ref, z_ref, lo_ref, hi_ref):
    even = is_even("gy")
    for inward, one_ref, two_ref, corner_ref in ((1, yb_ref, ya_ref, clo_ref), (-1, ya_ref, yb_ref, chi_ref)):
        for k, (key, dist) in enumerate(axis_list(1, inward)):
            start = CELLS * REACH + CELLS - dist if inward > 0 else CELLS * (REACH + 1) + dist - 1
            h_ref[key, pl.ds(start, CELLS, stride=CELLS), :] = jnp.where(
                even, one_ref[pl.ds(k * CELLS, CELLS), :], two_ref[pl.ds(k * CELLS, CELLS), :]
            )
        for k, (key, dist, x) in enumerate(corner_list(inward)):
            plane = x + REACH
            row = CELLS * plane + CELLS - dist if inward > 0 else CELLS * (plane + 1) + dist - 1
            h_ref[key, pl.ds(row, 1), :] = corner_ref[pl.ds(k, 1), :]
    halo = pack_halo(h_ref, 3)
    early = lanes_of(CELLS) % GROUP < REACH
    for key in range(29):
        z_ref[key] = halo[key]
    for part, values in enumerate(([main_ref[key] for key in range(29)], halo)):
        rows = pl.ds(part * CELLS, CELLS)
        for out_ref, shift in ((lo_ref, -REACH), (hi_ref, REACH)):
            for k in range(HALF):
                value = values[k]
                if k + HALF < 29:
                    other = turn(values[k + HALF], shift, 1)
                    value = jnp.where(early, other, value) if shift < 0 else jnp.where(early, value, other)
                out_ref[k, rows, :] = value


def plane_rows(plane, y):
    return pl.ds(plane * ROWS + CELLS + y, CELLS)


def row_slice(plane, y):
    return pl.ds(plane * ROWS + CELLS + y, CELLS, stride=ROWS)


def velocity(f, solid):
    density, first, second, third = moments(f)
    scale = (1.0 - solid) / density
    return first * scale, second * scale, third * scale


def steps_kernel(p_ref, xlo_ref, xhi_ref, h_ref, adv_ref, flow_ref, high_ref, e_ref, g_ref):
    for plane in range(SPAN):
        for key in range(29):
            if held(key, plane - REACH):
                e_ref[key, plane_rows(plane, 0), :] = plane_ref(key, plane - REACH, p_ref, xlo_ref, xhi_ref)[...]
    for tile in range(SPAN + 1):
        for key in range(29):
            e_ref[key, pl.ds(tile * ROWS, CELLS), :] = h_ref[key, pl.ds(tile * CELLS, CELLS), :]

    def stream(ref, rows):
        out = [None] * 27
        for move in (-1, 1, 0):
            for i, (a, b, c) in enumerate(DIRS):
                if c == move:
                    out[i] = turn(ref[i, rows(a, b), :], c, 1)
        return out

    def plane_stream(ref, plane, y):
        return stream(ref, lambda a, b: plane_rows(plane - a, y - b))

    def row_stream(ref, y):
        return stream(ref, lambda a, b: row_slice(REACH - a, y - b))

    def settle(rows, f):
        post = collide(f, e_ref[SOLID, rows, :] > 0.5, e_ref[JET, rows, :] > 0.5)
        for i in range(27):
            g_ref[i, rows, :] = post[i]

    def step_one(plane, y):
        settle(plane_rows(plane, y), plane_stream(e_ref, plane, y))

    def step_one_own(k, carry):
        step_one(REACH + 2 * k, 0)
        step_one(REACH + 2 * k + 1, 0)
        return carry

    def step_one_halo(k, carry):
        plane = k + 1 + CELLS * (k // 2)
        step_one(plane, -2)
        step_one(plane, 6)
        return carry

    lax.fori_loop(0, CELLS // 2, step_one_own, 0)
    lax.fori_loop(0, 4, step_one_halo, 0)
    for y in (-2, -1, CELLS, CELLS + 1):
        settle(row_slice(REACH, y), row_stream(e_ref, y))

    def store_flow(rows, f):
        for c, value in enumerate(velocity(f, e_ref[SOLID, rows, :])):
            flow_ref[c, rows, :] = value

    def step_two(plane):
        f = plane_stream(g_ref, plane, 0)
        rows = pl.ds(pl.multiple_of((plane - REACH) * CELLS, CELLS), CELLS)
        for i in range(27):
            adv_ref[i, rows, :] = f[i]
        store_flow(plane_rows(plane, 0), f)

    def step_two_own(k, carry):
        step_two(REACH + 2 * k)
        step_two(REACH + 2 * k + 1)
        return carry

    lax.fori_loop(0, CELLS // 2, step_two_own, 0)
    for plane in (REACH - 1, REACH + CELLS):
        store_flow(plane_rows(plane, 0), plane_stream(g_ref, plane, 0))
    for y in (-1, CELLS):
        store_flow(row_slice(REACH, y), row_stream(g_ref, y))
    for key, value in enumerate(pack_halo(h_ref, 5)):
        high_ref[key] = value


def render_kernel(
    p_ref, adv_ref, flow_ref, lmain_ref, lhalo_ref, hmain_ref, hhalo_ref, zlo_ref, zhi_ref,
    adv_hbm, out_ref, low_ref, high_ref, lpost_ref, hpost_ref, done_ref, rim_ref, sem,
):
    lane = lanes_of(CELLS)
    slot = lane % GROUP
    ends = (lane < 2) | (lane >= LANES - 2)

    for part in range(2):
        rows = pl.ds(part * CELLS, CELLS)
        own_low, own_high = (lmain_ref, hmain_ref) if part == 0 else (lhalo_ref, hhalo_ref)
        low = [zlo_ref[key, rows, :] for key in range(HALF)]
        low += [turn(zlo_ref[key, rows, :], -REACH, 1) for key in range(29 - HALF)]
        high = [turn(zhi_ref[key, rows, :], 2, 1) for key in range(HALF)]
        high += [turn(zhi_ref[key, rows, :], REACH + 2, 1) for key in range(29 - HALF)]
        for key in range(29):
            first = jnp.where(slot < 3, low[key], own_low[key])
            second = jnp.where(slot >= 5, high[key], own_high[key])
            for start in (CELLS,) if part == 0 else (0, 2 * CELLS):
                low_ref[key, pl.ds(start, CELLS), :] = first
                high_ref[key, pl.ds(start, CELLS), :] = second

    def edge_stream(ref, rows):
        out = [None] * 27
        for a in (-1, 0, 1):
            for c in (-1, 0, 1):
                for b in (-1, 0, 1):
                    i = 9 * a + 3 * b + c + 13
                    out[i] = turn(ref[i, rows(b), :], c - GROUP * a, 1)
        return out

    for y in (-2, 6):
        for ref, post_ref in ((low_ref, lpost_ref), (high_ref, hpost_ref)):
            rows = pl.ds(CELLS + y, CELLS)
            f = edge_stream(ref, lambda b: pl.ds(CELLS + y - b, CELLS))
            post = collide(f, ref[SOLID, rows, :] > 0.5, ref[JET, rows, :] > 0.5)
            for i in range(27):
                post_ref[i, rows, :] = post[i]

    def join(low, high):
        return jnp.where(lanes_of(low.shape[0]) % GROUP < 3, turn(high, -2, 1), low)

    f_low = edge_stream(lpost_ref, lambda b: pl.ds(CELLS - b, CELLS))
    flow_low = velocity(f_low, low_ref[SOLID, pl.ds(CELLS, CELLS), :])
    f_high = edge_stream(hpost_ref, lambda b: pl.ds(CELLS - b, CELLS))
    flow_high = velocity(f_high, high_ref[SOLID, pl.ds(CELLS, CELLS), :])
    joined = [join(low, high) for low, high in zip(f_low, f_high)]
    for x in range(CELLS):
        rows = pl.ds(x * CELLS, CELLS)
        shift = -(GROUP * (LAST - REACH - x) + 3)
        for i in range(27):
            done_ref[i, rows, :] = jnp.where(ends, turn(joined[i], shift, 1), adv_ref[i, rows, :])
    save = pltpu.make_async_copy(done_ref, adv_hbm, sem)
    save.start()
    joined = [join(low, high) for low, high in zip(flow_low, flow_high)]
    for plane in range(REACH - 1, REACH + CELLS + 1):
        rows = plane_rows(plane, 0)
        shift = -(GROUP * (LAST - plane) + 3)
        for c in range(3):
            rim_ref[c, rows, :] = jnp.where(ends, turn(joined[c], shift, 1), flow_ref[c, rows, :])
    beside = pl.ds(CELLS - 1, 2, stride=CELLS + 1)
    side_low = velocity(
        edge_stream(lpost_ref, lambda b: pl.ds(CELLS - 1 - b, 2, stride=CELLS + 1)), low_ref[SOLID, beside, :]
    )
    side_high = velocity(
        edge_stream(hpost_ref, lambda b: pl.ds(CELLS - 1 - b, 2, stride=CELLS + 1)), high_ref[SOLID, beside, :]
    )
    for c in range(3):
        joined = join(side_low[c], side_high[c])
        for k, y in enumerate((-1, CELLS)):
            rows = row_slice(REACH, y)
            spread = pltpu.roll(
                jnp.broadcast_to(joined[k : k + 1], (CELLS, LANES)),
                LANES - (GROUP * (LAST - REACH) + 3),
                1,
                stride=GROUP,
                stride_axis=0,
            )
            rim_ref[c, rows, :] = jnp.where(ends, spread, flow_ref[c, rows, :])

    own = range(REACH, REACH + CELLS)

    def here(c):
        return [rim_ref[c, plane_rows(plane, 0), :] for plane in own]

    def along_first(c):
        return [
            0.5 * (rim_ref[c, plane_rows(plane + 1, 0), :] - rim_ref[c, plane_rows(plane - 1, 0), :]) for plane in own
        ]

    def along_second(c):
        return [0.5 * (rim_ref[c, plane_rows(plane, 1), :] - rim_ref[c, plane_rows(plane, -1), :]) for plane in own]

    def along_third(c):
        low = [turn(value, 1, 1) for value in here(c)]
        high = [turn(value, -1, 1) for value in here(c)]
        out = []
        for k, plane in enumerate(own):
            base = GROUP * (LAST - plane)
            first = jnp.where(lane == 0, turn(flow_low[c], -2 - base, 1), low[k])
            second = jnp.where(lane == LANES - 1, turn(flow_high[c], -6 - base, 1), high[k])
            out.append(0.5 * (second - first))
        return out

    def minus(first, second):
        return [a - b for a, b in zip(first, second)]

    vort = (
        minus(along_second(2), along_third(1)),
        minus(along_third(0), along_first(2)),
        minus(along_first(1), along_second(0)),
    )
    s_two = jnp.concatenate([a * a + b * b + c * c for a, b, c in zip(*vort)], axis=0)
    flow_first = jnp.concatenate(here(0), axis=0)
    solid_on = p_ref[SOLID] > 0.5
    ratio = s_two / (s_two + shade_scale)
    alpha = jnp.where(solid_on, solid_alpha, alpha_top * (1.0 - jnp.exp(-s_two / shade_scale)))
    red = jnp.where(solid_on, 0.6, 0.3 + 1.5 * ratio)
    green = jnp.where(solid_on, 0.6, 1.2 - 0.9 * ratio)
    blue = jnp.where(solid_on, 0.6, 0.8 + 0.4 * jnp.tanh(20.0 * flow_first))
    logs = jnp.log1p(-alpha)
    running = logs
    wide = lanes_of(CELLS * CELLS)
    for step in (1, 2, 4, 8, 16, 32, 64):
        running = running + jnp.where(wide >= step, turn(running, step, 1), 0.0)
    weight = alpha * jnp.exp(running - logs)
    acc = jnp.zeros((CELLS, LANES), jnp.float32)
    for ch, value in enumerate((red * weight, green * weight, blue * weight, logs)):
        total = jnp.sum(value, axis=1, keepdims=True)
        for x in range(CELLS):
            acc = jnp.where(lane // UP == ch * CELLS + x, total[x * CELLS : (x + 1) * CELLS], acc)
    out_ref[...] = acc
    save.wait()


def last_kernel(slab_ref, rank_ref, out_ref):
    slabs = slab_ref[...]
    rank = rank_ref[...]
    channel = lanes_of(CELLS) // (CELLS * UP)
    logs = slabs
    for ch in range(3):
        logs = jnp.where(channel == ch, turn(slabs, (ch + 1) * CELLS * UP, 1), logs)
    front = jnp.zeros_like(slabs)
    for s in range(CELLS):
        front = front + jnp.where(rank[s : s + 1] < rank, logs[s : s + 1], 0.0)
    colour = jnp.sum(jnp.exp(front) * slabs, axis=0, keepdims=True)
    opacity = 1.0 - jnp.exp(jnp.sum(logs, axis=0, keepdims=True))
    row = jnp.where(channel[:1] == 3, opacity, colour)
    for ch in range(4):
        out_ref[ch] = jnp.broadcast_to(turn(row, -ch * CELLS * UP, 1)[:, : CELLS * UP], (UP, CELLS * UP))


def call(kernel, outs, scratch=(), first_out_hbm=False, in_hbm=False):
    shapes = tuple(jax.ShapeDtypeStruct(shape, jnp.float32) for shape in outs)
    extra = {}
    if in_hbm:
        extra["in_specs"] = [pl.BlockSpec(memory_space=pltpu.HBM)] * 3
    if first_out_hbm:
        spaces = [pltpu.HBM] + [pltpu.VMEM] * (len(outs) - 1)
        extra["out_specs"] = tuple(pl.BlockSpec(memory_space=space) for space in spaces)
    return pl.pallas_call(
        kernel,
        out_shape=shapes,
        scratch_shapes=scratch,
        compiler_params=pltpu.CompilerParams(vmem_limit_bytes=24 * 1024 * 1024),
        **extra,
    )


def both_ways(lo, hi, axis):
    count = lax.axis_size(axis)
    forward = [(i, (i + 1) % count) for i in range(count)]
    backward = [(target, source) for source, target in forward]
    return lax.ppermute(hi, axis, forward), lax.ppermute(lo, axis, backward)


def in_pairs(first, second, axis):
    count = lax.axis_size(axis)
    out = []
    for start, value in ((0, first), (1, second)):
        pairs = []
        for i in range(start, count + start, 2):
            left, right = i % count, (i + 1) % count
            pairs += [(left, right), (right, left)]
        out.append(lax.ppermute(value, axis, pairs))
    return out


def body(populations, solid_mask, jet_mask, visibility):
    cells = CELLS * CELLS
    f = populations.reshape(27, cells, LANES)
    solid = solid_mask.reshape(cells, LANES)
    jet = jet_mask.reshape(cells, LANES)
    f, solid, jet = [pltpu.with_memory_space_constraint(value, pltpu.HBM) for value in (f, solid, jet)]
    x_shape = (X_COUNT, CELLS, LANES)
    y_shape = (Y_OWN, LANES)
    post, lo, hi, ya, yb = call(
        first_kernel,
        ((29, cells, LANES), x_shape, x_shape, y_shape, y_shape),
        (
            pltpu.VMEM((27, cells, LANES), jnp.float32),
            pltpu.VMEM((cells, LANES), jnp.int32),
            pltpu.VMEM((cells, LANES), jnp.int32),
            pltpu.SemaphoreType.DMA((CELLS + 2,)),
        ),
        in_hbm=True,
    )(f, solid, jet)
    xlo, xhi = both_ways(lo, hi, "gx")
    ya, yb = in_pairs(ya, yb, "gy")
    corner_shape = (Y_CORNER, LANES)
    lo, hi = call(second_kernel, (corner_shape, corner_shape))(xlo, xhi)
    clo, chi = both_ways(lo, hi, "gy")
    tile_shape = (29, CELLS, LANES)
    low, high = call(faces_kernel, (tile_shape, tile_shape))(post, xlo, xhi)
    half_shape = (HALF, 2 * CELLS, LANES)
    halo, low_halo, lo, hi = call(
        third_kernel, ((29, (SPAN + 1) * CELLS, LANES), tile_shape, half_shape, half_shape)
    )(ya, yb, clo, chi, low)
    zlo, zhi = both_ways(lo, hi, "gz")
    height = SPAN * ROWS + CELLS
    moved, flow, high_halo = call(
        steps_kernel,
        ((27, cells, LANES), (3, height, LANES), tile_shape),
        (pltpu.VMEM((29, height, LANES), jnp.float32), pltpu.VMEM((27, height, LANES), jnp.float32)),
    )(post, xlo, xhi, halo)
    edge = pltpu.VMEM((29, 3 * CELLS, LANES), jnp.float32)
    edge_post = pltpu.VMEM((27, 3 * CELLS, LANES), jnp.float32)
    advanced, slabs = call(
        render_kernel,
        ((27, cells, LANES), (CELLS, LANES)),
        (
            edge,
            edge,
            edge_post,
            edge_post,
            pltpu.VMEM((27, cells, LANES), jnp.float32),
            pltpu.VMEM((3, height, LANES), jnp.float32),
            pltpu.SemaphoreType.DMA,
        ),
        first_out_hbm=True,
    )(post, moved, flow, low, low_halo, high, high_halo, zlo, zhi)
    slabs = lax.all_to_all(slabs, "gz", 0, 0, tiled=True)
    rank = jnp.broadcast_to(visibility[:, None], (CELLS, LANES))
    (image,) = call(last_kernel, ((4, UP, CELLS * UP),))(slabs, rank)
    return advanced.reshape(27, CELLS, CELLS, LANES), jnp.swapaxes(image, 1, 2)


def solution(mesh):
    return jax.shard_map(
        body,
        mesh=mesh,
        in_specs=(P(None, "gx", "gy", "gz"), P("gx", "gy", "gz"), P("gx", "gy", "gz"), P()),
        out_specs=(P(None, "gx", "gy", "gz"), P(None, "gx", ("gy", "gz"))),
        check_vma=False,
    )
```
